32 devices in a mesh: seq: 4 (over z), batch: 8 (over y, x, core).
Axes of the slice: x: 2, y: 2, z: 4, core: 2. Of those that a mesh axis runs over, the one named last changes fastest.
Arguments:
- image: bfloat16 [8, 128, 32, 512], P('batch', 'seq'), may hold values from -64 to 64
- tile_map: int32 [8, 128, 32], P('batch', 'seq'), may hold values from 0 to 1003, as said below
- out_grad: bfloat16 [8, 128, 32, 512], P('batch', 'seq'), may hold values from -6 to 6
- conv_weight: bfloat16 [2, 3, 3, 512, 512], replicated, may hold values from -0.09375 to 0.09375
- conv_bias: bfloat16 [2, 512], replicated, may hold values from -1.75 to 1.75
- norm_gain: bfloat16 [3, 512], replicated, may hold values from 0.5 to 1.5
- norm_shift: bfloat16 [3, 512], replicated, may hold values from -2.5 to 2.5
- qk_weight: bfloat16 [2, 512, 512], replicated, may hold values from -0.375 to 0.375
- value_weight: bfloat16 [512, 512], replicated, may hold values from -0.25 to 0.25
- proj_weight: bfloat16 [512, 512], replicated, may hold values from -1 to 1
- qv_bias: bfloat16 [2, 512], replicated, may hold values from -1.75 to 1.75
- proj_bias: bfloat16 [512], replicated, may hold values from -1.75 to 1.75
Outputs:
- output: bfloat16 [8, 128, 32, 512], P('batch', 'seq')
- image_grad: bfloat16 [8, 128, 32, 512], P('batch', 'seq')
- conv_weight_grad: float32 [2, 3, 3, 512, 512], replicated
- conv_bias_grad: float32 [2, 512], replicated
- norm_gain_grad: float32 [3, 512], replicated
- norm_shift_grad: float32 [3, 512], replicated
- qk_weight_grad: float32 [2, 512, 512], replicated
- value_weight_grad: float32 [512, 512], replicated
- proj_weight_grad: float32 [512, 512], replicated
- qv_bias_grad: float32 [2, 512], replicated
- proj_bias_grad: float32 [512], replicated
The draws below stay inside these ranges and needn't reach their ends.
Inputs may be any that keep to these rules, and one draw needn't show every extreme that they name: `tile_map`: tile ids label regions of a canvas: each tile is one region of pixels, and distinct tiles of a canvas have distinct ids.
All inputs are finite; a program needn't handle non-finite values.
Results may differ from the reference program's by a relative error of at most 0.017.
The reference program's roundings to bfloat16 on the way count: a program that leaves them out, or rounds other values in their place, can miss the bound.
Values may be sent and summed in bfloat16 or wider, within the bound.
No kernel may reach another device: no remote copies, remote signals or barrier semaphores. Data moves between devices by JAX's collectives and lax.ppermute only.
A program may use at most 256 MiB of HBM per device.

```python
import math
import jax
import jax.numpy as jnp
from jax import lax

C = 512
GROUPS = 32
W = 32
H = 128
CANVASES = 8


def draw_image(key, part):
    key = jax.random.fold_in(key, 11)
    keys = jax.random.split(key, 2)
    ramp = 1.0 + 2.0 * jnp.arange(H, dtype=jnp.float32) / max(H - 1, 1)
    base = jax.random.normal(keys[0], (CANVASES, H, W, C), jnp.float32)
    channel_scale = jnp.exp(jax.random.uniform(keys[1], (C,), jnp.float32, math.log(0.5), math.log(2.0)))
    values = base * channel_scale * ramp[None, :, None, None]
    return values.astype(jnp.bfloat16)


def draw_tile_map(key, part):
    key = jax.random.fold_in(key, 23)

    def one_canvas(subkey):
        pieces = jax.random.split(subkey, 4)
        column_cut = jax.random.randint(pieces[0], (), W // 4, 3 * W // 4 + 1, dtype=jnp.int32)
        mirror = jax.random.randint(pieces[1], (), 0, 2, dtype=jnp.int32)
        base_id = jax.random.randint(pieces[2], (), 0, 1000, dtype=jnp.int32)
        jitter = jax.random.randint(pieces[3], (3,), -(H // 8), H // 8 + 1, dtype=jnp.int32)
        bounds = jnp.arange(1, 4, dtype=jnp.int32) * (H // 4) + jitter
        row_index = jnp.arange(H, dtype=jnp.int32)[:, None]
        col_index = jnp.arange(W, dtype=jnp.int32)[None, :]
        col_index = jnp.where(mirror == 1, W - 1 - col_index, col_index)
        strip = jnp.sum((row_index[:, :, None] >= bounds[None, None, :]).astype(jnp.int32), axis=2)
        labels = jnp.where(col_index < column_cut, base_id, base_id + 1 + strip)
        return labels.astype(jnp.int32)
    return jax.vmap(one_canvas)(jax.random.split(key, CANVASES))


def shard_levels(rng, extent, shards, least, high):
    loudness = 1.0
    for position, blocks in shards:
        heights = jax.random.uniform(jax.random.fold_in(jax.random.fold_in(rng, 6), position), (blocks,), jnp.float32, least / len(shards), high / len(shards))
        loudness = loudness * jnp.repeat(jnp.exp(heights), extent[position] // blocks).reshape((-1,) + (1,) * (len(extent) - 1 - position))
    return loudness


def bell_draw(key, shape, spread, most, cuts=(), kind=jnp.bfloat16):
    entries = spread * jax.random.normal(key, shape, jnp.float32)
    if cuts:
        entries = entries * shard_levels(key, shape, cuts, -0.22, 0.18)
    return jnp.clip(entries, -most, most).astype(kind)


def setup_inputs(seed: int = 0) -> dict:
    splits = jax.random.split(jax.random.key(seed), 13)
    return {
        "image": draw_image(jax.random.fold_in(splits[12], 71), 0),
        "tile_map": draw_tile_map(jax.random.fold_in(splits[12], 71), 0),
        "out_grad": bell_draw(splits[2], (CANVASES, H, W, C), 1.0, 6.0, ((0, 8), (1, 4))),
        "conv_weight": bell_draw(splits[3], (2, 3, 3, C, C), (9 * C) ** -0.5, 0.09375),
        "conv_bias": bell_draw(splits[4], (2, C), 0.3, 1.75),
        "norm_gain": jnp.clip(1.0 + 0.1 * jax.random.normal(splits[5], (3, C), jnp.float32), 0.5, 1.5).astype(jnp.bfloat16),
        "norm_shift": bell_draw(splits[6], (3, C), 0.4, 2.5),
        "qk_weight": bell_draw(splits[7], (2, C, C), (C // 2) ** -0.5, 0.375),
        "value_weight": bell_draw(splits[8], (C, C), C ** -0.5, 0.25),
        "proj_weight": bell_draw(splits[9], (C, C), (C // 16) ** -0.5, 1.0),
        "qv_bias": bell_draw(splits[10], (2, C), 0.3, 1.75),
        "proj_bias": bell_draw(splits[11], (C,), 0.3, 1.75),
    }


@jax.custom_vjp
def low(v):
    return lax.optimization_barrier(v.astype(jnp.bfloat16)).astype(jnp.float32)

@jax.custom_vjp
def low_back(v):
    return v

def low_keep(v):
    return (low(v), None)

def low_pass(kept, grad):
    return (grad,)

def back_keep(v):
    return (v, None)

def back_low(kept, grad):
    return (low(grad),)
low.defvjp(low_keep, low_pass)
low_back.defvjp(back_keep, back_low)
EPSILON = 1e-06
MASKED_SCORE = -1e+30
PRECISE = lax.Precision.HIGHEST

def group_norm(values, gain, shift):
    pixels = values.shape[0]
    grouped = values.reshape(pixels, GROUPS, C // GROUPS)
    group_mean = lax.optimization_barrier(jnp.mean(grouped, axis=(0, 2), keepdims=True))
    centered = grouped - group_mean
    group_var = lax.optimization_barrier(jnp.mean(centered * centered, axis=(0, 2), keepdims=True))
    normal_form = (centered * lax.rsqrt(group_var + EPSILON)).reshape(pixels, C)
    return normal_form * gain + shift

def swish(values):
    return values * jax.nn.sigmoid(values)

def masked_conv(field, weight, bias, tile_ids):
    padded = jnp.pad(field, ((1, 1), (1, 1), (0, 0)))
    framed = jnp.pad(tile_ids, 1, constant_values=-1)
    columns = []
    for row_off in range(3):
        for col_off in range(3):
            tap_keep = (framed[row_off:row_off + H, col_off:col_off + W] == tile_ids).astype(jnp.float32)
            columns.append(padded[row_off:row_off + H, col_off:col_off + W] * tap_keep[:, :, None])
    tap_rows = jnp.stack(columns, 2).reshape(H * W, 9 * C)
    product = low_back(jnp.dot(tap_rows, weight.reshape(9 * C, C), precision=PRECISE))
    return product + bias

def canvas_forward(canvas, tile_ids, conv_weight, conv_bias, norm_gain, norm_shift, qk_weight, value_weight, proj_weight, qv_bias, proj_bias):
    pixels = canvas.reshape(H * W, C)
    act_one = low(swish(group_norm(pixels, norm_gain[0], norm_shift[0])))
    middle = masked_conv(act_one.reshape(H, W, C), conv_weight[0], conv_bias[0], tile_ids)
    act_two = low(swish(group_norm(middle, norm_gain[1], norm_shift[1])))
    residual = pixels + masked_conv(act_two.reshape(H, W, C), conv_weight[1], conv_bias[1], tile_ids)
    normed = low(group_norm(residual, norm_gain[2], norm_shift[2]))
    queries = low_back(low(jnp.dot(normed, qk_weight[0], precision=PRECISE) + qv_bias[0]))
    key_rows = low_back(low(jnp.dot(normed, qk_weight[1], precision=PRECISE)))
    value_rows = low_back(low(jnp.dot(normed, value_weight, precision=PRECISE) + qv_bias[1]))
    flat_ids = tile_ids.reshape(H * W)
    allowed = flat_ids[:, None] == flat_ids[None, :]
    scores = low_back(jnp.dot(queries, key_rows.T, precision=PRECISE) * C ** (-0.5))
    scores = jnp.where(allowed, scores, MASKED_SCORE)
    log_total = jax.nn.logsumexp(scores, axis=1, keepdims=True)
    weights_low = low(jnp.exp(scores - log_total))
    attended = low_back(low(jnp.dot(weights_low, value_rows, precision=PRECISE)))
    output = residual + jnp.dot(attended, proj_weight, precision=PRECISE) + proj_bias
    return output.reshape(H, W, C)

def reference(image, tile_map, out_grad, conv_weight, conv_bias, norm_gain, norm_shift, qk_weight, value_weight, proj_weight, qv_bias, proj_bias):
    parameters = tuple((member.astype(jnp.float32) for member in (conv_weight, conv_bias, norm_gain, norm_shift, qk_weight, value_weight, proj_weight, qv_bias, proj_bias)))

    def one_canvas(totals, element):
        canvas, tile_ids, cotangent = element

        def forward(values, *weights):
            return canvas_forward(values, tile_ids, *weights)
        output, pullback = jax.vjp(forward, canvas.astype(jnp.float32), *parameters)
        gradients = pullback(cotangent.astype(jnp.float32))
        totals = tuple((running + update for running, update in zip(totals, gradients[1:])))
        return (totals, (output.astype(jnp.bfloat16), gradients[0].astype(jnp.bfloat16)))
    start_totals = tuple((jnp.zeros(member.shape, jnp.float32) for member in parameters))
    totals, (outputs, image_grads) = lax.scan(one_canvas, start_totals, (image, tile_map, out_grad))
    return (outputs, image_grads, totals[0], totals[1], totals[2], totals[3], totals[4], totals[5], totals[6], totals[7], totals[8])
```

```python
import functools

import jax
import jax.numpy as jnp
from jax import lax
from jax.experimental import pallas as pl
from jax.experimental.pallas import tpu as pltpu
from jax.sharding import PartitionSpec as P

GROUPS = 32
EPSILON = 1e-06
MASKED_SCORE = -1e30
F32 = jnp.float32
BF16 = jnp.bfloat16
MIB = 1024 * 1024
PIECES = 32


def params(mib):
    return pltpu.CompilerParams(vmem_limit_bytes=mib * MIB)


def shape(dims, dtype):
    return jax.ShapeDtypeStruct(dims, dtype)


SMEM = pl.BlockSpec(memory_space=pltpu.SMEM)


def whole(*dims):
    return pl.BlockSpec(dims, lambda *_: (0,) * len(dims))


def group_sum(row):
    channels = row.shape[1]
    lane = lax.broadcasted_iota(jnp.int32, row.shape, 1)
    step = 1
    while step < channels // GROUPS:
        ahead = pltpu.roll(row, channels - step, 1)
        behind = pltpu.roll(row, step, 1)
        row = row + jnp.where((lane & step) == 0, ahead, behind)
        step *= 2
    return row


def rows_of(*parts):
    channels = parts[0].shape[1]
    line = lax.broadcasted_iota(jnp.int32, (8, channels), 0)
    out = jnp.zeros((8, channels), F32)
    for i, part in enumerate(parts):
        out = jnp.where(line == i, jnp.broadcast_to(part, (8, channels)), out)
    return out


def eight(row):
    return jnp.broadcast_to(row, (8, row.shape[1]))


def local_stats(values, channels, pixels):
    count = float(pixels * (channels // GROUPS))
    mean = group_sum(eight(jnp.sum(values, axis=0, keepdims=True)))[0:1] / count
    centered = values - mean
    square = group_sum(eight(jnp.sum(centered * centered, axis=0, keepdims=True)))[0:1]
    return mean, square


def joined_stats(own, near, cross, pair, pixels):
    bands = [own[0:2], near[32:34], cross[32:34], pair[0:2]]
    channels = bands[0].shape[1]
    count = float(pixels * (channels // GROUPS))
    mean = (bands[0][0:1] + bands[1][0:1] + bands[2][0:1] + bands[3][0:1]) * 0.25
    total = 0.0
    for band in bands:
        gap = band[0:1] - mean
        total = total + band[1:2] + count * gap * gap
    return mean, lax.rsqrt(total / (4.0 * count) + EPSILON)


def joined_sums(own, near, cross, pair, pixels):
    bands = [own[0:2], near[32:34], cross[32:34], pair[0:2]]
    channels = bands[0].shape[1]
    count = 4.0 * float(pixels * (channels // GROUPS))
    sums = (bands[0] + bands[1]) + (bands[2] + bands[3])
    return sums[0:1] / count, sums[1:2] / count


def sigmoid(values):
    return 0.5 * jnp.tanh(0.5 * values) + 0.5


def edges_out(side_ref, out_ref, near_ref, cross_ref, stats):
    pixels = out_ref.shape[0]
    side = side_ref[0]
    last = pixels - 32
    near_ref[0:32, :] = out_ref[pl.ds(pl.multiple_of(last * (1 - side), 32), 32), :].astype(F32)
    cross_ref[0:32, :] = out_ref[pl.ds(pl.multiple_of(last * side, 32), 32), :].astype(F32)
    near_ref[32:40, :] = stats
    cross_ref[32:40, :] = stats


def columns_of(frame, shifted, rows):
    for b in range(3):
        shifted[b] = frame[7 + b : 7 + b + rows, :].astype(BF16)


def masked(values, mask):
    channels = values.shape[1]
    return [values[:, i * 128 : (i + 1) * 128] * mask for i in range(channels // 128)]


def tap_rows(shifted, mask_ref, start, count, row):
    parts = []
    for b in range(3):
        block = shifted[b, pl.ds(pl.multiple_of(row * 32 + start, 32), count), :]
        parts += masked(block, mask_ref[b, start : start + count, :])
    return parts


def first_kernel(image_ref, tiles_ref, side_ref, near_ref, cross_ref, stats_ref):
    pixels, channels = image_ref.shape
    mean, square = local_stats(image_ref[...].astype(F32), channels, pixels)
    stats = rows_of(mean, square, tiles_ref[0:1], tiles_ref[1:2])
    stats_ref[...] = stats
    edges_out(side_ref, image_ref, near_ref, cross_ref, stats)


def mask_kernel(where_ref, own_ref, near_ref, cross_ref, pair_ref, mask_ref, column_ref, row_ref, frame):
    side, first, last = where_ref[0], where_ref[1], where_ref[2]

    def line(ref, base):
        return jnp.concatenate([ref[base + 2 : base + 3, :], ref[base + 3 : base + 4, :]], axis=1)

    own, near, cross, pair = line(own_ref, 0), line(near_ref, 32), line(cross_ref, 32), line(pair_ref, 0)
    pixels = own.shape[1]
    row_ref[...] = jnp.concatenate([own, pair, near, cross], axis=1)

    def upright(row):
        return jnp.transpose(jnp.broadcast_to(row, (128, row.shape[1])))

    column = upright(own)
    column_ref[...] = column
    above = jnp.where(side == 0, cross[:, pixels - 128 :], near[:, pixels - 128 :])
    below = jnp.where(side == 0, near[:, :128], cross[:, :128])
    outside = jnp.full((32, 128), -1.0, F32)
    frame[0:8, :] = jnp.zeros((8, 128), F32)
    frame[8:40, :] = jnp.where(first == 1, outside, upright(above)[96:128, :])
    frame[40 : 40 + pixels, :] = column
    frame[40 + pixels : 72 + pixels, :] = jnp.where(last == 1, outside, upright(below)[0:32, :])
    frame[72 + pixels : 80 + pixels, :] = jnp.zeros((8, 128), F32)
    place = lax.broadcasted_iota(jnp.int32, (pixels, 128), 0) & 31
    for a in range(3):
        for b in range(3):
            start = 8 + a * 32 + b - 1
            same = frame[start : start + pixels, :] == column
            if b == 0:
                same = same & (place > 0)
            if b == 2:
                same = same & (place < 31)
            mask_ref[a * 3 + b] = jnp.where(same, 1.0, 0.0).astype(BF16)


def conv_kernel(
    side_ref, x_ref, near_ref, cross_ref, pair_ref, stats_ref, rows_ref, mask_ref, weight_ref, skip_ref,
    out_ref, act_ref, near_out, cross_out, stats_out, frame, shifted,
):
    row = pl.program_id(0)
    pixels, channels = x_ref.shape

    @pl.when(row == 0)
    def _():
        mean, inverse = joined_stats(stats_ref[...], near_ref[...], cross_ref[...], pair_ref[...], pixels)
        scale, shift, bias = rows_ref[0:1, :], rows_ref[1:2, :], rows_ref[2:3, :]

        def act(values):
            pre = (values - mean) * inverse * scale + shift
            return pre * sigmoid(pre)

        side = side_ref[0]
        near, cross = near_ref[0:32, :], cross_ref[0:32, :]
        frame[0:8, :] = jnp.zeros((8, channels), F32)
        frame[8:40, :] = act(jnp.where(side == 0, cross, near))
        frame[40 : 40 + pixels, :] = act(x_ref[...].astype(F32))
        frame[40 + pixels : 72 + pixels, :] = act(jnp.where(side == 0, near, cross))
        frame[72 + pixels : 80 + pixels, :] = jnp.zeros((8, channels), F32)
        columns_of(frame, shifted, pixels + 64)
        act_ref[...] = shifted[1, 32 : 32 + pixels, :]
        start = jnp.broadcast_to(bias, (pixels, channels))
        if skip_ref is not None:
            start = start + skip_ref[...].astype(F32)
        out_ref[...] = start

    weight = weight_ref[...].reshape(3 * channels, channels)
    for i in range(pixels // 256):
        taps = jnp.concatenate(tap_rows(shifted, mask_ref, i * 256, 256, row), axis=1)
        out_ref[i * 256 : (i + 1) * 256, :] += jnp.dot(taps, weight, preferred_element_type=F32)

    @pl.when(row == 2)
    def _():
        mean, square = local_stats(out_ref[...], channels, pixels)
        stats = rows_of(mean, square)
        stats_out[...] = stats
        edges_out(side_ref, out_ref, near_out, cross_out, stats)


def normed_kernel(x_ref, near_ref, cross_ref, pair_ref, stats_ref, rows_ref, out_ref):
    pixels = x_ref.shape[0]
    mean, inverse = joined_stats(stats_ref[...], near_ref[...], cross_ref[...], pair_ref[...], pixels)
    out_ref[...] = ((x_ref[...] - mean) * inverse * rows_ref[0:1, :] + rows_ref[1:2, :]).astype(BF16)


def nn(left, right):
    return jnp.dot(left, right, preferred_element_type=F32)


def nt(left, right):
    return lax.dot_general(left, right, (((1,), (1,)), ((), ())), preferred_element_type=F32)


def project_kernel(transposed, *refs):
    blocks, (matrix_ref, bias_ref, out_ref) = refs[:4], refs[4:]
    pixels = blocks[0].shape[0]
    product = nt if transposed else nn
    for i, block in enumerate(blocks):
        values = product(block[...], matrix_ref[...])
        out_ref[i * pixels : (i + 1) * pixels, :] = (values + bias_ref[0:1, :]).astype(BF16)


def attend_kernel(
    own_ref, pair_ref, near_ref, cross_ref, grad_ref, qk_ref, value_ref, bias_ref, column_ref, row_ref,
    attended_ref, query_grad_ref, totals_ref, keys, values,
):
    pixels, channels = own_ref.shape
    scale = channels ** (-0.5)
    for i, block in enumerate((own_ref, pair_ref, near_ref, cross_ref)):
        rows = block[...]
        keys[i * pixels : (i + 1) * pixels, :] = nn(rows, qk_ref[1]).astype(BF16)
        values[i * pixels : (i + 1) * pixels, :] = (nn(rows, value_ref[...]) + bias_ref[1:2, :]).astype(BF16)

    def step(i, carry):
        part = pl.ds(pl.multiple_of(i * 256, 256), 256)
        queries = (nn(own_ref[part, :], qk_ref[0]) + bias_ref[0:1, :]).astype(BF16)
        scores = nt(queries, keys[...]) * scale
        scores = jnp.where(column_ref[part, 0:1] == row_ref[...], scores, MASKED_SCORE)
        top = jnp.max(scores, axis=1, keepdims=True)
        weights = jnp.exp(scores - top)
        total = jnp.sum(weights, axis=1, keepdims=True)
        attended = nn(weights.astype(BF16), values[...]) / total
        attended_ref[part, :] = attended.astype(BF16)
        upstream = grad_ref[part, :]
        delta = jnp.sum(attended * upstream.astype(F32), axis=1, keepdims=True)
        prob_grad = nt(upstream, values[...])
        score_grad = (weights * (1.0 / total) * (prob_grad - delta)).astype(BF16)
        query_grad_ref[part, :] = (nn(score_grad, keys[...]) * scale).astype(BF16)
        log_total = jnp.transpose(jnp.broadcast_to(top + jnp.log(total), (256, 128)))
        turned = jnp.transpose(jnp.broadcast_to(delta, (256, 128)))
        totals_ref[i, 0:1, :] = log_total[0:1, :]
        totals_ref[i, 1:2, :] = turned[0:1, :]
        totals_ref[i, 2:8, :] = jnp.zeros((6, 256), F32)
        return carry

    lax.fori_loop(0, pixels // 256, step, 0)


def out_kernel(attended_ref, residual_ref, matrix_ref, bias_ref, out_ref):
    out_ref[...] = (residual_ref[...] + nn(attended_ref[...], matrix_ref[...]) + bias_ref[0:1, :]).astype(BF16)


def norm_back_sums(upstream, hat, gain):
    outer = jnp.sum(upstream * hat, axis=0, keepdims=True)
    inner = jnp.sum(upstream, axis=0, keepdims=True)
    first = group_sum(eight(inner * gain))[0:1]
    second = group_sum(eight(outer * gain))[0:1]
    return rows_of(outer, inner), rows_of(first, second)


def key_kernel(
    side_ref, own_ref, queries_ref, grads_ref, query_grad_ref, qk_ref, value_ref, bias_ref,
    totals_own, totals_pair, totals_near, totals_cross, column_ref, row_ref,
    residual_ref, stats_ref, near_ref, cross_ref, pair_ref, rows_ref,
    key_grad_ref, value_grad_ref, normed_grad_ref, near_out, cross_out, stats_out, sums_out,
    keys, values, key_sum, value_sum,
):
    pixels, channels = own_ref.shape
    scale = channels ** (-0.5)
    keys[...] = nn(own_ref[...], qk_ref[1]).astype(BF16)
    values[...] = (nn(own_ref[...], value_ref[...]) + bias_ref[1:2, :]).astype(BF16)
    key_sum[...] = jnp.zeros_like(key_sum)
    value_sum[...] = jnp.zeros_like(value_sum)
    blocks = pixels // 256
    for group, totals in enumerate((totals_own, totals_pair, totals_near, totals_cross)):

        def step(i, carry, group=group, totals=totals):
            part = pl.ds(pl.multiple_of(group * pixels + i * 256, 256), 256)
            queries, upstream = queries_ref[part, :], grads_ref[part, :]
            scores = nt(keys[...], queries) * scale
            weights = jnp.exp(scores - totals[i, 0:1, :])
            weights = jnp.where(column_ref[:, 0:1] == row_ref[group * blocks + i, 0:1, :], weights, 0.0)
            value_sum[...] += nn(weights.astype(BF16), upstream)
            prob_grad = nt(values[...], upstream)
            score_grad = (weights * (prob_grad - totals[i, 1:2, :])).astype(BF16)
            key_sum[...] += nn(score_grad, queries)
            return carry

        lax.fori_loop(0, blocks, step, 0)
    key_grad = (key_sum[...] * scale).astype(BF16)
    value_grad = value_sum[...].astype(BF16)
    key_grad_ref[...] = key_grad
    value_grad_ref[...] = value_grad
    normed_grad = nt(query_grad_ref[...], qk_ref[0]) + nt(key_grad, qk_ref[1]) + nt(value_grad, value_ref[...])
    normed_grad_ref[...] = normed_grad
    mean, inverse = joined_stats(stats_ref[...], near_ref[...], cross_ref[...], pair_ref[...], pixels)
    hat = (residual_ref[...] - mean) * inverse
    sums, groups = norm_back_sums(normed_grad, hat, rows_ref[0:1, :])
    sums_out[...] = sums
    stats_out[...] = groups
    edges_out(side_ref, normed_grad_ref, near_out, cross_out, groups)


def scatter_pieces(place_ref, product, tap, first_ref, second_ref):
    rows, channels = product.shape
    half, height = channels // 2, rows // PIECES
    for j in range(PIECES):
        piece = product[j * height : (j + 1) * height, :].astype(BF16)
        first_ref[j ^ place_ref[0], tap] = piece[:, :half]
        second_ref[j ^ place_ref[1], tap] = piece[:, half:]


def tn(left, right):
    return lax.dot_general(left, right, (((0,), (0,)), ((), ())), preferred_element_type=F32)


def matrix_kernel(
    place_ref, normed_ref, query_grad_ref, key_grad_ref, value_grad_ref, attended_ref, cotangent_ref,
    first_ref, second_ref, sums_ref, turned,
):
    turned[...] = jnp.transpose(normed_ref[...])
    for tap, ref in enumerate((query_grad_ref, key_grad_ref, value_grad_ref)):
        scatter_pieces(place_ref, nn(turned[...], ref[...]), tap, first_ref, second_ref)
    turned[...] = jnp.transpose(attended_ref[...])
    scatter_pieces(place_ref, nn(turned[...], cotangent_ref[...]), 3, first_ref, second_ref)
    total = [
        jnp.sum(ref[...].astype(F32), axis=0, keepdims=True)
        for ref in (query_grad_ref, value_grad_ref, cotangent_ref)
    ]
    sums_ref[...] = rows_of(*total)


def weight_grad_kernel(
    with_cotangent, place_ref, side_ref, x_ref, x_near, x_cross, stats_ref, near_ref, cross_ref, pair_ref,
    g_ref, g_near, g_cross, g_pair, g_stats, rows_ref, act_ref, mask_ref, *rest,
):
    if with_cotangent:
        cot_ref, first_ref, second_ref, shifted, sums_ref, own_ref, frame, turned = rest
    else:
        first_ref, second_ref, shifted, sums_ref, frame, turned = rest
    row = pl.program_id(0)
    pixels, channels = x_ref.shape

    @pl.when(row == 0)
    def _():
        mean, inverse = joined_stats(stats_ref[...], near_ref[...], cross_ref[...], pair_ref[...], pixels)
        mean_h, mean_hx = joined_sums(g_stats[...], g_near[...], g_cross[...], g_pair[...], pixels)
        gain = rows_ref[0:1, :]
        side = side_ref[0]

        def back(grad, values):
            hat = (values - mean) * inverse
            return inverse * (grad * gain - mean_h - hat * mean_hx)

        def pick(near, cross):
            return jnp.where(side == 0, cross, near), jnp.where(side == 0, near, cross)

        g_above, g_below = pick(g_near[0:32, :], g_cross[0:32, :])
        x_above, x_below = pick(x_near[0:32, :], x_cross[0:32, :])
        above, below = back(g_above, x_above), back(g_below, x_below)
        own = back(g_ref[...], x_ref[...])
        if with_cotangent:
            c_above, c_below = pick(x_near[32:64, :], x_cross[32:64, :])
            above, below = above + c_above, below + c_below
            own = own + cot_ref[...].astype(F32)
            own_ref[...] = own
        sums_ref[...] = rows_of(jnp.sum(own, axis=0, keepdims=True))
        frame[0:8, :] = jnp.zeros((8, channels), F32)
        frame[8:40, :] = above
        frame[40 : 40 + pixels, :] = own
        frame[40 + pixels : 72 + pixels, :] = below
        frame[72 + pixels : 80 + pixels, :] = jnp.zeros((8, channels), F32)
        columns_of(frame, shifted, pixels + 64)
        turned[...] = jnp.transpose(act_ref[...])

    for b in range(3):
        block = shifted[b, pl.ds(pl.multiple_of(row * 32, 32), pixels), :]
        block = jnp.concatenate(masked(block, mask_ref[b]), axis=1)
        product = nn(turned[...], block)
        scatter_pieces(place_ref, product, 8 - row * 3 - b, first_ref, second_ref)


def conv_back_kernel(
    side_ref, shifted, mask_ref, weight_ref, x_ref, stats_ref, near_ref, cross_ref, pair_ref, rows_ref,
    out_ref, near_out, cross_out, stats_out, sums_out,
):
    row = pl.program_id(0)
    pixels, channels = x_ref.shape

    @pl.when(row == 0)
    def _():
        out_ref[...] = jnp.zeros_like(out_ref)

    weight = jnp.concatenate([weight_ref[2 - b] for b in range(3)], axis=1)
    for i in range(pixels // 256):
        taps = jnp.concatenate(tap_rows(shifted, mask_ref, i * 256, 256, row), axis=1)
        out_ref[i * 256 : (i + 1) * 256, :] += nt(taps, weight)

    @pl.when(row == 2)
    def _():
        mean, inverse = joined_stats(stats_ref[...], near_ref[...], cross_ref[...], pair_ref[...], pixels)
        gain, shift = rows_ref[0:1, :], rows_ref[1:2, :]
        hat = (x_ref[...].astype(F32) - mean) * inverse
        pre = hat * gain + shift
        gate = sigmoid(pre)
        upstream = out_ref[...] * (gate * (1.0 + pre * (1.0 - gate)))
        out_ref[...] = upstream
        sums, groups = norm_back_sums(upstream, hat, gain)
        sums_out[...] = sums
        stats_out[...] = groups
        edges_out(side_ref, out_ref, near_out, cross_out, groups)


def last_kernel(
    g_ref, g_near, g_cross, g_pair, g_stats, x_ref, stats_ref, near_ref, cross_ref, pair_ref, rows_ref, add_ref, out_ref
):
    pixels = x_ref.shape[0]
    mean, inverse = joined_stats(stats_ref[...], near_ref[...], cross_ref[...], pair_ref[...], pixels)
    mean_h, mean_hx = joined_sums(g_stats[...], g_near[...], g_cross[...], g_pair[...], pixels)
    hat = (x_ref[...].astype(F32) - mean) * inverse
    grad = inverse * (g_ref[...] * rows_ref[0:1, :] - mean_h - hat * mean_hx)
    out_ref[...] = (add_ref[...] + grad).astype(BF16)


def unpack_kernel(place_ref, first_ref, second_ref, *rest):
    out_ref = rest[-1]
    height, half = first_ref.shape[2], first_ref.shape[3]
    for j in range(PIECES):
        lines = slice(j * height, (j + 1) * height)
        out_ref[0, lines, :half] = first_ref[j ^ place_ref[0], 0].astype(F32)
        out_ref[0, lines, half:] = second_ref[j ^ place_ref[1], 0].astype(F32)


def body(
    image,
    tile_map,
    out_grad,
    conv_weight,
    conv_bias,
    norm_gain,
    norm_shift,
    qk_weight,
    value_weight,
    proj_weight,
    qv_bias,
    proj_bias,
):
    band, width, channels = image.shape[1], image.shape[2], image.shape[3]
    pixels = band * width
    lanes = lax.axis_size("batch")
    devices = 4 * lanes

    def turned(flat):
        s, b = flat // lanes, flat % lanes
        core, high = b % 2, s // 2
        return (core * 2 + s % 2) * lanes + (b - core + high)

    def xored(flat, bits):
        return flat ^ bits

    def permute(x, to):
        return lax.ppermute(x, ("seq", "batch"), [(i, to(i)) for i in range(devices)])

    near_bit, pair_bit = lanes, 1

    def to_near(i):
        return i ^ near_bit

    def to_pair(i):
        return i ^ pair_bit

    def to_cross(i):
        return i ^ (near_bit | pair_bit)

    def meet(near, cross, stats):
        return permute(near, to_near), permute(cross, to_cross), permute(stats, to_pair)

    seq, lane = lax.axis_index("seq"), lax.axis_index("batch")
    core, low, high = lane % 2, seq % 2, seq // 2
    side = low.astype(jnp.int32).reshape(1)
    spot = jnp.stack([low, ((low == 0) & (core == 0)), ((low == 1) & (core == 1))]).astype(jnp.int32)
    x_bit, y_bit = (lane // 2) % 2, (lane // 4) % 2
    tail = low * 2 + high
    place = jnp.stack(
        [core * 16 + x_bit * 8 + y_bit * 4 + tail, core * 16 + y_bit * 8 + x_bit * 4 + tail]
    ).astype(jnp.int32)

    def block8(*rows):
        rows = [r.astype(F32).reshape(1, channels) for r in rows]
        return jnp.concatenate(rows + [jnp.zeros((8 - len(rows), channels), F32)], axis=0)

    norm_rows = [block8(norm_gain[i], norm_shift[i], conv_bias[min(i, 1)]) for i in range(3)]
    bias_rows = block8(qv_bias[0], qv_bias[1], proj_bias, jnp.zeros((channels,), F32))

    row_f32 = shape((40, channels), F32)
    stat_f32 = shape((8, channels), F32)
    field_f32 = shape((pixels, channels), F32)
    field_b16 = shape((pixels, channels), BF16)
    field = whole(pixels, channels)
    edge = whole(40, channels)
    stat = whole(8, channels)

    image_flat = image.reshape(pixels, channels)
    cot_flat = out_grad.reshape(pixels, channels)
    tiles = tile_map.astype(F32).reshape(2, pixels // 2)
    x = permute(image_flat, turned)
    near0, cross0, stats0 = pl.pallas_call(
        first_kernel,
        in_specs=[field, whole(2, pixels // 2), SMEM],
        out_specs=[edge, edge, stat],
        out_shape=[row_f32, row_f32, stat_f32],
        grid=(1,),
        compiler_params=params(16),
        name="first",
    )(image_flat, tiles, side)
    own0 = permute(stats0, turned)
    pair0 = permute(stats0, lambda i: to_pair(turned(i)))
    near0 = permute(near0, lambda i: to_near(turned(i)))
    cross0 = permute(cross0, lambda i: to_cross(turned(i)))
    masks, column_tiles, row_tiles = pl.pallas_call(
        mask_kernel,
        in_specs=[SMEM, stat, edge, edge, stat],
        out_specs=[whole(9, pixels, 128), whole(pixels, 128), whole(1, 4 * pixels)],
        out_shape=[shape((9, pixels, 128), BF16), shape((pixels, 128), F32), shape((1, 4 * pixels), F32)],
        scratch_shapes=[pltpu.VMEM((pixels + 80, 128), F32)],
        grid=(1,),
        compiler_params=params(24),
        name="masks",
    )(spot, own0, near0, cross0, pair0)

    cotangent = permute(cot_flat, turned)

    mask_block = pl.BlockSpec((3, pixels, 128), lambda i: (i, 0, 0))

    def conv(x, met, stats, rows, index, skip, name):
        near, cross, pair = met
        specs = [
            SMEM, field, edge, edge, stat, stat, stat, mask_block,
            pl.BlockSpec((None, 1, 3, channels, channels), lambda i: (index, i, 0, 0, 0)),
        ]
        operands = [side, x, near, cross, pair, stats, rows, masks, conv_weight]
        kernel = conv_kernel
        if skip is None:

            def kernel(*refs):
                return conv_kernel(*refs[:9], None, *refs[9:])
        else:
            specs.append(field)
            operands.append(skip)
        return pl.pallas_call(
            kernel,
            in_specs=specs,
            out_specs=[field, field, edge, edge, stat],
            out_shape=[field_f32, field_b16, row_f32, row_f32, stat_f32],
            scratch_shapes=[pltpu.VMEM((pixels + 80, channels), F32), pltpu.VMEM((3, pixels + 64, channels), BF16)],
            grid=(3,),
            compiler_params=params(40),
            name=name,
        )(*operands)

    met0 = (near0, cross0, pair0)
    middle, act_one, near1, cross1, stats1 = conv(x, met0, own0, norm_rows[0], 0, None, "conv_one")
    met1 = meet(near1, cross1, stats1)
    residual, act_two, near2, cross2, stats2 = conv(middle, met1, stats1, norm_rows[1], 1, x, "conv_two")
    met2 = meet(near2, cross2, stats2)

    normed = pl.pallas_call(
        normed_kernel,
        in_specs=[field, edge, edge, stat, stat, stat],
        out_specs=field,
        out_shape=field_b16,
        grid=(1,),
        compiler_params=params(16),
        name="normed",
    )(residual, *met2, stats2, norm_rows[2])

    normed_near = permute(normed, to_near)
    normed_pair = permute(normed, to_pair)
    normed_cross = permute(normed_near, to_pair)
    cot_near = permute(cotangent, to_near)
    cot_pair = permute(cotangent, to_pair)
    cot_cross = permute(cot_near, to_pair)

    def project(blocks, matrix, bias, transposed, name):
        return pl.pallas_call(
            functools.partial(project_kernel, transposed),
            in_specs=[field] * 4 + [whole(channels, channels), stat],
            out_specs=whole(4 * pixels, channels),
            out_shape=shape((4 * pixels, channels), BF16),
            grid=(1,),
            compiler_params=params(32),
            name=name,
        )(*blocks, matrix, bias)

    zero_rows = jnp.zeros((8, channels), F32)
    all_grads = project((cotangent, cot_pair, cot_near, cot_cross), proj_weight, zero_rows, True, "grad_att")

    totals_shape = shape((pixels // 256, 8, 256), F32)
    totals_spec = whole(pixels // 256, 8, 256)
    attended, query_grad, totals = pl.pallas_call(
        attend_kernel,
        in_specs=[field] * 5
        + [whole(2, channels, channels), whole(channels, channels), stat, whole(pixels, 128), whole(1, 4 * pixels)],
        out_specs=[field, field, totals_spec],
        out_shape=[field_b16, field_b16, totals_shape],
        scratch_shapes=[pltpu.VMEM((4 * pixels, channels), BF16)] * 2,
        grid=(1,),
        compiler_params=params(56),
        name="attend",
    )(normed, normed_pair, normed_near, normed_cross, all_grads, qk_weight, value_weight, bias_rows, column_tiles, row_tiles)

    totals_pair, totals_near, totals_cross = (permute(totals, to) for to in (to_pair, to_near, to_cross))
    cot32 = cotangent.astype(F32)
    cot_top, cot_bottom = cot32[:32], cot32[pixels - 32 :]
    near_edge = jnp.where(low == 0, cot_bottom, cot_top)
    cross_edge = jnp.where(low == 0, cot_top, cot_bottom)
    edge_near = permute(near_edge, to_near)
    edge_cross = permute(cross_edge, to_cross)
    wide_near = jnp.concatenate([met2[0][:32], edge_near], axis=0)
    wide_cross = jnp.concatenate([met2[1][:32], edge_cross], axis=0)

    all_queries = project((normed, normed_pair, normed_near, normed_cross), qk_weight[0], bias_rows, False, "queries")
    output = pl.pallas_call(
        out_kernel,
        in_specs=[field, field, whole(channels, channels), stat],
        out_specs=field,
        out_shape=field_b16,
        grid=(1,),
        compiler_params=params(16),
        name="output",
    )(attended, residual, proj_weight, block8(proj_bias))
    output = permute(output, turned)

    blocks = pixels // 256
    key_grad, value_grad, normed_grad, near3, cross3, stats3, sums3 = pl.pallas_call(
        key_kernel,
        in_specs=[SMEM, field, whole(4 * pixels, channels), whole(4 * pixels, channels), field]
        + [whole(2, channels, channels), whole(channels, channels), stat]
        + [totals_spec] * 4
        + [whole(pixels, 128), whole(4 * blocks, 1, 256), field, stat, edge, edge, stat, stat],
        out_specs=[field, field, field, edge, edge, stat, stat],
        out_shape=[field_b16, field_b16, field_f32, row_f32, row_f32, stat_f32, stat_f32],
        scratch_shapes=[pltpu.VMEM((pixels, channels), BF16)] * 2 + [pltpu.VMEM((pixels, channels), F32)] * 2,
        grid=(1,),
        compiler_params=params(56),
        name="key_value_grad",
    )(
        side, normed, all_queries, all_grads, query_grad, qk_weight, value_weight, bias_rows,
        totals, totals_pair, totals_near, totals_cross, column_tiles, row_tiles.reshape(4 * blocks, 1, 256),
        residual, stats2, *met2, norm_rows[2],
    )
    met3 = meet(near3, cross3, stats3)

    def piece_shapes(taps):
        dims = (PIECES, taps, channels // PIECES, channels // 2)
        return [whole(*dims)] * 2, [shape(dims, BF16)] * 2

    specs, shapes = piece_shapes(4)
    matrix_first, matrix_second, matrix_sums = pl.pallas_call(
        matrix_kernel,
        in_specs=[SMEM] + [field] * 6,
        out_specs=specs + [stat],
        out_shape=shapes + [stat_f32],
        scratch_shapes=[pltpu.VMEM((channels, pixels), BF16)],
        grid=(1,),
        compiler_params=params(32),
        name="matrix_grad",
    )(place, normed, query_grad, key_grad, value_grad, attended, cotangent)

    def weight_grad(x, x_near, x_cross, stats, met, grad, grad_met, grad_stats, rows, act, cot, name):
        specs, shapes = piece_shapes(9)
        wide = whole(x_near.shape[0], channels)
        extra_in, extra_out = ([field], [field]) if cot is not None else ([], [])
        near, cross, pair = met
        g_near, g_cross, g_pair = grad_met
        spread = (3, pixels + 64, channels)
        return pl.pallas_call(
            functools.partial(weight_grad_kernel, cot is not None),
            in_specs=[SMEM, SMEM, field, wide, wide, stat, edge, edge, stat, field, edge, edge, stat, stat, stat, field, mask_block]
            + extra_in,
            out_specs=specs + [whole(*spread), stat] + extra_out,
            out_shape=shapes + [shape(spread, BF16), stat_f32] + ([field_f32] if extra_out else []),
            scratch_shapes=[pltpu.VMEM((pixels + 80, channels), F32), pltpu.VMEM((channels, pixels), BF16)],
            grid=(3,),
            compiler_params=params(56),
            name=name,
        )(
            place, side, x, x_near, x_cross, stats, near, cross, pair, grad, g_near, g_cross, g_pair, grad_stats,
            rows, act, masks, *([cot] if cot is not None else []),
        )

    def conv_back(shifted, index, x, stats, met, rows, name):
        return pl.pallas_call(
            conv_back_kernel,
            in_specs=[
                SMEM, whole(3, pixels + 64, channels), mask_block,
                pl.BlockSpec((None, None, 3, channels, channels), lambda i: (index, 2 - i, 0, 0, 0)),
                field, stat, edge, edge, stat, stat,
            ],
            out_specs=[field, edge, edge, stat, stat],
            out_shape=[field_f32, row_f32, row_f32, stat_f32, stat_f32],
            grid=(3,),
            compiler_params=params(40),
            name=name,
        )(side, shifted, masks, conv_weight, x, stats, *met, rows)

    two_first, two_second, shifted_two, bias_two, residual_grad = weight_grad(
        residual, wide_near, wide_cross, stats2, met2, normed_grad, met3, stats3, norm_rows[2], act_two, cotangent,
        "weight_two_grad",
    )
    grad_two, near4, cross4, stats4, sums4 = conv_back(shifted_two, 1, middle, stats1, met1, norm_rows[1], "conv_two_back")
    met4 = meet(near4, cross4, stats4)
    one_first, one_second, shifted_one, bias_one = weight_grad(
        middle, met1[0], met1[1], stats1, met1, grad_two, met4, stats4, norm_rows[1], act_one, None, "weight_one_grad"
    )
    grad_one, near5, cross5, stats5, sums5 = conv_back(shifted_one, 0, x, own0, met0, norm_rows[0], "conv_one_back")
    met5 = meet(near5, cross5, stats5)
    image_grad = pl.pallas_call(
        last_kernel,
        in_specs=[field, edge, edge, stat, stat, field, stat, edge, edge, stat, stat, field],
        out_specs=field,
        out_shape=field_b16,
        grid=(1,),
        compiler_params=params(32),
        name="image_grad",
    )(grad_one, *met5, stats5, x, own0, *met0, norm_rows[0], residual_grad)
    image_grad = permute(image_grad, turned)

    far_bit = 2 * lanes
    orders = ((1, 2, 4, near_bit, far_bit), (1, 4, 2, near_bit, far_bit))
    others = []
    bit = 8
    while bit < lanes:
        others.append(bit)
        bit *= 2

    def swap(x, bit):
        return permute(x, lambda i: i ^ bit)

    def total(pieces, order):
        for bit in order:
            half = pieces.shape[0] // 2
            coming = swap(pieces[half:], bit)
            pieces = (pieces[:half].astype(F32) + coming.astype(F32)).astype(BF16)
        for bit in others:
            pieces = (pieces.astype(F32) + swap(pieces, bit).astype(F32)).astype(BF16)
        for bit in order[::-1]:
            pieces = jnp.concatenate([pieces, swap(pieces, bit)], axis=0)
        return pieces

    matrix_parts = total(matrix_first, orders[0]), total(matrix_second, orders[1])
    two_parts = total(two_first, orders[0]), total(two_second, orders[1])
    one_parts = total(one_first, orders[0]), total(one_second, orders[1])

    def unpack(parts, taps, slots, base, into, name):
        block = pl.BlockSpec((PIECES, 1, channels // PIECES, channels // 2), lambda i: (0, i, 0, 0))
        extra = [] if into is None else [into]
        return pl.pallas_call(
            unpack_kernel,
            in_specs=[SMEM, block, block] + [pl.BlockSpec(memory_space=pl.ANY)] * len(extra),
            out_specs=pl.BlockSpec((1, channels, channels), lambda i: (base + i, 0, 0)),
            out_shape=shape((slots, channels, channels), F32),
            grid=(taps,),
            input_output_aliases={3: 0} if extra else {},
            compiler_params=params(16),
            name=name,
        )(place, *parts, *extra)

    matrices = unpack(matrix_parts, 4, 4, 0, None, "unpack_matrices")
    weights = unpack(two_parts, 9, 18, 9, None, "unpack_two")
    weights = unpack(one_parts, 9, 18, 0, weights, "unpack_one")

    small = jnp.concatenate(
        [bias_one[:1], bias_two[:1], sums5[:1], sums4[:1], sums3[:1], sums5[1:2], sums4[1:2], sums3[1:2], matrix_sums[:3]]
        + [jnp.zeros((5, channels), F32)],
        axis=0,
    )
    bit = 1
    while bit < devices:
        small = small + swap(small, bit)
        bit *= 2

    return (
        output.reshape(1, band, width, channels),
        image_grad.reshape(1, band, width, channels),
        weights.reshape(2, 3, 3, channels, channels),
        small[0:2],
        small[2:5],
        small[5:8],
        matrices[0:2],
        matrices[2],
        matrices[3],
        small[8:10],
        small[10],
    )


def solution(mesh):
    split = P("batch", "seq", None, None)
    in_specs = (split, P("batch", "seq", None), split) + (P(),) * 9
    out_specs = (split, split) + (P(),) * 9
    return jax.shard_map(body, mesh=mesh, in_specs=in_specs, out_specs=out_specs, check_vma=False)
```

```python
import functools

import jax
import jax.numpy as jnp
from jax import lax
from jax.experimental import pallas as pl
from jax.experimental.pallas import tpu as pltpu
from jax.sharding import PartitionSpec as P

GROUPS = 32
EPSILON = 1e-06
MASKED_SCORE = -1e30
F32 = jnp.float32
BF16 = jnp.bfloat16
MIB = 1024 * 1024
PIECES = 32


def params(mib):
    return pltpu.CompilerParams(vmem_limit_bytes=mib * MIB)


def shape(dims, dtype):
    return jax.ShapeDtypeStruct(dims, dtype)


SMEM = pl.BlockSpec(memory_space=pltpu.SMEM)


def whole(*dims):
    return pl.BlockSpec(dims, lambda *_: (0,) * len(dims))


def group_sum(row):
    channels = row.shape[1]
    lane = lax.broadcasted_iota(jnp.int32, row.shape, 1)
    step = 1
    while step < channels // GROUPS:
        ahead = pltpu.roll(row, channels - step, 1)
        behind = pltpu.roll(row, step, 1)
        row = row + jnp.where((lane & step) == 0, ahead, behind)
        step *= 2
    return row


def rows_of(*parts):
    channels = parts[0].shape[1]
    line = lax.broadcasted_iota(jnp.int32, (8, channels), 0)
    out = jnp.zeros((8, channels), F32)
    for i, part in enumerate(parts):
        out = jnp.where(line == i, jnp.broadcast_to(part, (8, channels)), out)
    return out


def eight(row):
    return jnp.broadcast_to(row, (8, row.shape[1]))


def local_stats(values, channels, pixels):
    count = float(pixels * (channels // GROUPS))
    mean = group_sum(eight(jnp.sum(values, axis=0, keepdims=True)))[0:1] / count
    centered = values - mean
    square = group_sum(eight(jnp.sum(centered * centered, axis=0, keepdims=True)))[0:1]
    return mean, square


def joined_stats(own, near, cross, pair, pixels):
    bands = [own[0:2], near[32:34], cross[32:34], pair[0:2]]
    channels = bands[0].shape[1]
    count = float(pixels * (channels // GROUPS))
    mean = (bands[0][0:1] + bands[1][0:1] + bands[2][0:1] + bands[3][0:1]) * 0.25
    total = 0.0
    for band in bands:
        gap = band[0:1] - mean
        total = total + band[1:2] + count * gap * gap
    return mean, lax.rsqrt(total / (4.0 * count) + EPSILON)


def joined_sums(own, near, cross, pair, pixels):
    bands = [own[0:2], near[32:34], cross[32:34], pair[0:2]]
    channels = bands[0].shape[1]
    count = 4.0 * float(pixels * (channels // GROUPS))
    sums = (bands[0] + bands[1]) + (bands[2] + bands[3])
    return sums[0:1] / count, sums[1:2] / count


def sigmoid(values):
    return 0.5 * jnp.tanh(0.5 * values) + 0.5


def edges_out(side_ref, out_ref, near_ref, cross_ref, stats):
    pixels = out_ref.shape[0]
    side = side_ref[0]
    last = pixels - 32
    near_ref[0:32, :] = out_ref[pl.ds(pl.multiple_of(last * (1 - side), 32), 32), :].astype(F32)
    cross_ref[0:32, :] = out_ref[pl.ds(pl.multiple_of(last * side, 32), 32), :].astype(F32)
    near_ref[32:40, :] = stats
    cross_ref[32:40, :] = stats


def columns_of(frame, shifted, rows):
    for b in range(3):
        shifted[b] = frame[7 + b : 7 + b + rows, :].astype(BF16)


def masked(values, mask):
    channels = values.shape[1]
    return [values[:, i * 128 : (i + 1) * 128] * mask for i in range(channels // 128)]


def tap_rows(shifted, mask_ref, start, count, row):
    parts = []
    for b in range(3):
        block = shifted[b, pl.ds(pl.multiple_of(row * 32 + start, 32), count), :]
        parts += masked(block, mask_ref[b, start : start + count, :])
    return parts


def first_kernel(image_ref, tiles_ref, side_ref, near_ref, cross_ref, stats_ref):
    pixels, channels = image_ref.shape
    mean, square = local_stats(image_ref[...].astype(F32), channels, pixels)
    stats = rows_of(mean, square, tiles_ref[0:1], tiles_ref[1:2])
    stats_ref[...] = stats
    edges_out(side_ref, image_ref, near_ref, cross_ref, stats)


def mask_kernel(where_ref, own_ref, near_ref, cross_ref, pair_ref, mask_ref, column_ref, row_ref, frame):
    side, first, last = where_ref[0], where_ref[1], where_ref[2]

    def line(ref, base):
        return jnp.concatenate([ref[base + 2 : base + 3, :], ref[base + 3 : base + 4, :]], axis=1)

    own, near, cross, pair = line(own_ref, 0), line(near_ref, 32), line(cross_ref, 32), line(pair_ref, 0)
    pixels = own.shape[1]
    row_ref[...] = jnp.concatenate([own, pair, near, cross], axis=1)

    def upright(row):
        return jnp.transpose(jnp.broadcast_to(row, (128, row.shape[1])))

    column = upright(own)
    column_ref[...] = column
    above = jnp.where(side == 0, cross[:, pixels - 128 :], near[:, pixels - 128 :])
    below = jnp.where(side == 0, near[:, :128], cross[:, :128])
    outside = jnp.full((32, 128), -1.0, F32)
    frame[0:8, :] = jnp.zeros((8, 128), F32)
    frame[8:40, :] = jnp.where(first == 1, outside, upright(above)[96:128, :])
    frame[40 : 40 + pixels, :] = column
    frame[40 + pixels : 72 + pixels, :] = jnp.where(last == 1, outside, upright(below)[0:32, :])
    frame[72 + pixels : 80 + pixels, :] = jnp.zeros((8, 128), F32)
    place = lax.broadcasted_iota(jnp.int32, (pixels, 128), 0) & 31
    for a in range(3):
        for b in range(3):
            start = 8 + a * 32 + b - 1
            same = frame[start : start + pixels, :] == column
            if b == 0:
                same = same & (place > 0)
            if b == 2:
                same = same & (place < 31)
            mask_ref[a * 3 + b] = jnp.where(same, 1.0, 0.0).astype(BF16)


def conv_kernel(
    side_ref, x_ref, near_ref, cross_ref, pair_ref, stats_ref, rows_ref, mask_ref, weight_ref, skip_ref,
    out_ref, act_ref, near_out, cross_out, stats_out, frame, shifted,
):
    row = pl.program_id(0)
    pixels, channels = x_ref.shape

    @pl.when(row == 0)
    def _():
        mean, inverse = joined_stats(stats_ref[...], near_ref[...], cross_ref[...], pair_ref[...], pixels)
        scale, shift, bias = rows_ref[0:1, :], rows_ref[1:2, :], rows_ref[2:3, :]

        def act(values):
            pre = (values - mean) * inverse * scale + shift
            return pre * sigmoid(pre)

        side = side_ref[0]
        near, cross = near_ref[0:32, :], cross_ref[0:32, :]
        frame[0:8, :] = jnp.zeros((8, channels), F32)
        frame[8:40, :] = act(jnp.where(side == 0, cross, near))
        frame[40 : 40 + pixels, :] = act(x_ref[...].astype(F32))
        frame[40 + pixels : 72 + pixels, :] = act(jnp.where(side == 0, near, cross))
        frame[72 + pixels : 80 + pixels, :] = jnp.zeros((8, channels), F32)
        columns_of(frame, shifted, pixels + 64)
        act_ref[...] = shifted[1, 32 : 32 + pixels, :]
        start = jnp.broadcast_to(bias, (pixels, channels))
        if skip_ref is not None:
            start = start + skip_ref[...].astype(F32)
        out_ref[...] = start

    weight = weight_ref[...].reshape(3 * channels, channels)
    for i in range(pixels // 256):
        taps = jnp.concatenate(tap_rows(shifted, mask_ref, i * 256, 256, row), axis=1)
        out_ref[i * 256 : (i + 1) * 256, :] += jnp.dot(taps, weight, preferred_element_type=F32)

    @pl.when(row == 2)
    def _():
        mean, square = local_stats(out_ref[...], channels, pixels)
        stats = rows_of(mean, square)
        stats_out[...] = stats
        edges_out(side_ref, out_ref, near_out, cross_out, stats)


def normed_kernel(x_ref, near_ref, cross_ref, pair_ref, stats_ref, rows_ref, out_ref):
    pixels = x_ref.shape[0]
    mean, inverse = joined_stats(stats_ref[...], near_ref[...], cross_ref[...], pair_ref[...], pixels)
    out_ref[...] = ((x_ref[...] - mean) * inverse * rows_ref[0:1, :] + rows_ref[1:2, :]).astype(BF16)


def nn(left, right):
    return jnp.dot(left, right, preferred_element_type=F32)


def nt(left, right):
    return lax.dot_general(left, right, (((1,), (1,)), ((), ())), preferred_element_type=F32)


def early_kernel(
    own_ref, pair_ref, cot_own, cot_pair, qk_ref, value_ref, proj_ref, bias_ref, keys_ref, values_ref, queries_ref, grads_ref
):
    pixels = own_ref.shape[0]
    for i, (rows_ref, cot_ref) in enumerate(((own_ref, cot_own), (pair_ref, cot_pair))):
        part = slice(i * pixels, (i + 1) * pixels)
        rows = rows_ref[...]
        queries_ref[part, :] = (nn(rows, qk_ref[0]) + bias_ref[0:1, :]).astype(BF16)
        keys_ref[part, :] = nn(rows, qk_ref[1]).astype(BF16)
        values_ref[part, :] = (nn(rows, value_ref[...]) + bias_ref[1:2, :]).astype(BF16)
        grads_ref[part, :] = nt(cot_ref[...], proj_ref[...]).astype(BF16)


def attend_kernel(
    near_ref, cross_ref, keys_ref, values_ref, queries_ref, grads_ref, qk_ref, value_ref, bias_ref, column_ref, row_ref,
    attended_ref, query_grad_ref, totals_ref, far_keys, far_values,
):
    pixels, channels = near_ref.shape
    scale = channels ** (-0.5)
    for i, ref in enumerate((near_ref, cross_ref)):
        part = slice(i * pixels, (i + 1) * pixels)
        rows = ref[...]
        far_keys[part, :] = nn(rows, qk_ref[1]).astype(BF16)
        far_values[part, :] = (nn(rows, value_ref[...]) + bias_ref[1:2, :]).astype(BF16)
    block = totals_ref.shape[2]
    halves = ((keys_ref, values_ref, slice(0, 2 * pixels)), (far_keys, far_values, slice(2 * pixels, 4 * pixels)))

    def step(i, carry):
        part = pl.ds(pl.multiple_of(i * block, block), block)
        queries, upstream = queries_ref[part, :], grads_ref[part, :]
        column = column_ref[part, 0:1]
        scores = []
        for keys, _, span in halves:
            product = nt(queries, keys[...]) * scale
            scores.append(jnp.where(column == row_ref[:, span], product, MASKED_SCORE))
        top = jnp.maximum(*[jnp.max(s, axis=1, keepdims=True) for s in scores])
        weights = [jnp.exp(s - top) for s in scores]
        total = sum(jnp.sum(w, axis=1, keepdims=True) for w in weights)
        inverse = 1.0 / total
        attended = sum(nn(w.astype(BF16), values[...]) for w, (_, values, _) in zip(weights, halves)) * inverse
        attended_ref[part, :] = attended.astype(BF16)
        delta = jnp.sum(attended * upstream.astype(F32), axis=1, keepdims=True)
        query_grad = 0.0
        for w, (keys, values, _) in zip(weights, halves):
            prob_grad = nt(upstream, values[...])
            score_grad = (w * inverse * (prob_grad - delta)).astype(BF16)
            query_grad = query_grad + nn(score_grad, keys[...])
        query_grad_ref[part, :] = (query_grad * scale).astype(BF16)
        log_total = jnp.transpose(jnp.broadcast_to(top + jnp.log(total), (block, 128)))
        turned = jnp.transpose(jnp.broadcast_to(delta, (block, 128)))
        totals_ref[i, 0:1, :] = log_total[0:1, :]
        totals_ref[i, 1:2, :] = turned[0:1, :]
        totals_ref[i, 2:8, :] = jnp.zeros((6, block), F32)
        return carry

    lax.fori_loop(0, pixels // block, step, 0)


def out_kernel(attended_ref, residual_ref, matrix_ref, bias_ref, out_ref):
    out_ref[...] = (residual_ref[...] + nn(attended_ref[...], matrix_ref[...]) + bias_ref[0:1, :]).astype(BF16)


def norm_back_sums(upstream, hat, gain):
    outer = jnp.sum(upstream * hat, axis=0, keepdims=True)
    inner = jnp.sum(upstream, axis=0, keepdims=True)
    first = group_sum(eight(inner * gain))[0:1]
    second = group_sum(eight(outer * gain))[0:1]
    return rows_of(outer, inner), rows_of(first, second)


def key_kernel(
    side_ref, keys, values, queries_ref, grads_ref, near_hbm, cross_hbm, cot_near_hbm, cot_cross_hbm, query_grad_hbm,
    qk_ref, value_ref, proj_ref, bias_ref,
    totals_own, totals_pair, totals_near, totals_cross, column_ref, row_ref,
    residual_hbm, stats_ref, near_ref, cross_ref, pair_ref, rows_ref,
    key_grad_ref, value_grad_ref, normed_grad_ref, near_out, cross_out, stats_out, sums_out,
    key_sum, value_sum, far, query_grad_ref, residual_ref, arrived,
):
    pixels, channels = keys.shape
    scale = channels ** (-0.5)
    coming = [
        pltpu.make_async_copy(source, target, arrived.at[i])
        for i, (source, target) in enumerate(
            (
                (near_hbm, far.at[0]), (cot_near_hbm, far.at[1]), (cross_hbm, far.at[2]), (cot_cross_hbm, far.at[3]),
                (query_grad_hbm, query_grad_ref), (residual_hbm, residual_ref),
            )
        )
    ]
    for copy in coming:
        copy.start()
    key_sum[...] = jnp.zeros_like(key_sum)
    value_sum[...] = jnp.zeros_like(value_sum)
    chunk = totals_own.shape[2]
    blocks = pixels // chunk

    def add(queries, upstream, totals, i, at):
        scores = nt(keys[...], queries) * scale
        weights = jnp.exp(scores - totals[i, 0:1, :])
        weights = jnp.where(column_ref[:, 0:1] == row_ref[at, 0:1, :], weights, 0.0)
        value_sum[...] += nn(weights.astype(BF16), upstream)
        prob_grad = nt(values[...], upstream)
        score_grad = (weights * (prob_grad - totals[i, 1:2, :])).astype(BF16)
        key_sum[...] += nn(score_grad, queries)

    for group, totals in enumerate((totals_own, totals_pair)):

        def step(i, carry, group=group, totals=totals):
            part = pl.ds(pl.multiple_of(group * pixels + i * chunk, chunk), chunk)
            add(queries_ref[part, :], grads_ref[part, :], totals, i, group * blocks + i)
            return carry

        lax.fori_loop(0, blocks, step, 0)
    for group, totals in enumerate((totals_near, totals_cross)):
        coming[2 * group].wait()
        coming[2 * group + 1].wait()

        def far_step(i, carry, group=group, totals=totals):
            part = pl.ds(pl.multiple_of(i * chunk, chunk), chunk)
            queries = (nn(far[2 * group, part, :], qk_ref[0]) + bias_ref[0:1, :]).astype(BF16)
            upstream = nt(far[2 * group + 1, part, :], proj_ref[...]).astype(BF16)
            add(queries, upstream, totals, i, (group + 2) * blocks + i)
            return carry

        lax.fori_loop(0, blocks, far_step, 0)
    coming[4].wait()
    coming[5].wait()
    key_grad = (key_sum[...] * scale).astype(BF16)
    value_grad = value_sum[...].astype(BF16)
    key_grad_ref[...] = key_grad
    value_grad_ref[...] = value_grad
    normed_grad = nt(query_grad_ref[...], qk_ref[0]) + nt(key_grad, qk_ref[1]) + nt(value_grad, value_ref[...])
    normed_grad_ref[...] = normed_grad
    mean, inverse = joined_stats(stats_ref[...], near_ref[...], cross_ref[...], pair_ref[...], pixels)
    hat = (residual_ref[...] - mean) * inverse
    sums, groups = norm_back_sums(normed_grad, hat, rows_ref[0:1, :])
    sums_out[...] = sums
    stats_out[...] = groups
    edges_out(side_ref, normed_grad_ref, near_out, cross_out, groups)


def scatter_pieces(place_ref, product, tap, keep_ref, send_ref, matrix):
    rows, channels = product.shape
    half, height = channels // 2, rows // PIECES
    matrix[...] = product.astype(BF16)
    for q in range(PIECES):
        into = keep_ref if q < PIECES // 2 else send_ref
        for stream in range(2):
            start = pl.multiple_of((q ^ place_ref[stream]) * height, height)
            into[stream, q % (PIECES // 2), tap] = matrix[pl.ds(start, height), stream * half : (stream + 1) * half]


def tn(left, right):
    return lax.dot_general(left, right, (((0,), (0,)), ((), ())), preferred_element_type=F32)


def matrix_kernel(
    place_ref, normed_ref, query_grad_ref, key_grad_ref, value_grad_ref, attended_ref, cotangent_ref,
    keep_ref, send_ref, sums_ref, turned, matrix,
):
    turned[...] = jnp.transpose(normed_ref[...])
    for tap, ref in enumerate((query_grad_ref, key_grad_ref, value_grad_ref)):
        scatter_pieces(place_ref, nn(turned[...], ref[...]), tap, keep_ref, send_ref, matrix)
    turned[...] = jnp.transpose(attended_ref[...])
    scatter_pieces(place_ref, nn(turned[...], cotangent_ref[...]), 3, keep_ref, send_ref, matrix)
    total = [
        jnp.sum(ref[...].astype(F32), axis=0, keepdims=True)
        for ref in (query_grad_ref, value_grad_ref, cotangent_ref)
    ]
    sums_ref[...] = rows_of(*total)


def weight_grad_kernel(
    with_cotangent, place_ref, side_ref, x_ref, x_near, x_cross, stats_ref, near_ref, cross_ref, pair_ref,
    g_ref, g_near, g_cross, g_pair, g_stats, rows_ref, act_ref, mask_ref, *rest,
):
    if with_cotangent:
        cot_ref, cot_edges, matrix_keep, matrix_send = rest[0], rest[1:5], rest[5], rest[6]
        keep_ref, send_ref, shifted, sums_ref, own_ref, frame, turned, matrix = rest[7:]
    else:
        keep_ref, send_ref, shifted, sums_ref, frame, turned, matrix = rest
    row = pl.program_id(0)
    pixels, channels = x_ref.shape

    @pl.when(row == 0)
    def _():
        mean, inverse = joined_stats(stats_ref[...], near_ref[...], cross_ref[...], pair_ref[...], pixels)
        mean_h, mean_hx = joined_sums(g_stats[...], g_near[...], g_cross[...], g_pair[...], pixels)
        gain = rows_ref[0:1, :]
        side = side_ref[0]

        def back(grad, values):
            hat = (values - mean) * inverse
            return inverse * (grad * gain - mean_h - hat * mean_hx)

        def pick(near, cross):
            return jnp.where(side == 0, cross, near), jnp.where(side == 0, near, cross)

        g_above, g_below = pick(g_near[0:32, :], g_cross[0:32, :])
        x_above, x_below = pick(x_near[0:32, :], x_cross[0:32, :])
        above, below = back(g_above, x_above), back(g_below, x_below)
        own = back(g_ref[...], x_ref[...])
        if with_cotangent:
            near_top, near_bottom, cross_top, cross_bottom = [ref[...].astype(F32) for ref in cot_edges]
            above = above + jnp.where(side == 0, cross_bottom, near_bottom)
            below = below + jnp.where(side == 0, near_top, cross_top)
            own = own + cot_ref[...].astype(F32)
            own_ref[...] = own
            for tap in range(4):
                keep_ref[:, :, 9 + tap] = matrix_keep[:, :, tap]
                send_ref[:, :, 9 + tap] = matrix_send[:, :, tap]
        sums_ref[...] = rows_of(jnp.sum(own, axis=0, keepdims=True))
        frame[0:8, :] = jnp.zeros((8, channels), F32)
        frame[8:40, :] = above
        frame[40 : 40 + pixels, :] = own
        frame[40 + pixels : 72 + pixels, :] = below
        frame[72 + pixels : 80 + pixels, :] = jnp.zeros((8, channels), F32)
        columns_of(frame, shifted, pixels + 64)
        turned[...] = jnp.transpose(act_ref[...])

    for b in range(3):
        block = shifted[b, pl.ds(pl.multiple_of(row * 32, 32), pixels), :]
        block = jnp.concatenate(masked(block, mask_ref[b]), axis=1)
        product = nn(turned[...], block)
        scatter_pieces(place_ref, product, 8 - row * 3 - b, keep_ref, send_ref, matrix)


def conv_back_kernel(
    side_ref, shifted, mask_ref, weight_ref, x_ref, stats_ref, near_ref, cross_ref, pair_ref, rows_ref,
    out_ref, near_out, cross_out, stats_out, sums_out,
):
    row = pl.program_id(0)
    pixels, channels = x_ref.shape

    @pl.when(row == 0)
    def _():
        out_ref[...] = jnp.zeros_like(out_ref)

    weight = jnp.concatenate([weight_ref[2 - b] for b in range(3)], axis=1)
    for i in range(pixels // 256):
        taps = jnp.concatenate(tap_rows(shifted, mask_ref, i * 256, 256, row), axis=1)
        out_ref[i * 256 : (i + 1) * 256, :] += nt(taps, weight)

    @pl.when(row == 2)
    def _():
        mean, inverse = joined_stats(stats_ref[...], near_ref[...], cross_ref[...], pair_ref[...], pixels)
        gain, shift = rows_ref[0:1, :], rows_ref[1:2, :]
        hat = (x_ref[...].astype(F32) - mean) * inverse
        pre = hat * gain + shift
        gate = sigmoid(pre)
        upstream = out_ref[...] * (gate * (1.0 + pre * (1.0 - gate)))
        out_ref[...] = upstream
        sums, groups = norm_back_sums(upstream, hat, gain)
        sums_out[...] = sums
        stats_out[...] = groups
        edges_out(side_ref, out_ref, near_out, cross_out, groups)


def last_kernel(
    g_ref, g_near, g_cross, g_pair, g_stats, x_ref, stats_ref, near_ref, cross_ref, pair_ref, rows_ref, add_ref,
    bias_one, bias_two, sums_one, sums_two, sums_three, matrix_sums, out_ref, small_ref,
):
    pixels = x_ref.shape[0]
    small_ref[...] = jnp.zeros_like(small_ref)
    parts = [bias_one[0:1], bias_two[0:1]]
    parts += [ref[i : i + 1] for i in range(2) for ref in (sums_one, sums_two, sums_three)]
    parts += [matrix_sums[i : i + 1] for i in range(3)]
    for i, part in enumerate(parts):
        small_ref[i : i + 1, :] = part
    mean, inverse = joined_stats(stats_ref[...], near_ref[...], cross_ref[...], pair_ref[...], pixels)
    mean_h, mean_hx = joined_sums(g_stats[...], g_near[...], g_cross[...], g_pair[...], pixels)
    hat = (x_ref[...].astype(F32) - mean) * inverse
    grad = inverse * (g_ref[...] * rows_ref[0:1, :] - mean_h - hat * mean_hx)
    out_ref[...] = (add_ref[...] + grad).astype(BF16)


def unpack_kernel(place_ref, own_ref, other_ref, *rest):
    out_ref = rest[-1]
    height, half = own_ref.shape[3], own_ref.shape[4]
    for tap in range(out_ref.shape[0]):
        for q in range(PIECES):
            pieces = own_ref if q < PIECES // 2 else other_ref
            for stream in range(2):
                start = pl.multiple_of((q ^ place_ref[stream]) * height, height)
                values = pieces[stream, q % (PIECES // 2), tap].astype(F32)
                out_ref[tap, pl.ds(start, height), stream * half : (stream + 1) * half] = values


def body(
    image,
    tile_map,
    out_grad,
    conv_weight,
    conv_bias,
    norm_gain,
    norm_shift,
    qk_weight,
    value_weight,
    proj_weight,
    qv_bias,
    proj_bias,
):
    band, width, channels = image.shape[1], image.shape[2], image.shape[3]
    pixels = band * width
    lanes = lax.axis_size("batch")
    devices = 4 * lanes

    def turned(flat):
        s, b = flat // lanes, flat % lanes
        core, high = b % 2, s // 2
        return (core * 2 + s % 2) * lanes + (b - core + high)

    def xored(flat, bits):
        return flat ^ bits

    def permute(x, to):
        return lax.ppermute(x, ("seq", "batch"), [(i, to(i)) for i in range(devices)])

    near_bit, pair_bit = lanes, 1

    def to_near(i):
        return i ^ near_bit

    def to_pair(i):
        return i ^ pair_bit

    def to_cross(i):
        return i ^ (near_bit | pair_bit)

    def meet(near, cross, stats):
        return permute(near, to_near), permute(cross, to_cross), permute(stats, to_pair)

    seq, lane = lax.axis_index("seq"), lax.axis_index("batch")
    core, low, high = lane % 2, seq % 2, seq // 2
    side = low.astype(jnp.int32).reshape(1)
    spot = jnp.stack([low, ((low == 0) & (core == 0)), ((low == 1) & (core == 1))]).astype(jnp.int32)
    x_bit, y_bit = (lane // 2) % 2, (lane // 4) % 2
    tail = low * 2 + high
    place = jnp.stack(
        [core * 16 + x_bit * 8 + y_bit * 4 + tail, core * 16 + y_bit * 8 + x_bit * 4 + tail]
    ).astype(jnp.int32)

    def block8(*rows):
        rows = [r.astype(F32).reshape(1, channels) for r in rows]
        return jnp.concatenate(rows + [jnp.zeros((8 - len(rows), channels), F32)], axis=0)

    norm_rows = [block8(norm_gain[i], norm_shift[i], conv_bias[min(i, 1)]) for i in range(3)]
    bias_rows = block8(qv_bias[0], qv_bias[1], proj_bias, jnp.zeros((channels,), F32))

    row_f32 = shape((40, channels), F32)
    stat_f32 = shape((8, channels), F32)
    field_f32 = shape((pixels, channels), F32)
    field_b16 = shape((pixels, channels), BF16)
    field = whole(pixels, channels)
    edge = whole(40, channels)
    stat = whole(8, channels)

    def call(kernel, name, operands, in_specs, outs, mib, flops=0, scratch=(), grid=(1,), after=(), aliases=None):
        count = len(operands)

        def run(*refs):
            kernel(*refs[:count], *refs[count + len(after) :])

        moved = sum(o.size * o.dtype.itemsize for o in operands) + sum(o.size * o.dtype.itemsize for _, o in outs)
        return pl.pallas_call(
            run if after else kernel,
            in_specs=list(in_specs) + [pl.BlockSpec(memory_space=pl.ANY)] * len(after),
            out_specs=[spec for spec, _ in outs],
            out_shape=[out for _, out in outs],
            scratch_shapes=list(scratch),
            grid=grid,
            input_output_aliases=aliases or {},
            compiler_params=params(mib),
            cost_estimate=pl.CostEstimate(flops=int(flops), bytes_accessed=int(moved), transcendentals=0),
            name=name,
        )(*operands, *after)

    def behind(x, *deps):
        return lax.optimization_barrier((x,) + deps)[0]

    row_out, stat_out = (edge, row_f32), (stat, stat_f32)
    matmul = 2.0 * pixels * channels * channels

    image_flat = image.reshape(pixels, channels)
    cot_flat = out_grad.reshape(pixels, channels)
    tiles = tile_map.astype(F32).reshape(2, pixels // 2)
    x = permute(image_flat, turned)
    near0, cross0, stats0 = call(
        first_kernel, "first", (image_flat, tiles, side), [field, whole(2, pixels // 2), SMEM],
        [row_out, row_out, stat_out], 16,
    )
    own0 = permute(stats0, turned)
    pair0 = permute(stats0, lambda i: to_pair(turned(i)))
    near0 = permute(near0, lambda i: to_near(turned(i)))
    cross0 = permute(cross0, lambda i: to_cross(turned(i)))
    masks, column_tiles, row_tiles = call(
        mask_kernel, "masks", (spot, own0, near0, cross0, pair0), [SMEM, stat, edge, edge, stat],
        [
            (whole(9, pixels, 128), shape((9, pixels, 128), BF16)),
            (whole(pixels, 128), shape((pixels, 128), F32)),
            (whole(1, 4 * pixels), shape((1, 4 * pixels), F32)),
        ],
        24, scratch=[pltpu.VMEM((pixels + 80, 128), F32)],
    )

    half = pixels // 2
    cot_first = permute(behind(cot_flat[:half], x), turned)

    mask_block = pl.BlockSpec((3, pixels, 128), lambda i: (i, 0, 0))

    def conv(x, met, stats, rows, index, skip, name, after=()):
        near, cross, pair = met
        specs = [
            SMEM, field, edge, edge, stat, stat, stat, mask_block,
            pl.BlockSpec((None, 1, 3, channels, channels), lambda i: (index, i, 0, 0, 0)),
        ]
        operands = [side, x, near, cross, pair, stats, rows, masks, conv_weight]
        kernel = conv_kernel
        if skip is None:

            def kernel(*refs):
                return conv_kernel(*refs[:9], None, *refs[9:])
        else:
            specs.append(field)
            operands.append(skip)
        return call(
            kernel, name, operands, specs,
            [(field, field_f32), (field, field_b16), row_out, row_out, stat_out],
            40, 9 * matmul,
            [pltpu.VMEM((pixels + 80, channels), F32), pltpu.VMEM((3, pixels + 64, channels), BF16)],
            (3,), after,
        )

    met0 = (near0, cross0, pair0)
    middle, act_one, near1, cross1, stats1 = conv(x, met0, own0, norm_rows[0], 0, None, "conv_one")
    met1 = meet(near1, cross1, stats1)
    cot_second = permute(behind(cot_flat[half:], cot_first, met1[0]), turned)
    residual, act_two, near2, cross2, stats2 = conv(
        middle, met1, stats1, norm_rows[1], 1, x, "conv_two", (cot_first,)
    )
    met2 = meet(near2, cross2, stats2)

    (normed,) = call(
        normed_kernel, "normed", (residual, *met2, stats2, norm_rows[2]), [field, edge, edge, stat, stat, stat],
        [(field, field_b16)], 16, after=(cot_second,),
    )
    cotangent = jnp.concatenate([cot_first, cot_second], axis=0)

    normed_near = permute(normed, to_near)
    normed_pair = permute(normed, to_pair)

    block = 512
    anywhere = pl.BlockSpec(memory_space=pl.ANY)
    blocks = pixels // block
    totals_out = (whole(blocks, 8, block), shape((blocks, 8, block), F32))
    square = whole(channels, channels)
    two_fields, two_b16 = whole(2 * pixels, channels), shape((2 * pixels, channels), BF16)
    cot_pair = permute(cotangent, to_pair)
    keys, values, queries, grads = call(
        early_kernel, "early",
        (normed, normed_pair, cotangent, cot_pair, qk_weight, value_weight, proj_weight, bias_rows),
        [field] * 4 + [whole(2, channels, channels), square, square, stat],
        [(two_fields, two_b16)] * 4, 32, 8 * matmul,
    )
    normed_cross = permute(behind(normed_near, keys), to_pair)
    cot_near = permute(behind(cotangent, normed_near), to_near)
    attended, query_grad, totals = call(
        attend_kernel, "attend",
        (normed_near, normed_cross, keys, values, queries, grads, qk_weight, value_weight, bias_rows,
         column_tiles, row_tiles),
        [field] * 2 + [two_fields] * 2 + [field] * 2
        + [whole(2, channels, channels), square, stat, whole(pixels, 128), whole(1, 4 * pixels)],
        [(field, field_b16), (field, field_b16), totals_out],
        58, 4 * matmul + 4 * 4 * matmul * pixels / channels,
        [pltpu.VMEM((2 * pixels, channels), BF16)] * 2,
    )

    totals_pair, totals_near, totals_cross = (permute(totals, to) for to in (to_pair, to_near, to_cross))
    cot_cross = permute(behind(cot_near, attended), to_pair)
    (output,) = call(
        out_kernel, "output", (attended, residual, proj_weight, block8(proj_bias)), [field, field, square, stat],
        [(field, field_b16)], 16, matmul, after=(cot_near,),
    )
    output_there = permute(output, turned)

    key_grad, value_grad, normed_grad, near3, cross3, stats3, sums3 = call(
        key_kernel, "key_value_grad",
        (side, keys, values, queries, grads, normed_near, normed_cross, cot_near, cot_cross,
         query_grad, qk_weight, value_weight, proj_weight, bias_rows,
         totals, totals_pair, totals_near, totals_cross, column_tiles, row_tiles.reshape(4 * blocks, 1, block),
         residual, stats2, *met2, norm_rows[2]),
        [SMEM] + [field] * 2 + [two_fields] * 2 + [anywhere] * 5 + [whole(2, channels, channels), square, square, stat]
        + [totals_out[0]] * 4
        + [whole(pixels, 128), whole(4 * blocks, 1, block), anywhere, stat, edge, edge, stat, stat],
        [(field, field_b16), (field, field_b16), (field, field_f32), row_out, row_out, stat_out, stat_out],
        60, 7 * matmul + 4 * 4 * matmul * pixels / channels,
        [pltpu.VMEM((pixels, channels), F32)] * 2
        + [
            pltpu.VMEM((4, pixels, channels), BF16), pltpu.VMEM((pixels, channels), BF16),
            pltpu.VMEM((pixels, channels), F32), pltpu.SemaphoreType.DMA((6,)),
        ],
        after=(output,),
    )
    met3 = meet(near3, cross3, stats3)

    def pieces(taps):
        dims = (2, PIECES // 2, taps, channels // PIECES, channels // 2)
        return [(whole(*dims), shape(dims, BF16))] * 2

    matrix_keep, matrix_send, matrix_sums = call(
        matrix_kernel, "matrix_grad", (place, normed, query_grad, key_grad, value_grad, attended, cotangent),
        [SMEM] + [field] * 6, pieces(4) + [stat_out], 32, 4 * matmul,
        [pltpu.VMEM((channels, pixels), BF16), pltpu.VMEM((channels, channels), BF16)],
    )

    def weight_grad(x, x_near, x_cross, stats, met, grad, grad_met, grad_stats, rows, act, cot, name, after=()):
        near, cross, pair = met
        g_near, g_cross, g_pair = grad_met
        spread = (3, pixels + 64, channels)
        extra, extra_in, extra_out = [], [], []
        if cot is not None:
            top = pl.BlockSpec((32, channels), lambda i: (0, 0))
            bottom = pl.BlockSpec((32, channels), lambda i: (pixels // 32 - 1, 0))
            extra = [cot, cot_near, cot_near, cot_cross, cot_cross, matrix_keep, matrix_send]
            extra_in = [field, top, bottom, top, bottom] + [spec for spec, _ in pieces(4)]
            extra_out = [(field, field_f32)]
        return call(
            functools.partial(weight_grad_kernel, cot is not None), name,
            [place, side, x, x_near, x_cross, stats, near, cross, pair, grad, g_near, g_cross, g_pair, grad_stats,
             rows, act, masks] + extra,
            [SMEM, SMEM, field, edge, edge, stat, edge, edge, stat, field, edge, edge, stat, stat, stat, field, mask_block]
            + extra_in,
            pieces(9 if cot is None else 13) + [(whole(*spread), shape(spread, BF16)), stat_out] + extra_out,
            58, 9 * matmul,
            [pltpu.VMEM((pixels + 80, channels), F32), pltpu.VMEM((channels, pixels), BF16), pltpu.VMEM((channels, channels), BF16)],
            (3,), after,
        )

    def conv_back(shifted, index, x, stats, met, rows, name, after=()):
        return call(
            conv_back_kernel, name, (side, shifted, masks, conv_weight, x, stats, *met, rows),
            [
                SMEM, whole(3, pixels + 64, channels), mask_block,
                pl.BlockSpec((None, None, 3, channels, channels), lambda i: (index, 2 - i, 0, 0, 0)),
                field, stat, edge, edge, stat, stat,
            ],
            [(field, field_f32), row_out, row_out, stat_out, stat_out],
            40, 9 * matmul, grid=(3,), after=after,
        )

    far_bit = 2 * lanes
    others = []
    bit = 8
    while bit < lanes:
        others.append(bit)
        bit *= 2

    def swap(x, bit):
        return permute(x, lambda i: i ^ bit)

    def added(left, right):
        return (left.astype(F32) + right.astype(F32)).astype(BF16)

    def halve(part, bit, *deps):
        count = part.shape[0] // 2
        return part[:count], swap(part[count:], bit)

    def split(keep, coming):
        total = added(keep, coming)
        return total[0], total[1]

    far_both = near_bit | far_bit

    def z_send(first, second):
        part = jnp.stack([first, second], axis=1)
        return part[0], swap(part[1], far_bit), swap(part[2], near_bit), swap(part[3], far_both)

    def z_sum(own, *coming):
        part = own.astype(F32)
        for other in coming:
            part = part + other.astype(F32)
        part = part.astype(BF16)
        for bit in others:
            part = added(part, swap(part, bit))
        return part

    def z_share(part):
        return part, swap(part, far_bit), swap(part, near_bit), swap(part, far_both)

    def z_join(*parts):
        part = jnp.stack(parts)
        return part[:, 0], part[:, 1]

    def both(first, second, first_bit, second_bit):
        return swap(first, first_bit), swap(second, second_bit)

    def tied(token, *values):
        return lax.optimization_barrier(values + (token,))[:-1]

    def unpack(parts, taps, at_once, start, slots, base, into, name):
        piece = pl.BlockSpec(
            (2, PIECES // 2, at_once, channels // PIECES, channels // 2), lambda i: (0, 0, start // at_once + i, 0, 0)
        )
        operands, specs = [place, *parts], [SMEM, piece, piece]
        if into is not None:
            operands, specs = operands + [into], specs + [anywhere]
        out_spec = pl.BlockSpec((at_once, channels, channels), lambda i: (base // at_once + i, 0, 0))
        (out,) = call(
            unpack_kernel, name, operands, specs, [(out_spec, shape((slots, channels, channels), F32))],
            32, grid=(taps // at_once,), aliases={} if into is None else {3: 0},
        )
        return out

    two_keep, two_send, shifted_two, bias_two, residual_grad = weight_grad(
        residual, met2[0], met2[1], stats2, met2, normed_grad, met3, stats3, norm_rows[2], act_two, cotangent,
        "weight_two_grad",
    )
    two_coming = swap(two_send, 1)
    grad_two, near4, cross4, stats4, sums4 = conv_back(
        shifted_two, 1, middle, stats1, met1, norm_rows[1], "conv_two_back"
    )
    met4 = meet(near4, cross4, stats4)
    two_first, two_second = split(two_keep, behind(two_coming, near4))
    two_first, two_second = halve(two_first, 2), halve(two_second, 4)
    one_keep, one_send, shifted_one, bias_one = weight_grad(
        middle, met1[0], met1[1], stats1, met1, grad_two, met4, stats4, norm_rows[1], act_one, None,
        "weight_one_grad", (output_there,),
    )
    one_coming = swap(behind(one_send, two_first[1], two_second[1]), 1)
    two_first = added(two_first[0], behind(two_first[1], shifted_one))
    two_second = added(two_second[0], behind(two_second[1], shifted_one))
    two_first, two_second = halve(two_first, 4), halve(two_second, 2)
    grad_one, near5, cross5, stats5, sums5 = conv_back(
        shifted_one, 0, x, own0, met0, norm_rows[0], "conv_one_back"
    )
    one_first, one_second = split(one_keep, behind(one_coming, near5))
    token = one_first
    one_first, one_second = halve(one_first, 2), halve(one_second, 4)
    met5 = meet(*tied(token, near5, cross5, stats5))

    two_coming = tied(token, two_first[1], two_second[1])
    two_first, two_second = added(two_first[0], two_coming[0]), added(two_second[0], two_coming[1])
    token = two_first
    two = z_send(two_first, two_second)

    small_rows = shape((16, channels), F32)
    image_grad, small = call(
        last_kernel, "image_grad",
        (grad_one, *met5, stats5, x, own0, *met0, norm_rows[0], residual_grad,
         bias_one, bias_two, sums5, sums4, sums3, matrix_sums),
        [field, edge, edge, stat, stat, field, stat, edge, edge, stat, stat, field] + [stat] * 6,
        [(field, field_b16), (whole(16, channels), small_rows)], 32, after=(token,),
    )
    small = small + swap(small, 1)

    one_coming = tied(small, one_first[1], one_second[1])
    one_first, one_second = added(one_first[0], one_coming[0]), added(one_second[0], one_coming[1])
    token = one_first
    one_first, one_second = halve(one_first, 4), halve(one_second, 2)

    two = z_sum(*tied(token, *two))
    token = two
    two = z_share(two)

    one_coming = tied(token, one_first[1], one_second[1])
    one_first, one_second = added(one_first[0], one_coming[0]), added(one_second[0], one_coming[1])
    token = one_first
    one = z_send(one_first, one_second)

    (small,) = tied(token, small)
    bit = 2
    while bit < near_bit:
        small = small + swap(small, bit)
        bit *= 2

    two_first, two_second = z_join(*tied(small, *two))
    token = two_first
    two_coming = both(two_first, two_second, 4, 2)

    one = z_sum(*tied(token, *one))
    token = one
    one = z_share(one)

    two_coming = tied(token, *two_coming)
    two_first, two_second = jnp.concatenate([two_first, two_coming[0]]), jnp.concatenate([two_second, two_coming[1]])
    token = two_first
    two_coming = both(two_first, two_second, 2, 4)

    (small,) = tied(token, small)
    bit = near_bit
    while bit < devices:
        small = small + swap(small, bit)
        bit *= 2

    one_first, one_second = z_join(*tied(small, *one))
    token = one_first
    one_coming = both(one_first, one_second, 4, 2)
    (image_grad,) = tied(token, image_grad)
    image_there = permute(image_grad, turned)

    two_coming = tied(token, *two_coming)
    two = jnp.stack([jnp.concatenate([two_first, two_coming[0]]), jnp.concatenate([two_second, two_coming[1]])])
    token = two
    two = two, swap(two, 1)

    one_coming = tied(token, *one_coming)
    one_first, one_second = jnp.concatenate([one_first, one_coming[0]]), jnp.concatenate([one_second, one_coming[1]])
    token = one_first
    one_coming = both(one_first, one_second, 2, 4)

    two = tied(token, *two)
    weights = unpack(two, 9, 3, 0, 18, 9, None, "unpack_two")
    qk_grad = unpack(two, 2, 1, 9, 2, 0, None, "unpack_qk")
    value_grad_sum = unpack(two, 1, 1, 11, 1, 0, None, "unpack_value")
    proj_grad = unpack(two, 1, 1, 12, 1, 0, None, "unpack_proj")

    one_coming = tied(weights, *one_coming)
    one_coming = tied(image_there, *one_coming)
    one = jnp.stack([jnp.concatenate([one_first, one_coming[0]]), jnp.concatenate([one_second, one_coming[1]])])
    one = one, swap(one, 1)
    weights = unpack(one, 9, 3, 0, 18, 0, weights, "unpack_one")

    return (
        output_there.reshape(1, band, width, channels),
        image_there.reshape(1, band, width, channels),
        weights.reshape(2, 3, 3, channels, channels),
        small[0:2],
        small[2:5],
        small[5:8],
        qk_grad,
        value_grad_sum[0],
        proj_grad[0],
        small[8:10],
        small[10],
    )


def solution(mesh):
    split = P("batch", "seq", None, None)
    in_specs = (split, P("batch", "seq", None), split) + (P(),) * 9
    out_specs = (split, split) + (P(),) * 9
    return jax.shard_map(body, mesh=mesh, in_specs=in_specs, out_specs=out_specs, check_vma=False)
```

```python
import functools

import jax
import jax.numpy as jnp
from jax import lax
from jax.experimental import pallas as pl
from jax.experimental.pallas import tpu as pltpu
from jax.sharding import PartitionSpec as P

GROUPS = 32
EPSILON = 1e-06
MASKED_SCORE = -1e30
F32 = jnp.float32
BF16 = jnp.bfloat16
MIB = 1024 * 1024
PIECES = 32
LIMITS = {
    "conv_one": 46, "conv_two": 46, "weight_two_grad": 24, "weight_one_grad": 20, "conv_two_back": 36, "conv_one_back": 36,
    "attend": 40, "key_value_grad": 60, "early": 14, "matrix_grad": 16, "unpack_two": 40, "unpack_one": 16,
    "first": 8, "masks": 12, "normed": 8, "output": 8, "image_grad": 12,
}


def params(mib):
    return pltpu.CompilerParams(vmem_limit_bytes=mib * MIB)


def shape(dims, dtype):
    return jax.ShapeDtypeStruct(dims, dtype)


SMEM = pl.BlockSpec(memory_space=pltpu.SMEM)
IN_HBM = pl.BlockSpec(memory_space=pltpu.HBM)


def whole(*dims):
    return pl.BlockSpec(dims, lambda *_: (0,) * len(dims))


def group_sum(row):
    channels = row.shape[1]
    lane = lax.broadcasted_iota(jnp.int32, row.shape, 1)
    step = 1
    while step < channels // GROUPS:
        ahead = pltpu.roll(row, channels - step, 1)
        behind = pltpu.roll(row, step, 1)
        row = row + jnp.where((lane & step) == 0, ahead, behind)
        step *= 2
    return row


def rows_of(*parts):
    channels = parts[0].shape[1]
    line = lax.broadcasted_iota(jnp.int32, (8, channels), 0)
    out = jnp.zeros((8, channels), F32)
    for i, part in enumerate(parts):
        out = jnp.where(line == i, jnp.broadcast_to(part, (8, channels)), out)
    return out


def eight(row):
    return jnp.broadcast_to(row, (8, row.shape[1]))


def local_stats(values, channels, pixels):
    count = float(pixels * (channels // GROUPS))
    mean = group_sum(eight(jnp.sum(values, axis=0, keepdims=True)))[0:1] / count
    centered = values - mean
    square = group_sum(eight(jnp.sum(centered * centered, axis=0, keepdims=True)))[0:1]
    return mean, square


def joined_stats(own, near, cross, pair, pixels):
    bands = [own[0:2], near[32:34], cross[32:34], pair[0:2]]
    channels = bands[0].shape[1]
    count = float(pixels * (channels // GROUPS))
    mean = (bands[0][0:1] + bands[1][0:1] + bands[2][0:1] + bands[3][0:1]) * 0.25
    total = 0.0
    for band in bands:
        gap = band[0:1] - mean
        total = total + band[1:2] + count * gap * gap
    return mean, lax.rsqrt(total / (4.0 * count) + EPSILON)


def joined_sums(own, near, cross, pair, pixels):
    bands = [own[0:2], near[32:34], cross[32:34], pair[0:2]]
    channels = bands[0].shape[1]
    count = 4.0 * float(pixels * (channels // GROUPS))
    sums = (bands[0] + bands[1]) + (bands[2] + bands[3])
    return sums[0:1] / count, sums[1:2] / count


def sigmoid(values):
    return 0.5 * jnp.tanh(0.5 * values) + 0.5


def edges_out(side_ref, out_ref, near_ref, cross_ref, stats):
    pixels = out_ref.shape[0]
    side = side_ref[0]
    last = pixels - 32
    near_ref[0:32, :] = out_ref[pl.ds(pl.multiple_of(last * (1 - side), 32), 32), :].astype(F32)
    cross_ref[0:32, :] = out_ref[pl.ds(pl.multiple_of(last * side, 32), 32), :].astype(F32)
    near_ref[32:40, :] = stats
    cross_ref[32:40, :] = stats


def columns_of(frame, shifted, rows):
    for b in range(3):
        shifted[b] = frame[7 + b : 7 + b + rows, :].astype(BF16)


def masked(values, mask):
    channels = values.shape[1]
    return [values[:, i * 128 : (i + 1) * 128] * mask for i in range(channels // 128)]


def tap_rows(shifted, mask_ref, start, count, row):
    parts = []
    for b in range(3):
        block = shifted[b, pl.ds(pl.multiple_of(row * 32 + start, 32), count), :]
        parts += masked(block, mask_ref[b, start : start + count, :])
    return parts


def fetch_rows(weights, index, buffer, arrived, row, order):
    copies = [
        pltpu.make_async_copy(weights.at[index, r], buffer.at[r], arrived.at[r]) for r in order
    ]

    @pl.when(row == 0)
    def _():
        for copy in copies:
            copy.start()

    return copies


def wait_row(copies, row):
    for step, copy in enumerate(copies):

        @pl.when(row == step)
        def _(copy=copy):
            copy.wait()


def first_kernel(image_ref, tiles_ref, side_ref, near_ref, cross_ref, stats_ref):
    pixels, channels = image_ref.shape
    mean, square = local_stats(image_ref[...].astype(F32), channels, pixels)
    stats = rows_of(mean, square, tiles_ref[0:1], tiles_ref[1:2])
    stats_ref[...] = stats
    edges_out(side_ref, image_ref, near_ref, cross_ref, stats)


def mask_kernel(where_ref, own_ref, near_ref, cross_ref, pair_ref, mask_ref, column_ref, row_ref, frame):
    side, first, last = where_ref[0], where_ref[1], where_ref[2]

    def line(ref, base):
        return jnp.concatenate([ref[base + 2 : base + 3, :], ref[base + 3 : base + 4, :]], axis=1)

    own, near, cross, pair = line(own_ref, 0), line(near_ref, 32), line(cross_ref, 32), line(pair_ref, 0)
    pixels = own.shape[1]
    row_ref[...] = jnp.concatenate([own, pair, near, cross], axis=1)

    def upright(row):
        return jnp.transpose(jnp.broadcast_to(row, (128, row.shape[1])))

    column = upright(own)
    column_ref[...] = column
    above = jnp.where(side == 0, cross[:, pixels - 128 :], near[:, pixels - 128 :])
    below = jnp.where(side == 0, near[:, :128], cross[:, :128])
    outside = jnp.full((32, 128), -1.0, F32)
    frame[0:8, :] = jnp.zeros((8, 128), F32)
    frame[8:40, :] = jnp.where(first == 1, outside, upright(above)[96:128, :])
    frame[40 : 40 + pixels, :] = column
    frame[40 + pixels : 72 + pixels, :] = jnp.where(last == 1, outside, upright(below)[0:32, :])
    frame[72 + pixels : 80 + pixels, :] = jnp.zeros((8, 128), F32)
    place = lax.broadcasted_iota(jnp.int32, (pixels, 128), 0) & 31
    for a in range(3):
        for b in range(3):
            start = 8 + a * 32 + b - 1
            same = frame[start : start + pixels, :] == column
            if b == 0:
                same = same & (place > 0)
            if b == 2:
                same = same & (place < 31)
            mask_ref[a * 3 + b] = jnp.where(same, 1.0, 0.0).astype(BF16)


def conv_kernel(
    index, side_ref, x_ref, near_ref, cross_ref, pair_ref, stats_ref, rows_ref, mask_ref, weights, skip_ref,
    out_ref, act_ref, near_out, cross_out, stats_out, frame, shifted, buffer, arrived,
):
    row = pl.program_id(0)
    pixels, channels = x_ref.shape
    copies = fetch_rows(weights, index, buffer, arrived, row, (0, 1, 2))

    @pl.when(row == 0)
    def _():
        mean, inverse = joined_stats(stats_ref[...], near_ref[...], cross_ref[...], pair_ref[...], pixels)
        scale, shift, bias = rows_ref[0:1, :], rows_ref[1:2, :], rows_ref[2:3, :]

        def act(values):
            pre = (values - mean) * inverse * scale + shift
            return pre * sigmoid(pre)

        side = side_ref[0]
        near, cross = near_ref[0:32, :], cross_ref[0:32, :]
        frame[0:8, :] = jnp.zeros((8, channels), F32)
        frame[8:40, :] = act(jnp.where(side == 0, cross, near))
        frame[40 : 40 + pixels, :] = act(x_ref[...].astype(F32))
        frame[40 + pixels : 72 + pixels, :] = act(jnp.where(side == 0, near, cross))
        frame[72 + pixels : 80 + pixels, :] = jnp.zeros((8, channels), F32)
        columns_of(frame, shifted, pixels + 64)
        act_ref[...] = shifted[1, 32 : 32 + pixels, :]
        start = jnp.broadcast_to(bias, (pixels, channels))
        if skip_ref is not None:
            start = start + skip_ref[...].astype(F32)
        out_ref[...] = start

    wait_row(copies, row)
    weight = buffer[row].reshape(3 * channels, channels)
    for i in range(pixels // 256):
        taps = jnp.concatenate(tap_rows(shifted, mask_ref, i * 256, 256, row), axis=1)
        out_ref[i * 256 : (i + 1) * 256, :] += jnp.dot(taps, weight, preferred_element_type=F32)

    @pl.when(row == 2)
    def _():
        mean, square = local_stats(out_ref[...], channels, pixels)
        stats = rows_of(mean, square)
        stats_out[...] = stats
        edges_out(side_ref, out_ref, near_out, cross_out, stats)


def normed_kernel(x_ref, near_ref, cross_ref, pair_ref, stats_ref, rows_ref, out_ref):
    pixels = x_ref.shape[0]
    mean, inverse = joined_stats(stats_ref[...], near_ref[...], cross_ref[...], pair_ref[...], pixels)
    out_ref[...] = ((x_ref[...] - mean) * inverse * rows_ref[0:1, :] + rows_ref[1:2, :]).astype(BF16)


def nn(left, right):
    return jnp.dot(left, right, preferred_element_type=F32)


def nt(left, right):
    return lax.dot_general(left, right, (((1,), (1,)), ((), ())), preferred_element_type=F32)


def early_kernel(own_ref, pair_ref, cot_own, cot_pair, qk_ref, value_ref, proj_ref, bias_ref, *outs):
    for rows_ref, cot_ref, (keys, values, queries, grads) in ((own_ref, cot_own, outs[:4]), (pair_ref, cot_pair, outs[4:])):
        rows = rows_ref[...]
        queries[...] = (nn(rows, qk_ref[0]) + bias_ref[0:1, :]).astype(BF16)
        keys[...] = nn(rows, qk_ref[1]).astype(BF16)
        values[...] = (nn(rows, value_ref[...]) + bias_ref[1:2, :]).astype(BF16)
        grads[...] = nt(cot_ref[...], proj_ref[...]).astype(BF16)


def attend_kernel(
    near_ref, cross_ref, keys_own, values_own, keys_pair, values_pair, queries_ref, grads_ref, qk_ref, value_ref,
    bias_ref, column_ref, row_ref, attended_ref, query_grad_ref, totals_ref, far_keys, far_values,
):
    pixels, channels = near_ref.shape
    scale = channels ** (-0.5)
    for i, ref in enumerate((near_ref, cross_ref)):
        part = slice(i * pixels, (i + 1) * pixels)
        rows = ref[...]
        far_keys[part, :] = nn(rows, qk_ref[1]).astype(BF16)
        far_values[part, :] = (nn(rows, value_ref[...]) + bias_ref[1:2, :]).astype(BF16)
    block = totals_ref.shape[2]
    halves = (
        (keys_own, values_own, slice(0, pixels)),
        (keys_pair, values_pair, slice(pixels, 2 * pixels)),
        (far_keys, far_values, slice(2 * pixels, 4 * pixels)),
    )

    def step(i, carry):
        part = pl.ds(pl.multiple_of(i * block, block), block)
        queries, upstream = queries_ref[part, :], grads_ref[part, :]
        column = column_ref[part, 0:1]
        scores = []
        for keys, _, span in halves:
            product = nt(queries, keys[...]) * scale
            scores.append(jnp.where(column == row_ref[:, span], product, MASKED_SCORE))
        top = functools.reduce(jnp.maximum, [jnp.max(s, axis=1, keepdims=True) for s in scores])
        weights = [jnp.exp(s - top) for s in scores]
        total = sum(jnp.sum(w, axis=1, keepdims=True) for w in weights)
        inverse = 1.0 / total
        attended = sum(nn(w.astype(BF16), values[...]) for w, (_, values, _) in zip(weights, halves)) * inverse
        attended_ref[part, :] = attended.astype(BF16)
        delta = jnp.sum(attended * upstream.astype(F32), axis=1, keepdims=True)
        query_grad = 0.0
        for w, (keys, values, _) in zip(weights, halves):
            prob_grad = nt(upstream, values[...])
            score_grad = (w * inverse * (prob_grad - delta)).astype(BF16)
            query_grad = query_grad + nn(score_grad, keys[...])
        query_grad_ref[part, :] = (query_grad * scale).astype(BF16)
        log_total = jnp.transpose(jnp.broadcast_to(top + jnp.log(total), (block, 128)))
        turned = jnp.transpose(jnp.broadcast_to(delta, (block, 128)))
        totals_ref[i, 0:1, :] = log_total[0:1, :]
        totals_ref[i, 1:2, :] = turned[0:1, :]
        totals_ref[i, 2:8, :] = jnp.zeros((6, block), F32)
        return carry

    lax.fori_loop(0, pixels // block, step, 0)


def out_kernel(attended_ref, residual_ref, matrix_ref, bias_ref, out_ref):
    out_ref[...] = (residual_ref[...] + nn(attended_ref[...], matrix_ref[...]) + bias_ref[0:1, :]).astype(BF16)


def norm_back_sums(upstream, hat, gain):
    outer = jnp.sum(upstream * hat, axis=0, keepdims=True)
    inner = jnp.sum(upstream, axis=0, keepdims=True)
    first = group_sum(eight(inner * gain))[0:1]
    second = group_sum(eight(outer * gain))[0:1]
    return rows_of(outer, inner), rows_of(first, second)


def key_kernel(
    side_ref, keys, values, queries_own, grads_own, queries_pair, grads_pair, near_hbm, cot_near_hbm, cross_hbm,
    cot_cross_hbm, query_grad_hbm, qk_ref, value_ref, proj_ref, bias_ref,
    totals_own, totals_pair, totals_near, totals_cross, column_ref, row_ref,
    residual_hbm, stats_ref, near_ref, cross_ref, pair_ref, rows_ref,
    key_grad_ref, value_grad_ref, normed_grad_ref, near_out, cross_out, stats_out, sums_out,
    key_sum, value_sum, held, query_grad_ref, residual_ref, arrived,
):
    pixels, channels = keys.shape
    scale = channels ** (-0.5)
    sources = (
        queries_own, grads_own, queries_pair, grads_pair, near_hbm, cot_near_hbm, cross_hbm, cot_cross_hbm,
        query_grad_hbm, residual_hbm,
    )
    targets = [held.at[i] for i in range(8)] + [query_grad_ref, residual_ref]
    coming = [
        pltpu.make_async_copy(source, target, arrived.at[i]) for i, (source, target) in enumerate(zip(sources, targets))
    ]
    for copy in coming:
        copy.start()
    key_sum[...] = jnp.zeros_like(key_sum)
    value_sum[...] = jnp.zeros_like(value_sum)
    chunk = totals_own.shape[2]
    blocks = pixels // chunk

    def add(queries, upstream, totals, i, at):
        scores = nt(keys[...], queries) * scale
        weights = jnp.exp(scores - totals[i, 0:1, :])
        weights = jnp.where(column_ref[:, 0:1] == row_ref[at, 0:1, :], weights, 0.0)
        value_sum[...] += nn(weights.astype(BF16), upstream)
        prob_grad = nt(values[...], upstream)
        score_grad = (weights * (prob_grad - totals[i, 1:2, :])).astype(BF16)
        key_sum[...] += nn(score_grad, queries)

    for group, totals in enumerate((totals_own, totals_pair, totals_near, totals_cross)):
        coming[2 * group].wait()
        coming[2 * group + 1].wait()

        def step(i, carry, group=group, totals=totals):
            part = pl.ds(pl.multiple_of(i * chunk, chunk), chunk)
            queries, upstream = held[2 * group, part, :], held[2 * group + 1, part, :]
            if group >= 2:
                queries = (nn(queries, qk_ref[0]) + bias_ref[0:1, :]).astype(BF16)
                upstream = nt(upstream, proj_ref[...]).astype(BF16)
            add(queries, upstream, totals, i, group * blocks + i)
            return carry

        lax.fori_loop(0, blocks, step, 0)
    coming[8].wait()
    coming[9].wait()
    key_grad = (key_sum[...] * scale).astype(BF16)
    value_grad = value_sum[...].astype(BF16)
    key_grad_ref[...] = key_grad
    value_grad_ref[...] = value_grad
    normed_grad = nt(query_grad_ref[...], qk_ref[0]) + nt(key_grad, qk_ref[1]) + nt(value_grad, value_ref[...])
    normed_grad_ref[...] = normed_grad
    mean, inverse = joined_stats(stats_ref[...], near_ref[...], cross_ref[...], pair_ref[...], pixels)
    hat = (residual_ref[...] - mean) * inverse
    sums, groups = norm_back_sums(normed_grad, hat, rows_ref[0:1, :])
    sums_out[...] = sums
    stats_out[...] = groups
    edges_out(side_ref, normed_grad_ref, near_out, cross_out, groups)


def scatter_pieces(place_ref, product, tap, keep_ref, send_ref, matrix):
    rows, channels = product.shape
    half, height = channels // 2, rows // PIECES
    matrix[...] = product.astype(BF16)
    for q in range(PIECES):
        into = keep_ref if q < PIECES // 2 else send_ref
        for stream in range(2):
            start = pl.multiple_of((q ^ place_ref[stream]) * height, height)
            into[stream, q % (PIECES // 2), tap] = matrix[pl.ds(start, height), stream * half : (stream + 1) * half]


def tn(left, right):
    return lax.dot_general(left, right, (((0,), (0,)), ((), ())), preferred_element_type=F32)


def matrix_kernel(
    place_ref, normed_ref, query_grad_ref, key_grad_ref, value_grad_ref, attended_ref, cotangent_ref,
    keep_ref, send_ref, sums_ref, turned, matrix,
):
    turned[...] = jnp.transpose(normed_ref[...])
    for tap, ref in enumerate((query_grad_ref, key_grad_ref, value_grad_ref)):
        scatter_pieces(place_ref, nn(turned[...], ref[...]), tap, keep_ref, send_ref, matrix)
    turned[...] = jnp.transpose(attended_ref[...])
    scatter_pieces(place_ref, nn(turned[...], cotangent_ref[...]), 3, keep_ref, send_ref, matrix)
    total = [
        jnp.sum(ref[...].astype(F32), axis=0, keepdims=True)
        for ref in (query_grad_ref, value_grad_ref, cotangent_ref)
    ]
    sums_ref[...] = rows_of(*total)


def weight_grad_kernel(
    with_cotangent, place_ref, side_ref, x_ref, x_near, x_cross, stats_ref, near_ref, cross_ref, pair_ref,
    g_ref, g_near, g_cross, g_pair, g_stats, rows_ref, act_ref, mask_ref, *rest,
):
    if with_cotangent:
        cot_ref, cot_edges, matrix_keep, matrix_send = rest[0], rest[1:5], rest[5], rest[6]
        keep_ref, send_ref, shifted, sums_ref, own_ref, frame, turned, matrix = rest[7:]
    else:
        keep_ref, send_ref, shifted, sums_ref, frame, turned, matrix = rest
    row = pl.program_id(0)
    pixels, channels = x_ref.shape

    @pl.when(row == 0)
    def _():
        mean, inverse = joined_stats(stats_ref[...], near_ref[...], cross_ref[...], pair_ref[...], pixels)
        mean_h, mean_hx = joined_sums(g_stats[...], g_near[...], g_cross[...], g_pair[...], pixels)
        gain = rows_ref[0:1, :]
        side = side_ref[0]

        def back(grad, values):
            hat = (values - mean) * inverse
            return inverse * (grad * gain - mean_h - hat * mean_hx)

        def pick(near, cross):
            return jnp.where(side == 0, cross, near), jnp.where(side == 0, near, cross)

        g_above, g_below = pick(g_near[0:32, :], g_cross[0:32, :])
        x_above, x_below = pick(x_near[0:32, :], x_cross[0:32, :])
        above, below = back(g_above, x_above), back(g_below, x_below)
        own = back(g_ref[...], x_ref[...])
        if with_cotangent:
            near_top, near_bottom, cross_top, cross_bottom = [ref[...].astype(F32) for ref in cot_edges]
            above = above + jnp.where(side == 0, cross_bottom, near_bottom)
            below = below + jnp.where(side == 0, near_top, cross_top)
            own = own + cot_ref[...].astype(F32)
            own_ref[...] = own
            for tap in range(4):
                keep_ref[:, :, 9 + tap] = matrix_keep[:, :, tap]
                send_ref[:, :, 9 + tap] = matrix_send[:, :, tap]
        sums_ref[...] = rows_of(jnp.sum(own, axis=0, keepdims=True))
        frame[0:8, :] = jnp.zeros((8, channels), F32)
        frame[8:40, :] = above
        frame[40 : 40 + pixels, :] = own
        frame[40 + pixels : 72 + pixels, :] = below
        frame[72 + pixels : 80 + pixels, :] = jnp.zeros((8, channels), F32)
        columns_of(frame, shifted, pixels + 64)
        turned[...] = jnp.transpose(act_ref[...])

    for b in range(3):
        block = shifted[b, pl.ds(pl.multiple_of(row * 32, 32), pixels), :]
        block = jnp.concatenate(masked(block, mask_ref[b]), axis=1)
        product = nn(turned[...], block)
        scatter_pieces(place_ref, product, 8 - row * 3 - b, keep_ref, send_ref, matrix)


def conv_back_kernel(
    index, side_ref, shifted, mask_ref, weights, x_ref, stats_ref, near_ref, cross_ref, pair_ref, rows_ref,
    out_ref, near_out, cross_out, stats_out, sums_out, buffer, arrived,
):
    row = pl.program_id(0)
    pixels, channels = x_ref.shape
    copies = fetch_rows(weights, index, buffer, arrived, row, (2, 1, 0))

    @pl.when(row == 0)
    def _():
        out_ref[...] = jnp.zeros_like(out_ref)

    wait_row(copies, row)
    weight = jnp.concatenate([buffer[2 - row, 2 - b] for b in range(3)], axis=1)
    for i in range(pixels // 256):
        taps = jnp.concatenate(tap_rows(shifted, mask_ref, i * 256, 256, row), axis=1)
        out_ref[i * 256 : (i + 1) * 256, :] += nt(taps, weight)

    @pl.when(row == 2)
    def _():
        mean, inverse = joined_stats(stats_ref[...], near_ref[...], cross_ref[...], pair_ref[...], pixels)
        gain, shift = rows_ref[0:1, :], rows_ref[1:2, :]
        hat = (x_ref[...].astype(F32) - mean) * inverse
        pre = hat * gain + shift
        gate = sigmoid(pre)
        upstream = out_ref[...] * (gate * (1.0 + pre * (1.0 - gate)))
        out_ref[...] = upstream
        sums, groups = norm_back_sums(upstream, hat, gain)
        sums_out[...] = sums
        stats_out[...] = groups
        edges_out(side_ref, out_ref, near_out, cross_out, groups)


def last_kernel(
    g_ref, g_near, g_cross, g_pair, g_stats, x_ref, stats_ref, near_ref, cross_ref, pair_ref, rows_ref, add_ref,
    bias_one, bias_two, sums_one, sums_two, sums_three, matrix_sums, out_ref, small_ref,
):
    pixels = x_ref.shape[0]
    half = x_ref.shape[1] // 2
    parts = [bias_one[0:1], bias_two[0:1]]
    parts += [ref[i : i + 1] for i in range(2) for ref in (sums_one, sums_two, sums_three)]
    parts += [matrix_sums[i : i + 1] for i in range(3)]
    line = lax.broadcasted_iota(jnp.int32, (16, 2 * half), 0)
    rows = jnp.zeros((16, 2 * half), F32)
    for i, part in enumerate(parts):
        rows = jnp.where(line == i, jnp.broadcast_to(part, rows.shape), rows)
    high = rows.astype(BF16)
    low = (rows - high.astype(F32)).astype(BF16)
    for i, part in enumerate((high, low)):
        small_ref[2 * i] = part[:, :half]
        small_ref[2 * i + 1] = part[:, half:]
    mean, inverse = joined_stats(stats_ref[...], near_ref[...], cross_ref[...], pair_ref[...], pixels)
    mean_h, mean_hx = joined_sums(g_stats[...], g_near[...], g_cross[...], g_pair[...], pixels)
    hat = (x_ref[...].astype(F32) - mean) * inverse
    grad = inverse * (g_ref[...] * rows_ref[0:1, :] - mean_h - hat * mean_hx)
    out_ref[...] = (add_ref[...] + grad).astype(BF16)


def unpack_kernel(place_ref, own_ref, other_ref, *rest):
    out_ref = rest[-1]
    height, half = own_ref.shape[3], own_ref.shape[4]
    for tap in range(out_ref.shape[0]):
        for q in range(PIECES):
            pieces = own_ref if q < PIECES // 2 else other_ref
            for stream in range(2):
                start = pl.multiple_of((q ^ place_ref[stream]) * height, height)
                values = pieces[stream, q % (PIECES // 2), tap].astype(F32)
                out_ref[tap, pl.ds(start, height), stream * half : (stream + 1) * half] = values


def spread_pieces(place_ref, halves, tap, out):
    height, half = halves[0].shape[2], halves[0].shape[3]
    for q in range(PIECES):
        pieces = halves[q // (PIECES // 2)]
        for stream in range(2):
            start = pl.multiple_of((q ^ place_ref[stream]) * height, height)
            values = pieces[q % (PIECES // 2), stream * 17 + tap].astype(F32)
            out[pl.ds(start, height), stream * half : (stream + 1) * half] = values


def unpack_two_kernel(place_ref, own_ref, other_ref, weights_ref, qk_ref, value_ref, proj_ref):
    step = pl.program_id(0)
    halves = (own_ref, other_ref)

    @pl.when(step < 3)
    def _():
        for tap in range(3):
            spread_pieces(place_ref, halves, step * 3 + tap, weights_ref.at[tap])

    @pl.when(step == 3)
    def _():
        for tap, out in enumerate((qk_ref.at[0], qk_ref.at[1], value_ref, proj_ref)):
            spread_pieces(place_ref, halves, 9 + tap, out)


def body(
    image,
    tile_map,
    out_grad,
    conv_weight,
    conv_bias,
    norm_gain,
    norm_shift,
    qk_weight,
    value_weight,
    proj_weight,
    qv_bias,
    proj_bias,
):
    band, width, channels = image.shape[1], image.shape[2], image.shape[3]
    pixels = band * width
    lanes = lax.axis_size("batch")
    devices = 4 * lanes

    def turned(flat):
        s, b = flat // lanes, flat % lanes
        core, high = b % 2, s // 2
        return (core * 2 + s % 2) * lanes + (b - core + high)

    def xored(flat, bits):
        return flat ^ bits

    def permute(x, to):
        return lax.ppermute(x, ("seq", "batch"), [(i, to(i)) for i in range(devices)])

    near_bit, pair_bit = lanes, 1

    def to_near(i):
        return i ^ near_bit

    def to_pair(i):
        return i ^ pair_bit

    def to_cross(i):
        return i ^ (near_bit | pair_bit)

    def meet(near, cross, stats):
        return permute(near, to_near), permute(cross, to_cross), permute(stats, to_pair)

    seq, lane = lax.axis_index("seq"), lax.axis_index("batch")
    core, low, high = lane % 2, seq % 2, seq // 2
    side = low.astype(jnp.int32).reshape(1)
    spot = jnp.stack([low, ((low == 0) & (core == 0)), ((low == 1) & (core == 1))]).astype(jnp.int32)
    x_bit, y_bit = (lane // 2) % 2, (lane // 4) % 2
    tail = low * 2 + high
    place = jnp.stack(
        [core * 16 + x_bit * 8 + y_bit * 4 + tail, core * 16 + y_bit * 8 + x_bit * 4 + tail, tail]
    ).astype(jnp.int32)

    def block8(*rows):
        rows = [r.astype(F32).reshape(1, channels) for r in rows]
        return jnp.concatenate(rows + [jnp.zeros((8 - len(rows), channels), F32)], axis=0)

    norm_rows = [block8(norm_gain[i], norm_shift[i], conv_bias[min(i, 1)]) for i in range(3)]
    bias_rows = block8(qv_bias[0], qv_bias[1], proj_bias, jnp.zeros((channels,), F32))

    row_f32 = shape((40, channels), F32)
    stat_f32 = shape((8, channels), F32)
    field_f32 = shape((pixels, channels), F32)
    field_b16 = shape((pixels, channels), BF16)
    field = whole(pixels, channels)
    edge = whole(40, channels)
    stat = whole(8, channels)

    def call(kernel, name, operands, in_specs, outs, mib, flops=0, scratch=(), grid=(1,), after=(), aliases=None):
        count = len(operands)

        def run(*refs):
            kernel(*refs[:count], *refs[count + len(after) :])

        moved = sum(o.size * o.dtype.itemsize for o in operands) + sum(o.size * o.dtype.itemsize for _, o in outs)
        return pl.pallas_call(
            run if after else kernel,
            in_specs=list(in_specs) + [pl.BlockSpec(memory_space=pl.ANY)] * len(after),
            out_specs=[spec for spec, _ in outs],
            out_shape=[out for _, out in outs],
            scratch_shapes=list(scratch),
            grid=grid,
            input_output_aliases=aliases or {},
            compiler_params=params(LIMITS.get(name, mib)),
            cost_estimate=pl.CostEstimate(flops=int(flops), bytes_accessed=int(moved), transcendentals=0),
            name=name,
        )(*operands, *after)

    def behind(x, *deps):
        return lax.optimization_barrier((x,) + deps)[0]

    row_out, stat_out = (edge, row_f32), (stat, stat_f32)
    matmul = 2.0 * pixels * channels * channels

    image_flat = image.reshape(pixels, channels)
    cot_flat = out_grad.reshape(pixels, channels)
    tiles = tile_map.astype(F32).reshape(2, pixels // 2)
    x = permute(image_flat, turned)
    near0, cross0, stats0 = call(
        first_kernel, "first", (image_flat, tiles, side), [field, whole(2, pixels // 2), SMEM],
        [row_out, row_out, stat_out], 16,
    )
    own0 = permute(stats0, turned)
    pair0 = permute(stats0, lambda i: to_pair(turned(i)))
    near0 = permute(near0, lambda i: to_near(turned(i)))
    cross0 = permute(cross0, lambda i: to_cross(turned(i)))
    masks, column_tiles, row_tiles = call(
        mask_kernel, "masks", (spot, own0, near0, cross0, pair0), [SMEM, stat, edge, edge, stat],
        [
            (whole(9, pixels, 128), shape((9, pixels, 128), BF16)),
            (whole(pixels, 128), shape((pixels, 128), F32)),
            (whole(1, 4 * pixels), shape((1, 4 * pixels), F32)),
        ],
        24, scratch=[pltpu.VMEM((pixels + 80, 128), F32)],
    )

    half = pixels // 2
    cot_first = permute(behind(cot_flat[:half], x), turned)

    mask_block = pl.BlockSpec((3, pixels, 128), lambda i: (i, 0, 0))

    row_buffer = [pltpu.VMEM((3, 3, channels, channels), BF16), pltpu.SemaphoreType.DMA((3,))]

    def conv(x, met, stats, rows, index, skip, name, after=()):
        near, cross, pair = met
        specs = [
            SMEM, field, edge, edge, stat, stat, stat, mask_block, IN_HBM,
        ]
        operands = [side, x, near, cross, pair, stats, rows, masks, conv_weight]
        kernel = functools.partial(conv_kernel, index)
        if skip is None:

            def kernel(*refs):
                return conv_kernel(index, *refs[:9], None, *refs[9:])
        else:
            specs.append(field)
            operands.append(skip)
        return call(
            kernel, name, operands, specs,
            [(field, field_f32), (field, field_b16), row_out, row_out, stat_out],
            40, 9 * matmul,
            [pltpu.VMEM((pixels + 80, channels), F32), pltpu.VMEM((3, pixels + 64, channels), BF16), *row_buffer],
            (3,), after,
        )

    met0 = (near0, cross0, pair0)
    middle, act_one, near1, cross1, stats1 = conv(x, met0, own0, norm_rows[0], 0, None, "conv_one")
    met1 = meet(near1, cross1, stats1)
    cot_second = permute(behind(cot_flat[half:], cot_first, met1[2]), turned)
    residual, act_two, near2, cross2, stats2 = conv(
        middle, met1, stats1, norm_rows[1], 1, x, "conv_two", (cot_first,)
    )
    met2 = meet(near2, cross2, stats2)

    (normed,) = call(
        normed_kernel, "normed", (residual, *met2, stats2, norm_rows[2]), [field, edge, edge, stat, stat, stat],
        [(field, field_b16)], 16, after=(cot_second,),
    )
    cotangent = jnp.concatenate([cot_first, cot_second], axis=0)

    normed_near = permute(normed, to_near)
    normed_pair = permute(normed, to_pair)

    block = 512
    anywhere = pl.BlockSpec(memory_space=pl.ANY)
    blocks = pixels // block
    totals_out = (whole(blocks, 8, block), shape((blocks, 8, block), F32))
    square = whole(channels, channels)
    cot_pair = permute(cotangent, to_pair)
    keys, values, queries, grads, keys_pair, values_pair, queries_pair, grads_pair = call(
        early_kernel, "early",
        (normed, normed_pair, cotangent, cot_pair, qk_weight, value_weight, proj_weight, bias_rows),
        [field] * 4 + [whole(2, channels, channels), square, square, stat],
        [(field, field_b16)] * 8, 32, 8 * matmul,
    )
    normed_cross = permute(behind(normed_near, keys), to_pair)
    cot_near = permute(behind(cotangent, normed_near), to_near)
    attended, query_grad, totals = call(
        attend_kernel, "attend",
        (normed_near, normed_cross, keys, values, keys_pair, values_pair, queries, grads, qk_weight, value_weight, bias_rows,
         column_tiles, row_tiles),
        [field] * 8 + [whole(2, channels, channels), square, stat, whole(pixels, 128), whole(1, 4 * pixels)],
        [(field, field_b16), (field, field_b16), totals_out],
        58, 4 * matmul + 4 * 4 * matmul * pixels / channels,
        [pltpu.VMEM((2 * pixels, channels), BF16)] * 2,
    )

    totals_pair, totals_near, totals_cross = (permute(totals, to) for to in (to_pair, to_near, to_cross))
    cot_cross = permute(behind(cot_near, attended), to_pair)
    (output,) = call(
        out_kernel, "output", (attended, residual, proj_weight, block8(proj_bias)), [field, field, square, stat],
        [(field, field_b16)], 16, matmul, after=(cot_near,),
    )
    output_there = permute(output, turned)
    key_grad, value_grad, normed_grad, near3, cross3, stats3, sums3 = call(
        key_kernel, "key_value_grad",
        (side, keys, values, queries, grads, queries_pair, grads_pair, normed_near, cot_near, normed_cross, cot_cross,
         query_grad, qk_weight, value_weight, proj_weight, bias_rows,
         totals, totals_pair, totals_near, totals_cross, column_tiles, row_tiles.reshape(4 * blocks, 1, block),
         residual, stats2, *met2, norm_rows[2]),
        [SMEM] + [field] * 2 + [anywhere] * 9 + [whole(2, channels, channels), square, square, stat]
        + [totals_out[0]] * 4
        + [whole(pixels, 128), whole(4 * blocks, 1, block), anywhere, stat, edge, edge, stat, stat],
        [(field, field_b16), (field, field_b16), (field, field_f32), row_out, row_out, stat_out, stat_out],
        60, 7 * matmul + 4 * 4 * matmul * pixels / channels,
        [pltpu.VMEM((pixels, channels), F32)] * 2
        + [
            pltpu.VMEM((8, pixels, channels), BF16), pltpu.VMEM((pixels, channels), BF16),
            pltpu.VMEM((pixels, channels), F32), pltpu.SemaphoreType.DMA((10,)),
        ],
    )
    met3 = meet(near3, cross3, stats3)


    def pieces(taps):
        dims = (2, PIECES // 2, taps, channels // PIECES, channels // 2)
        return [(whole(*dims), shape(dims, BF16))] * 2

    matrix_keep, matrix_send, matrix_sums = call(
        matrix_kernel, "matrix_grad", (place, normed, query_grad, key_grad, value_grad, attended, cotangent),
        [SMEM] + [field] * 6, pieces(4) + [stat_out], 32, 4 * matmul,
        [pltpu.VMEM((channels, pixels), BF16), pltpu.VMEM((channels, channels), BF16)], after=(output_there,),
    )

    def weight_grad(x, x_near, x_cross, stats, met, grad, grad_met, grad_stats, rows, act, cot, name, after=()):
        near, cross, pair = met
        g_near, g_cross, g_pair = grad_met
        spread = (3, pixels + 64, channels)
        extra, extra_in, extra_out = [], [], []
        if cot is not None:
            top = pl.BlockSpec((32, channels), lambda i: (0, 0))
            bottom = pl.BlockSpec((32, channels), lambda i: (pixels // 32 - 1, 0))
            extra = [cot, cot_near, cot_near, cot_cross, cot_cross, matrix_keep, matrix_send]
            extra_in = [field, top, bottom, top, bottom] + [spec for spec, _ in pieces(4)]
            extra_out = [(field, field_f32)]
        return call(
            functools.partial(weight_grad_kernel, cot is not None), name,
            [place, side, x, x_near, x_cross, stats, near, cross, pair, grad, g_near, g_cross, g_pair, grad_stats,
             rows, act, masks] + extra,
            [SMEM, SMEM, field, edge, edge, stat, edge, edge, stat, field, edge, edge, stat, stat, stat, field, mask_block]
            + extra_in,
            pieces(9 if cot is None else 13) + [(whole(*spread), shape(spread, BF16)), stat_out] + extra_out,
            58, 9 * matmul,
            [pltpu.VMEM((pixels + 80, channels), F32), pltpu.VMEM((channels, pixels), BF16), pltpu.VMEM((channels, channels), BF16)],
            (3,), after,
        )

    def conv_back(shifted, index, x, stats, met, rows, name, after=()):
        return call(
            functools.partial(conv_back_kernel, index), name, (side, shifted, masks, conv_weight, x, stats, *met, rows),
            [
                SMEM, whole(3, pixels + 64, channels), mask_block, IN_HBM,
                field, stat, edge, edge, stat, stat,
            ],
            [(field, field_f32), row_out, row_out, stat_out, stat_out],
            40, 9 * matmul, row_buffer, (3,), after,
        )

    far_bit = 2 * lanes
    others = []
    bit = 8
    while bit < lanes:
        others.append(bit)
        bit *= 2

    def swap(x, bit):
        return permute(x, lambda i: i ^ bit)

    def added(left, right):
        return (left.astype(F32) + right.astype(F32)).astype(BF16)

    def halve(part, bit, *deps):
        count = part.shape[0] // 2
        return part[:count], swap(part[count:], bit)

    def split(keep, coming):
        total = added(keep, coming)
        return total[0], total[1]

    far_both = near_bit | far_bit

    def z_send(first, second):
        part = jnp.stack([first, second], axis=1)
        return part[0], swap(part[1], far_bit), swap(part[2], near_bit), swap(part[3], far_both)

    def z_sum(own, *coming):
        part = own.astype(F32)
        for other in coming:
            part = part + other.astype(F32)
        part = part.astype(BF16)
        for bit in others:
            part = added(part, swap(part, bit))
        return part

    def z_share(part):
        return part, swap(part, far_bit), swap(part, near_bit), swap(part, far_both)

    def z_join(*parts):
        part = jnp.stack(parts)
        return part[:, 0], part[:, 1]

    def both(first, second, first_bit, second_bit):
        return swap(first, first_bit), swap(second, second_bit)

    def tied(token, *values):
        return lax.optimization_barrier(values + (token,))[:-1]

    def unpack(parts, taps, at_once, start, slots, base, into, name):
        piece = pl.BlockSpec(
            (2, PIECES // 2, at_once, channels // PIECES, channels // 2), lambda i: (0, 0, start // at_once + i, 0, 0)
        )
        operands, specs = [place, *parts], [SMEM, piece, piece]
        if into is not None:
            operands, specs = operands + [into], specs + [anywhere]
        out_spec = pl.BlockSpec((at_once, channels, channels), lambda i: (base // at_once + i, 0, 0))
        (out,) = call(
            unpack_kernel, name, operands, specs, [(out_spec, shape((slots, channels, channels), F32))],
            32, grid=(taps // at_once,), aliases={} if into is None else {3: 0},
        )
        return out

    two_keep, two_send, shifted_two, bias_two, residual_grad = weight_grad(
        residual, met2[0], met2[1], stats2, met2, normed_grad, met3, stats3, norm_rows[2], act_two, cotangent,
        "weight_two_grad",
    )
    two_coming = swap(two_send, 1)
    grad_two, near4, cross4, stats4, sums4 = conv_back(
        shifted_two, 1, middle, stats1, met1, norm_rows[1], "conv_two_back"
    )
    met4 = meet(near4, cross4, stats4)
    two_first, two_second = split(two_keep, behind(two_coming, near4))
    two_first, two_second = halve(two_first, 2), halve(two_second, 4)
    one_keep, one_send, shifted_one, bias_one = weight_grad(
        middle, met1[0], met1[1], stats1, met1, grad_two, met4, stats4, norm_rows[1], act_one, None,
        "weight_one_grad",
    )
    def after_token(token, *values):
        return lax.optimization_barrier(values + (token,))[:-1]

    def add_halves(token, first, second):
        one, two = after_token(token, first[1], second[1])
        return added(first[0], one), added(second[0], two)

    def join_halves(token, first, second, coming):
        one, two = after_token(token, *coming)
        return jnp.concatenate([first, one]), jnp.concatenate([second, two])

    one_coming = swap(behind(one_send, two_first[1], two_second[1]), 1)
    two_first, two_second = add_halves(shifted_one, two_first, two_second)
    token = two_first
    two_first, two_second = halve(two_first, 4), halve(two_second, 2)
    grad_one, near5, cross5, stats5, sums5 = conv_back(
        shifted_one, 0, x, own0, met0, norm_rows[0], "conv_one_back", (two_first[0], two_second[0])
    )
    met5 = meet(near5, cross5, stats5)

    one_first, one_second = split(one_keep, *after_token(near5, one_coming))
    token = one_first
    one_first, one_second = halve(one_first, 2), halve(one_second, 4)

    two_first, two_second = add_halves(token, two_first, two_second)
    token = two_first
    two = z_send(two_first, two_second)

    piece_dims = (channels // PIECES, channels // 2)
    small_parts = shape((4,) + piece_dims, BF16)
    image_grad, small = call(
        last_kernel, "image_grad",
        (grad_one, *met5, stats5, x, own0, *met0, norm_rows[0], residual_grad,
         bias_one, bias_two, sums5, sums4, sums3, matrix_sums),
        [field, edge, edge, stat, stat, field, stat, edge, edge, stat, stat, field] + [stat] * 6,
        [(field, field_b16), (whole(4, *piece_dims), small_parts)], 32, after=(token,),
    )
    for bit in others:
        small = added(small, swap(small, bit))

    one_first, one_second = add_halves(small, one_first, one_second)
    token = one_first
    one_first, one_second = halve(one_first, 4), halve(one_second, 2)

    two = z_sum(*after_token(token, *two))
    token = two
    two = z_share(jnp.concatenate([two.reshape((-1,) + piece_dims), small]))

    one_first, one_second = add_halves(token, one_first, one_second)
    token = one_first
    one = z_send(one_first, one_second)

    two = jnp.stack(after_token(token, *two))
    token = two
    two_first = jnp.concatenate([two[:, :13], two[:, 26:]], axis=1)
    two_second = two[:, 13:26]
    two_coming = both(two_first, two_second, 4, 2)

    one = z_sum(*after_token(token, *one))
    token = one
    one = z_share(one)

    two_first, two_second = join_halves(token, two_first, two_second, two_coming)
    token = two_first
    two_coming = both(two_first, two_second, 2, 4)

    one_first, one_second = z_join(*after_token(token, *one))
    token = one_first
    one_coming = both(one_first, one_second, 4, 2)
    image_there = permute(behind(image_grad, token), turned)

    two = jnp.concatenate(join_halves(token, two_first, two_second, two_coming), axis=1)
    token = two
    two = two, swap(two, 1)

    one_first, one_second = join_halves(token, one_first, one_second, one_coming)
    token = one_first
    one_coming = both(one_first, one_second, 2, 4)

    two = after_token(token, *two)
    weights, qk_grad, value_weight_grad, proj_weight_grad = call(
        unpack_two_kernel, "unpack_two", (place, *two), [SMEM] + [whole(*two[0].shape)] * 2,
        [
            (
                pl.BlockSpec((3, channels, channels), lambda i: (3 + jnp.minimum(i, 2), 0, 0)),
                shape((18, channels, channels), F32),
            ),
            (whole(2, channels, channels), shape((2, channels, channels), F32)),
            (square, shape((channels, channels), F32)),
            (square, shape((channels, channels), F32)),
        ],
        40, grid=(4,),
    )
    small = jnp.stack(two)[:, :, 13:17].astype(F32)
    small = jnp.sum(small.reshape((-1, 2, 2) + piece_dims), axis=(0, 1))
    small = jnp.concatenate([small[0], small[1]], axis=1)
    token = qk_grad

    one = jnp.stack(join_halves(token, one_first, one_second, one_coming))
    one, image_there = lax.optimization_barrier((one, image_there))
    token = one
    one = one, swap(one, 1)

    weights = unpack(one, 9, 3, 0, 18, 0, weights, "unpack_one")

    return (
        output_there.reshape(1, band, width, channels),
        image_there.reshape(1, band, width, channels),
        weights.reshape(2, 3, 3, channels, channels),
        small[0:2],
        small[2:5],
        small[5:8],
        qk_grad,
        value_weight_grad,
        proj_weight_grad,
        small[8:10],
        small[10],
    )


def solution(mesh):
    split = P("batch", "seq", None, None)
    in_specs = (split, P("batch", "seq", None), split) + (P(),) * 9
    out_specs = (split, split) + (P(),) * 9
    return jax.shard_map(body, mesh=mesh, in_specs=in_specs, out_specs=out_specs, check_vma=False)
```

```python
import functools

import jax
import jax.numpy as jnp
from jax import lax
from jax.experimental import pallas as pl
from jax.experimental.pallas import tpu as pltpu
from jax.sharding import PartitionSpec as P

GROUPS = 32
EPSILON = 1e-06
MASKED_SCORE = -1e30
F32 = jnp.float32
BF16 = jnp.bfloat16
MIB = 1024 * 1024
PIECES = 32
LIMITS = {
    "conv_one": 46, "conv_two": 46, "weight_two_grad": 24, "weight_one_grad": 20, "conv_two_back": 36, "conv_one_back": 36,
    "attend": 40, "attend_first": 32, "key_value_grad": 60, "early": 14, "matrix_grad": 16, "unpack_two": 40, "unpack_one": 16,
    "first": 8, "masks": 12, "normed": 8, "output": 8, "image_grad": 12,
}


def params(mib):
    return pltpu.CompilerParams(vmem_limit_bytes=mib * MIB)


def shape(dims, dtype):
    return jax.ShapeDtypeStruct(dims, dtype)


SMEM = pl.BlockSpec(memory_space=pltpu.SMEM)
IN_HBM = pl.BlockSpec(memory_space=pltpu.HBM)


def whole(*dims):
    return pl.BlockSpec(dims, lambda *_: (0,) * len(dims))


def group_sum(row):
    channels = row.shape[1]
    lane = lax.broadcasted_iota(jnp.int32, row.shape, 1)
    step = 1
    while step < channels // GROUPS:
        ahead = pltpu.roll(row, channels - step, 1)
        behind = pltpu.roll(row, step, 1)
        row = row + jnp.where((lane & step) == 0, ahead, behind)
        step *= 2
    return row


def rows_of(*parts):
    channels = parts[0].shape[1]
    line = lax.broadcasted_iota(jnp.int32, (8, channels), 0)
    out = jnp.zeros((8, channels), F32)
    for i, part in enumerate(parts):
        out = jnp.where(line == i, jnp.broadcast_to(part, (8, channels)), out)
    return out


def eight(row):
    return jnp.broadcast_to(row, (8, row.shape[1]))


def local_stats(values, channels, pixels):
    count = float(pixels * (channels // GROUPS))
    mean = group_sum(eight(jnp.sum(values, axis=0, keepdims=True)))[0:1] / count
    centered = values - mean
    square = group_sum(eight(jnp.sum(centered * centered, axis=0, keepdims=True)))[0:1]
    return mean, square


def joined_stats(own, near, cross, pair, pixels):
    bands = [own[0:2], near[32:34], cross[32:34], pair[0:2]]
    channels = bands[0].shape[1]
    count = float(pixels * (channels // GROUPS))
    mean = (bands[0][0:1] + bands[1][0:1] + bands[2][0:1] + bands[3][0:1]) * 0.25
    total = 0.0
    for band in bands:
        gap = band[0:1] - mean
        total = total + band[1:2] + count * gap * gap
    return mean, lax.rsqrt(total / (4.0 * count) + EPSILON)


def joined_sums(own, near, cross, pair, pixels):
    bands = [own[0:2], near[32:34], cross[32:34], pair[0:2]]
    channels = bands[0].shape[1]
    count = 4.0 * float(pixels * (channels // GROUPS))
    sums = (bands[0] + bands[1]) + (bands[2] + bands[3])
    return sums[0:1] / count, sums[1:2] / count


def sigmoid(values):
    return 0.5 * jnp.tanh(0.5 * values) + 0.5


def edges_out(side_ref, out_ref, near_ref, cross_ref, stats):
    pixels = out_ref.shape[0]
    side = side_ref[0]
    last = pixels - 32
    near_ref[0:32, :] = out_ref[pl.ds(pl.multiple_of(last * (1 - side), 32), 32), :].astype(F32)
    cross_ref[0:32, :] = out_ref[pl.ds(pl.multiple_of(last * side, 32), 32), :].astype(F32)
    near_ref[32:40, :] = stats
    cross_ref[32:40, :] = stats


def columns_of(frame, shifted, rows):
    for b in range(3):
        shifted[b] = frame[7 + b : 7 + b + rows, :].astype(BF16)


def masked(values, mask):
    channels = values.shape[1]
    return [values[:, i * 128 : (i + 1) * 128] * mask for i in range(channels // 128)]


def tap_rows(shifted, mask_ref, start, count, row):
    parts = []
    for b in range(3):
        block = shifted[b, pl.ds(pl.multiple_of(row * 32 + start, 32), count), :]
        parts += masked(block, mask_ref[b, start : start + count, :])
    return parts


def fetch_rows(weights, index, buffer, arrived, row, order):
    copies = [
        pltpu.make_async_copy(weights.at[index, r], buffer.at[r], arrived.at[r]) for r in order
    ]

    @pl.when(row == 0)
    def _():
        for copy in copies:
            copy.start()

    return copies


def wait_row(copies, row):
    for step, copy in enumerate(copies):

        @pl.when(row == step)
        def _(copy=copy):
            copy.wait()


def first_kernel(image_ref, tiles_ref, side_ref, near_ref, cross_ref, stats_ref):
    pixels, channels = image_ref.shape
    mean, square = local_stats(image_ref[...].astype(F32), channels, pixels)
    stats = rows_of(mean, square, tiles_ref[0:1], tiles_ref[1:2])
    stats_ref[...] = stats
    edges_out(side_ref, image_ref, near_ref, cross_ref, stats)


def mask_kernel(where_ref, own_ref, near_ref, cross_ref, pair_ref, mask_ref, column_ref, row_ref, frame):
    side, first, last = where_ref[0], where_ref[1], where_ref[2]

    def line(ref, base):
        return jnp.concatenate([ref[base + 2 : base + 3, :], ref[base + 3 : base + 4, :]], axis=1)

    own, near, cross, pair = line(own_ref, 0), line(near_ref, 32), line(cross_ref, 32), line(pair_ref, 0)
    pixels = own.shape[1]
    row_ref[...] = jnp.concatenate([own, pair, near, cross], axis=1)

    def upright(row):
        return jnp.transpose(jnp.broadcast_to(row, (128, row.shape[1])))

    column = upright(own)
    column_ref[...] = column
    above = jnp.where(side == 0, cross[:, pixels - 128 :], near[:, pixels - 128 :])
    below = jnp.where(side == 0, near[:, :128], cross[:, :128])
    outside = jnp.full((32, 128), -1.0, F32)
    frame[0:8, :] = jnp.zeros((8, 128), F32)
    frame[8:40, :] = jnp.where(first == 1, outside, upright(above)[96:128, :])
    frame[40 : 40 + pixels, :] = column
    frame[40 + pixels : 72 + pixels, :] = jnp.where(last == 1, outside, upright(below)[0:32, :])
    frame[72 + pixels : 80 + pixels, :] = jnp.zeros((8, 128), F32)
    place = lax.broadcasted_iota(jnp.int32, (pixels, 128), 0) & 31
    for a in range(3):
        for b in range(3):
            start = 8 + a * 32 + b - 1
            same = frame[start : start + pixels, :] == column
            if b == 0:
                same = same & (place > 0)
            if b == 2:
                same = same & (place < 31)
            mask_ref[a * 3 + b] = jnp.where(same, 1.0, 0.0).astype(BF16)


def conv_kernel(
    index, side_ref, x_ref, near_ref, cross_ref, pair_ref, stats_ref, rows_ref, mask_ref, weights, skip_ref,
    out_ref, act_ref, near_out, cross_out, stats_out, frame, shifted, buffer, arrived,
):
    row = pl.program_id(0)
    pixels, channels = x_ref.shape
    copies = fetch_rows(weights, index, buffer, arrived, row, (0, 1, 2))

    @pl.when(row == 0)
    def _():
        mean, inverse = joined_stats(stats_ref[...], near_ref[...], cross_ref[...], pair_ref[...], pixels)
        scale, shift, bias = rows_ref[0:1, :], rows_ref[1:2, :], rows_ref[2:3, :]

        def act(values):
            pre = (values - mean) * inverse * scale + shift
            return pre * sigmoid(pre)

        side = side_ref[0]
        near, cross = near_ref[0:32, :], cross_ref[0:32, :]
        frame[0:8, :] = jnp.zeros((8, channels), F32)
        frame[8:40, :] = act(jnp.where(side == 0, cross, near))
        frame[40 : 40 + pixels, :] = act(x_ref[...].astype(F32))
        frame[40 + pixels : 72 + pixels, :] = act(jnp.where(side == 0, near, cross))
        frame[72 + pixels : 80 + pixels, :] = jnp.zeros((8, channels), F32)
        columns_of(frame, shifted, pixels + 64)
        act_ref[...] = shifted[1, 32 : 32 + pixels, :]
        start = jnp.broadcast_to(bias, (pixels, channels))
        if skip_ref is not None:
            start = start + skip_ref[...].astype(F32)
        out_ref[...] = start

    wait_row(copies, row)
    weight = buffer[row].reshape(3 * channels, channels)
    for i in range(pixels // 256):
        taps = jnp.concatenate(tap_rows(shifted, mask_ref, i * 256, 256, row), axis=1)
        out_ref[i * 256 : (i + 1) * 256, :] += jnp.dot(taps, weight, preferred_element_type=F32)

    @pl.when(row == 2)
    def _():
        mean, square = local_stats(out_ref[...], channels, pixels)
        stats = rows_of(mean, square)
        stats_out[...] = stats
        edges_out(side_ref, out_ref, near_out, cross_out, stats)


def normed_kernel(x_ref, near_ref, cross_ref, pair_ref, stats_ref, rows_ref, out_ref):
    pixels = x_ref.shape[0]
    mean, inverse = joined_stats(stats_ref[...], near_ref[...], cross_ref[...], pair_ref[...], pixels)
    out_ref[...] = ((x_ref[...] - mean) * inverse * rows_ref[0:1, :] + rows_ref[1:2, :]).astype(BF16)


def nn(left, right):
    return jnp.dot(left, right, preferred_element_type=F32)


def nt(left, right):
    return lax.dot_general(left, right, (((1,), (1,)), ((), ())), preferred_element_type=F32)


def early_kernel(own_ref, pair_ref, cot_own, cot_pair, qk_ref, value_ref, proj_ref, bias_ref, *outs):
    for rows_ref, cot_ref, (keys, values, queries, grads) in ((own_ref, cot_own, outs[:4]), (pair_ref, cot_pair, outs[4:])):
        rows = rows_ref[...]
        queries[...] = (nn(rows, qk_ref[0]) + bias_ref[0:1, :]).astype(BF16)
        keys[...] = nn(rows, qk_ref[1]).astype(BF16)
        values[...] = (nn(rows, value_ref[...]) + bias_ref[1:2, :]).astype(BF16)
        grads[...] = nt(cot_ref[...], proj_ref[...]).astype(BF16)


def attend_first_kernel(
    keys_own, values_own, keys_pair, values_pair, queries_ref, column_ref, row_ref,
    weights_ref, top_ref, total_ref, sum_ref,
):
    pixels, channels = queries_ref.shape
    scale = channels ** (-0.5)
    block = 512

    def step(i, carry):
        part = pl.ds(pl.multiple_of(i * block, block), block)
        queries = queries_ref[part, :]
        column = column_ref[part, 0:1]
        scores = []
        for j, keys in enumerate((keys_own, keys_pair)):
            product = nt(queries, keys[...]) * scale
            scores.append(jnp.where(column == row_ref[:, j * pixels : (j + 1) * pixels], product, MASKED_SCORE))
        top = jnp.maximum(*[jnp.max(s, axis=1, keepdims=True) for s in scores])
        total, summed = 0.0, 0.0
        for j, (score, values) in enumerate(zip(scores, (values_own, values_pair))):
            weights = jnp.exp(score - top)
            total = total + jnp.sum(weights, axis=1, keepdims=True)
            rounded = weights.astype(BF16)
            weights_ref[part, j * pixels : (j + 1) * pixels] = rounded
            summed = summed + nn(rounded, values[...])
        top_ref[part, :] = jnp.broadcast_to(top, (block, 128))
        total_ref[part, :] = jnp.broadcast_to(total, (block, 128))
        sum_ref[part, :] = summed
        return carry

    lax.fori_loop(0, pixels // block, step, 0)


def attend_kernel(
    near_ref, cross_ref, keys_own, values_own, keys_pair, values_pair, queries_ref, grads_ref,
    weights_ref, top_ref, total_ref, sum_ref, qk_ref, value_ref, bias_ref, column_ref, row_ref,
    attended_ref, query_grad_ref, totals_ref, far_keys, far_values,
):
    pixels, channels = near_ref.shape
    scale = channels ** (-0.5)
    for i, ref in enumerate((near_ref, cross_ref)):
        part = slice(i * pixels, (i + 1) * pixels)
        rows = ref[...]
        far_keys[part, :] = nn(rows, qk_ref[1]).astype(BF16)
        far_values[part, :] = (nn(rows, value_ref[...]) + bias_ref[1:2, :]).astype(BF16)
    block = totals_ref.shape[2]

    def step(i, carry):
        part = pl.ds(pl.multiple_of(i * block, block), block)
        queries, upstream = queries_ref[part, :], grads_ref[part, :]
        product = nt(queries, far_keys[...]) * scale
        scores = jnp.where(column_ref[part, 0:1] == row_ref[:, 2 * pixels :], product, MASKED_SCORE)
        first_top = top_ref[part, 0:1]
        top = jnp.maximum(first_top, jnp.max(scores, axis=1, keepdims=True))
        shrink = jnp.exp(first_top - top)
        weights = jnp.exp(scores - top)
        total = total_ref[part, 0:1] * shrink + jnp.sum(weights, axis=1, keepdims=True)
        inverse = 1.0 / total
        attended = (sum_ref[part, :] * shrink + nn(weights.astype(BF16), far_values[...])) * inverse
        attended_ref[part, :] = attended.astype(BF16)
        delta = jnp.sum(attended * upstream.astype(F32), axis=1, keepdims=True)
        score_grad = (weights * inverse * (nt(upstream, far_values[...]) - delta)).astype(BF16)
        query_grad = nn(score_grad, far_keys[...])
        factor = shrink * inverse
        for j, (keys, values) in enumerate(((keys_own, values_own), (keys_pair, values_pair))):
            held = weights_ref[part, j * pixels : (j + 1) * pixels].astype(F32)
            score_grad = (held * factor * (nt(upstream, values[...]) - delta)).astype(BF16)
            query_grad = query_grad + nn(score_grad, keys[...])
        query_grad_ref[part, :] = (query_grad * scale).astype(BF16)
        log_total = jnp.transpose(jnp.broadcast_to(top + jnp.log(total), (block, 128)))
        turned = jnp.transpose(jnp.broadcast_to(delta, (block, 128)))
        totals_ref[i, 0:1, :] = log_total[0:1, :]
        totals_ref[i, 1:2, :] = turned[0:1, :]
        totals_ref[i, 2:8, :] = jnp.zeros((6, block), F32)
        return carry

    lax.fori_loop(0, pixels // block, step, 0)


def out_kernel(attended_ref, residual_ref, matrix_ref, bias_ref, out_ref):
    out_ref[...] = (residual_ref[...] + nn(attended_ref[...], matrix_ref[...]) + bias_ref[0:1, :]).astype(BF16)


def norm_back_sums(upstream, hat, gain):
    outer = jnp.sum(upstream * hat, axis=0, keepdims=True)
    inner = jnp.sum(upstream, axis=0, keepdims=True)
    first = group_sum(eight(inner * gain))[0:1]
    second = group_sum(eight(outer * gain))[0:1]
    return rows_of(outer, inner), rows_of(first, second)


def key_kernel(
    side_ref, keys, values, queries_own, grads_own, queries_pair, grads_pair, near_hbm, cot_near_hbm, cross_hbm,
    cot_cross_hbm, query_grad_hbm, qk_ref, value_ref, proj_ref, bias_ref,
    totals_own, totals_pair, totals_near, totals_cross, column_ref, row_ref,
    residual_hbm, stats_ref, near_ref, cross_ref, pair_ref, rows_ref,
    key_grad_ref, value_grad_ref, normed_grad_ref, near_out, cross_out, stats_out, sums_out,
    key_sum, value_sum, held, query_grad_ref, residual_ref, arrived,
):
    pixels, channels = keys.shape
    scale = channels ** (-0.5)
    sources = (
        queries_own, grads_own, queries_pair, grads_pair, near_hbm, cot_near_hbm, cross_hbm, cot_cross_hbm,
        query_grad_hbm, residual_hbm,
    )
    targets = [held.at[i] for i in range(8)] + [query_grad_ref, residual_ref]
    coming = [
        pltpu.make_async_copy(source, target, arrived.at[i]) for i, (source, target) in enumerate(zip(sources, targets))
    ]
    for copy in coming:
        copy.start()
    key_sum[...] = jnp.zeros_like(key_sum)
    value_sum[...] = jnp.zeros_like(value_sum)
    chunk = totals_own.shape[2]
    blocks = pixels // chunk

    def add(queries, upstream, totals, i, at):
        scores = nt(keys[...], queries) * scale
        weights = jnp.exp(scores - totals[i, 0:1, :])
        weights = jnp.where(column_ref[:, 0:1] == row_ref[at, 0:1, :], weights, 0.0)
        value_sum[...] += nn(weights.astype(BF16), upstream)
        prob_grad = nt(values[...], upstream)
        score_grad = (weights * (prob_grad - totals[i, 1:2, :])).astype(BF16)
        key_sum[...] += nn(score_grad, queries)

    for group, totals in enumerate((totals_own, totals_pair, totals_near, totals_cross)):
        coming[2 * group].wait()
        coming[2 * group + 1].wait()

        def step(i, carry, group=group, totals=totals):
            part = pl.ds(pl.multiple_of(i * chunk, chunk), chunk)
            queries, upstream = held[2 * group, part, :], held[2 * group + 1, part, :]
            if group >= 2:
                queries = (nn(queries, qk_ref[0]) + bias_ref[0:1, :]).astype(BF16)
                upstream = nt(upstream, proj_ref[...]).astype(BF16)
            add(queries, upstream, totals, i, group * blocks + i)
            return carry

        lax.fori_loop(0, blocks, step, 0)
    coming[8].wait()
    coming[9].wait()
    key_grad = (key_sum[...] * scale).astype(BF16)
    value_grad = value_sum[...].astype(BF16)
    key_grad_ref[...] = key_grad
    value_grad_ref[...] = value_grad
    normed_grad = nt(query_grad_ref[...], qk_ref[0]) + nt(key_grad, qk_ref[1]) + nt(value_grad, value_ref[...])
    normed_grad_ref[...] = normed_grad
    mean, inverse = joined_stats(stats_ref[...], near_ref[...], cross_ref[...], pair_ref[...], pixels)
    hat = (residual_ref[...] - mean) * inverse
    sums, groups = norm_back_sums(normed_grad, hat, rows_ref[0:1, :])
    sums_out[...] = sums
    stats_out[...] = groups
    edges_out(side_ref, normed_grad_ref, near_out, cross_out, groups)


def scatter_pieces(place_ref, product, tap, keep_ref, send_ref, matrix):
    rows, channels = product.shape
    half, height = channels // 2, rows // PIECES
    matrix[...] = product.astype(BF16)
    for q in range(PIECES):
        into = keep_ref if q < PIECES // 2 else send_ref
        for stream in range(2):
            start = pl.multiple_of((q ^ place_ref[stream]) * height, height)
            into[stream, q % (PIECES // 2), tap] = matrix[pl.ds(start, height), stream * half : (stream + 1) * half]


def tn(left, right):
    return lax.dot_general(left, right, (((0,), (0,)), ((), ())), preferred_element_type=F32)


def matrix_kernel(
    place_ref, normed_ref, query_grad_ref, key_grad_ref, value_grad_ref, attended_ref, cotangent_ref,
    keep_ref, send_ref, sums_ref, turned, matrix,
):
    turned[...] = jnp.transpose(normed_ref[...])
    for tap, ref in enumerate((query_grad_ref, key_grad_ref, value_grad_ref)):
        scatter_pieces(place_ref, nn(turned[...], ref[...]), tap, keep_ref, send_ref, matrix)
    turned[...] = jnp.transpose(attended_ref[...])
    scatter_pieces(place_ref, nn(turned[...], cotangent_ref[...]), 3, keep_ref, send_ref, matrix)
    total = [
        jnp.sum(ref[...].astype(F32), axis=0, keepdims=True)
        for ref in (query_grad_ref, value_grad_ref, cotangent_ref)
    ]
    sums_ref[...] = rows_of(*total)


def weight_grad_kernel(
    with_cotangent, place_ref, side_ref, x_ref, x_near, x_cross, stats_ref, near_ref, cross_ref, pair_ref,
    g_ref, g_near, g_cross, g_pair, g_stats, rows_ref, act_ref, mask_ref, *rest,
):
    if with_cotangent:
        cot_ref, cot_edges, matrix_keep, matrix_send = rest[0], rest[1:5], rest[5], rest[6]
        keep_ref, send_ref, shifted, sums_ref, own_ref, frame, turned, matrix = rest[7:]
    else:
        keep_ref, send_ref, shifted, sums_ref, frame, turned, matrix = rest
    row = pl.program_id(0)
    pixels, channels = x_ref.shape

    @pl.when(row == 0)
    def _():
        mean, inverse = joined_stats(stats_ref[...], near_ref[...], cross_ref[...], pair_ref[...], pixels)
        mean_h, mean_hx = joined_sums(g_stats[...], g_near[...], g_cross[...], g_pair[...], pixels)
        gain = rows_ref[0:1, :]
        side = side_ref[0]

        def back(grad, values):
            hat = (values - mean) * inverse
            return inverse * (grad * gain - mean_h - hat * mean_hx)

        def pick(near, cross):
            return jnp.where(side == 0, cross, near), jnp.where(side == 0, near, cross)

        g_above, g_below = pick(g_near[0:32, :], g_cross[0:32, :])
        x_above, x_below = pick(x_near[0:32, :], x_cross[0:32, :])
        above, below = back(g_above, x_above), back(g_below, x_below)
        own = back(g_ref[...], x_ref[...])
        if with_cotangent:
            near_top, near_bottom, cross_top, cross_bottom = [ref[...].astype(F32) for ref in cot_edges]
            above = above + jnp.where(side == 0, cross_bottom, near_bottom)
            below = below + jnp.where(side == 0, near_top, cross_top)
            own = own + cot_ref[...].astype(F32)
            own_ref[...] = own
            for tap in range(4):
                keep_ref[:, :, 9 + tap] = matrix_keep[:, :, tap]
                send_ref[:, :, 9 + tap] = matrix_send[:, :, tap]
        sums_ref[...] = rows_of(jnp.sum(own, axis=0, keepdims=True))
        frame[0:8, :] = jnp.zeros((8, channels), F32)
        frame[8:40, :] = above
        frame[40 : 40 + pixels, :] = own
        frame[40 + pixels : 72 + pixels, :] = below
        frame[72 + pixels : 80 + pixels, :] = jnp.zeros((8, channels), F32)
        columns_of(frame, shifted, pixels + 64)
        turned[...] = jnp.transpose(act_ref[...])

    for b in range(3):
        block = shifted[b, pl.ds(pl.multiple_of(row * 32, 32), pixels), :]
        block = jnp.concatenate(masked(block, mask_ref[b]), axis=1)
        product = nn(turned[...], block)
        scatter_pieces(place_ref, product, 8 - row * 3 - b, keep_ref, send_ref, matrix)


def conv_back_kernel(
    index, side_ref, shifted, mask_ref, weights, x_ref, stats_ref, near_ref, cross_ref, pair_ref, rows_ref,
    out_ref, near_out, cross_out, stats_out, sums_out, buffer, arrived,
):
    row = pl.program_id(0)
    pixels, channels = x_ref.shape
    copies = fetch_rows(weights, index, buffer, arrived, row, (2, 1, 0))

    @pl.when(row == 0)
    def _():
        out_ref[...] = jnp.zeros_like(out_ref)

    wait_row(copies, row)
    weight = jnp.concatenate([buffer[2 - row, 2 - b] for b in range(3)], axis=1)
    for i in range(pixels // 256):
        taps = jnp.concatenate(tap_rows(shifted, mask_ref, i * 256, 256, row), axis=1)
        out_ref[i * 256 : (i + 1) * 256, :] += nt(taps, weight)

    @pl.when(row == 2)
    def _():
        mean, inverse = joined_stats(stats_ref[...], near_ref[...], cross_ref[...], pair_ref[...], pixels)
        gain, shift = rows_ref[0:1, :], rows_ref[1:2, :]
        hat = (x_ref[...].astype(F32) - mean) * inverse
        pre = hat * gain + shift
        gate = sigmoid(pre)
        upstream = out_ref[...] * (gate * (1.0 + pre * (1.0 - gate)))
        out_ref[...] = upstream
        sums, groups = norm_back_sums(upstream, hat, gain)
        sums_out[...] = sums
        stats_out[...] = groups
        edges_out(side_ref, out_ref, near_out, cross_out, groups)


def last_kernel(
    g_ref, g_near, g_cross, g_pair, g_stats, x_ref, stats_ref, near_ref, cross_ref, pair_ref, rows_ref, add_ref,
    bias_one, bias_two, sums_one, sums_two, sums_three, matrix_sums, out_ref, small_ref,
):
    pixels = x_ref.shape[0]
    half = x_ref.shape[1] // 2
    parts = [bias_one[0:1], bias_two[0:1]]
    parts += [ref[i : i + 1] for i in range(2) for ref in (sums_one, sums_two, sums_three)]
    parts += [matrix_sums[i : i + 1] for i in range(3)]
    line = lax.broadcasted_iota(jnp.int32, (16, 2 * half), 0)
    rows = jnp.zeros((16, 2 * half), F32)
    for i, part in enumerate(parts):
        rows = jnp.where(line == i, jnp.broadcast_to(part, rows.shape), rows)
    high = rows.astype(BF16)
    low = (rows - high.astype(F32)).astype(BF16)
    for i, part in enumerate((high, low)):
        small_ref[2 * i] = part[:, :half]
        small_ref[2 * i + 1] = part[:, half:]
    mean, inverse = joined_stats(stats_ref[...], near_ref[...], cross_ref[...], pair_ref[...], pixels)
    mean_h, mean_hx = joined_sums(g_stats[...], g_near[...], g_cross[...], g_pair[...], pixels)
    hat = (x_ref[...].astype(F32) - mean) * inverse
    grad = inverse * (g_ref[...] * rows_ref[0:1, :] - mean_h - hat * mean_hx)
    out_ref[...] = (add_ref[...] + grad).astype(BF16)


def unpack_kernel(place_ref, own_ref, other_ref, *rest):
    out_ref = rest[-1]
    height, half = own_ref.shape[3], own_ref.shape[4]
    for tap in range(out_ref.shape[0]):
        for q in range(PIECES):
            pieces = own_ref if q < PIECES // 2 else other_ref
            for stream in range(2):
                start = pl.multiple_of((q ^ place_ref[stream]) * height, height)
                values = pieces[stream, q % (PIECES // 2), tap].astype(F32)
                out_ref[tap, pl.ds(start, height), stream * half : (stream + 1) * half] = values


def spread_pieces(place_ref, halves, tap, out):
    height, half = halves[0].shape[2], halves[0].shape[3]
    for q in range(PIECES):
        pieces = halves[q // (PIECES // 2)]
        for stream in range(2):
            start = pl.multiple_of((q ^ place_ref[stream]) * height, height)
            values = pieces[q % (PIECES // 2), stream * 17 + tap].astype(F32)
            out[pl.ds(start, height), stream * half : (stream + 1) * half] = values


def unpack_two_kernel(place_ref, own_ref, other_ref, weights_ref, qk_ref, value_ref, proj_ref):
    step = pl.program_id(0)
    halves = (own_ref, other_ref)

    @pl.when(step < 3)
    def _():
        for tap in range(3):
            spread_pieces(place_ref, halves, step * 3 + tap, weights_ref.at[tap])

    @pl.when(step == 3)
    def _():
        for tap, out in enumerate((qk_ref.at[0], qk_ref.at[1], value_ref, proj_ref)):
            spread_pieces(place_ref, halves, 9 + tap, out)


def body(
    image,
    tile_map,
    out_grad,
    conv_weight,
    conv_bias,
    norm_gain,
    norm_shift,
    qk_weight,
    value_weight,
    proj_weight,
    qv_bias,
    proj_bias,
):
    band, width, channels = image.shape[1], image.shape[2], image.shape[3]
    pixels = band * width
    lanes = lax.axis_size("batch")
    devices = 4 * lanes

    def turned(flat):
        s, b = flat // lanes, flat % lanes
        core, high = b % 2, s // 2
        return (core * 2 + s % 2) * lanes + (b - core + high)

    def xored(flat, bits):
        return flat ^ bits

    def permute(x, to):
        return lax.ppermute(x, ("seq", "batch"), [(i, to(i)) for i in range(devices)])

    near_bit, pair_bit = lanes, 1

    def to_near(i):
        return i ^ near_bit

    def to_pair(i):
        return i ^ pair_bit

    def to_cross(i):
        return i ^ (near_bit | pair_bit)

    def meet(near, cross, stats):
        return permute(near, to_near), permute(cross, to_cross), permute(stats, to_pair)

    seq, lane = lax.axis_index("seq"), lax.axis_index("batch")
    core, low, high = lane % 2, seq % 2, seq // 2
    side = low.astype(jnp.int32).reshape(1)
    spot = jnp.stack([low, ((low == 0) & (core == 0)), ((low == 1) & (core == 1))]).astype(jnp.int32)
    x_bit, y_bit = (lane // 2) % 2, (lane // 4) % 2
    tail = low * 2 + high
    place = jnp.stack(
        [core * 16 + x_bit * 8 + y_bit * 4 + tail, core * 16 + y_bit * 8 + x_bit * 4 + tail, tail]
    ).astype(jnp.int32)

    def block8(*rows):
        rows = [r.astype(F32).reshape(1, channels) for r in rows]
        return jnp.concatenate(rows + [jnp.zeros((8 - len(rows), channels), F32)], axis=0)

    norm_rows = [block8(norm_gain[i], norm_shift[i], conv_bias[min(i, 1)]) for i in range(3)]
    bias_rows = block8(qv_bias[0], qv_bias[1], proj_bias, jnp.zeros((channels,), F32))

    row_f32 = shape((40, channels), F32)
    stat_f32 = shape((8, channels), F32)
    field_f32 = shape((pixels, channels), F32)
    field_b16 = shape((pixels, channels), BF16)
    field = whole(pixels, channels)
    edge = whole(40, channels)
    stat = whole(8, channels)

    def call(kernel, name, operands, in_specs, outs, mib, flops=0, scratch=(), grid=(1,), after=(), aliases=None):
        count = len(operands)

        def run(*refs):
            kernel(*refs[:count], *refs[count + len(after) :])

        moved = sum(o.size * o.dtype.itemsize for o in operands) + sum(o.size * o.dtype.itemsize for _, o in outs)
        return pl.pallas_call(
            run if after else kernel,
            in_specs=list(in_specs) + [pl.BlockSpec(memory_space=pl.ANY)] * len(after),
            out_specs=[spec for spec, _ in outs],
            out_shape=[out for _, out in outs],
            scratch_shapes=list(scratch),
            grid=grid,
            input_output_aliases=aliases or {},
            compiler_params=params(LIMITS.get(name, mib)),
            cost_estimate=pl.CostEstimate(flops=int(flops), bytes_accessed=int(moved), transcendentals=0),
            name=name,
        )(*operands, *after)

    def behind(x, *deps):
        return lax.optimization_barrier((x,) + deps)[0]

    row_out, stat_out = (edge, row_f32), (stat, stat_f32)
    matmul = 2.0 * pixels * channels * channels

    image_flat = image.reshape(pixels, channels)
    cot_flat = out_grad.reshape(pixels, channels)
    tiles = tile_map.astype(F32).reshape(2, pixels // 2)
    x = permute(image_flat, turned)
    near0, cross0, stats0 = call(
        first_kernel, "first", (image_flat, tiles, side), [field, whole(2, pixels // 2), SMEM],
        [row_out, row_out, stat_out], 16, after=(permute(block8(norm_gain[0]), to_pair),),
    )
    own0 = permute(stats0, turned)
    pair0 = permute(stats0, lambda i: to_pair(turned(i)))
    near0 = permute(near0, lambda i: to_near(turned(i)))
    cross0 = permute(cross0, lambda i: to_cross(turned(i)))
    masks, column_tiles, row_tiles = call(
        mask_kernel, "masks", (spot, own0, near0, cross0, pair0), [SMEM, stat, edge, edge, stat],
        [
            (whole(9, pixels, 128), shape((9, pixels, 128), BF16)),
            (whole(pixels, 128), shape((pixels, 128), F32)),
            (whole(1, 4 * pixels), shape((1, 4 * pixels), F32)),
        ],
        24, scratch=[pltpu.VMEM((pixels + 80, 128), F32)],
    )

    half = pixels // 2
    cot_first = permute(behind(cot_flat[:half], x), turned)

    mask_block = pl.BlockSpec((3, pixels, 128), lambda i: (i, 0, 0))

    row_buffer = [pltpu.VMEM((3, 3, channels, channels), BF16), pltpu.SemaphoreType.DMA((3,))]

    def conv(x, met, stats, rows, index, skip, name, after=()):
        near, cross, pair = met
        specs = [
            SMEM, field, edge, edge, stat, stat, stat, mask_block, IN_HBM,
        ]
        operands = [side, x, near, cross, pair, stats, rows, masks, conv_weight]
        kernel = functools.partial(conv_kernel, index)
        if skip is None:

            def kernel(*refs):
                return conv_kernel(index, *refs[:9], None, *refs[9:])
        else:
            specs.append(field)
            operands.append(skip)
        return call(
            kernel, name, operands, specs,
            [(field, field_f32), (field, field_b16), row_out, row_out, stat_out],
            40, 9 * matmul,
            [pltpu.VMEM((pixels + 80, channels), F32), pltpu.VMEM((3, pixels + 64, channels), BF16), *row_buffer],
            (3,), after,
        )

    met0 = (near0, cross0, pair0)
    middle, act_one, near1, cross1, stats1 = conv(x, met0, own0, norm_rows[0], 0, None, "conv_one")
    met1 = meet(near1, cross1, stats1)
    cot_second = permute(behind(cot_flat[half:], cot_first, met1[2]), turned)
    residual, act_two, near2, cross2, stats2 = conv(
        middle, met1, stats1, norm_rows[1], 1, x, "conv_two", (cot_first,)
    )
    met2 = meet(near2, cross2, stats2)

    (normed,) = call(
        normed_kernel, "normed", (residual, *met2, stats2, norm_rows[2]), [field, edge, edge, stat, stat, stat],
        [(field, field_b16)], 16, after=(cot_second,),
    )
    cotangent = jnp.concatenate([cot_first, cot_second], axis=0)

    normed_near = permute(normed, to_near)
    normed_pair = permute(normed, to_pair)

    block = 512
    anywhere = pl.BlockSpec(memory_space=pl.ANY)
    blocks = pixels // block
    totals_out = (whole(blocks, 8, block), shape((blocks, 8, block), F32))
    square = whole(channels, channels)
    cot_pair = permute(cotangent, to_pair)
    keys, values, queries, grads, keys_pair, values_pair, queries_pair, grads_pair = call(
        early_kernel, "early",
        (normed, normed_pair, cotangent, cot_pair, qk_weight, value_weight, proj_weight, bias_rows),
        [field] * 4 + [whole(2, channels, channels), square, square, stat],
        [(field, field_b16)] * 8, 32, 8 * matmul,
    )
    lane_field = (whole(pixels, 128), shape((pixels, 128), F32))
    weights, tops, sums, products = call(
        attend_first_kernel, "attend_first", (keys, values, keys_pair, values_pair, queries, column_tiles, row_tiles),
        [field] * 5 + [whole(pixels, 128), whole(1, 4 * pixels)],
        [(whole(pixels, 2 * pixels), shape((pixels, 2 * pixels), BF16)), lane_field, lane_field, (field, field_f32)],
        32, 2 * 2 * matmul * pixels / channels,
    )
    normed_cross = permute(behind(normed_near, products), to_pair)
    cot_near = permute(behind(cotangent, normed_near), to_near)
    attended, query_grad, totals = call(
        attend_kernel, "attend",
        (normed_near, normed_cross, keys, values, keys_pair, values_pair, queries, grads, weights, tops, sums, products, qk_weight, value_weight, bias_rows,
         column_tiles, row_tiles),
        [field] * 8 + [whole(pixels, 2 * pixels), whole(pixels, 128), whole(pixels, 128), field] + [whole(2, channels, channels), square, stat, whole(pixels, 128), whole(1, 4 * pixels)],
        [(field, field_b16), (field, field_b16), totals_out],
        58, 4 * matmul + 4 * 4 * matmul * pixels / channels,
        [pltpu.VMEM((2 * pixels, channels), BF16)] * 2,
    )

    totals_pair, totals_near, totals_cross = (permute(totals, to) for to in (to_pair, to_near, to_cross))
    cot_cross = permute(behind(cot_near, attended), to_pair)
    (output,) = call(
        out_kernel, "output", (attended, residual, proj_weight, block8(proj_bias)), [field, field, square, stat],
        [(field, field_b16)], 16, matmul, after=(cot_near,),
    )
    output_there = permute(output.reshape(1, band, width, channels), turned)
    key_grad, value_grad, normed_grad, near3, cross3, stats3, sums3 = call(
        key_kernel, "key_value_grad",
        (side, keys, values, queries, grads, queries_pair, grads_pair, normed_near, cot_near, normed_cross, cot_cross,
         query_grad, qk_weight, value_weight, proj_weight, bias_rows,
         totals, totals_pair, totals_near, totals_cross, column_tiles, row_tiles.reshape(4 * blocks, 1, block),
         residual, stats2, *met2, norm_rows[2]),
        [SMEM] + [field] * 2 + [anywhere] * 9 + [whole(2, channels, channels), square, square, stat]
        + [totals_out[0]] * 4
        + [whole(pixels, 128), whole(4 * blocks, 1, block), anywhere, stat, edge, edge, stat, stat],
        [(field, field_b16), (field, field_b16), (field, field_f32), row_out, row_out, stat_out, stat_out],
        60, 7 * matmul + 4 * 4 * matmul * pixels / channels,
        [pltpu.VMEM((pixels, channels), F32)] * 2
        + [
            pltpu.VMEM((8, pixels, channels), BF16), pltpu.VMEM((pixels, channels), BF16),
            pltpu.VMEM((pixels, channels), F32), pltpu.SemaphoreType.DMA((10,)),
        ],
    )
    met3 = meet(near3, cross3, stats3)


    def pieces(taps):
        dims = (2, PIECES // 2, taps, channels // PIECES, channels // 2)
        return [(whole(*dims), shape(dims, BF16))] * 2

    matrix_keep, matrix_send, matrix_sums = call(
        matrix_kernel, "matrix_grad", (place, normed, query_grad, key_grad, value_grad, attended, cotangent),
        [SMEM] + [field] * 6, pieces(4) + [stat_out], 32, 4 * matmul,
        [pltpu.VMEM((channels, pixels), BF16), pltpu.VMEM((channels, channels), BF16)], after=(output_there,),
    )

    def weight_grad(x, x_near, x_cross, stats, met, grad, grad_met, grad_stats, rows, act, cot, name, after=()):
        near, cross, pair = met
        g_near, g_cross, g_pair = grad_met
        spread = (3, pixels + 64, channels)
        extra, extra_in, extra_out = [], [], []
        if cot is not None:
            top = pl.BlockSpec((32, channels), lambda i: (0, 0))
            bottom = pl.BlockSpec((32, channels), lambda i: (pixels // 32 - 1, 0))
            extra = [cot, cot_near, cot_near, cot_cross, cot_cross, matrix_keep, matrix_send]
            extra_in = [field, top, bottom, top, bottom] + [spec for spec, _ in pieces(4)]
            extra_out = [(field, field_f32)]
        return call(
            functools.partial(weight_grad_kernel, cot is not None), name,
            [place, side, x, x_near, x_cross, stats, near, cross, pair, grad, g_near, g_cross, g_pair, grad_stats,
             rows, act, masks] + extra,
            [SMEM, SMEM, field, edge, edge, stat, edge, edge, stat, field, edge, edge, stat, stat, stat, field, mask_block]
            + extra_in,
            pieces(9 if cot is None else 13) + [(whole(*spread), shape(spread, BF16)), stat_out] + extra_out,
            58, 9 * matmul,
            [pltpu.VMEM((pixels + 80, channels), F32), pltpu.VMEM((channels, pixels), BF16), pltpu.VMEM((channels, channels), BF16)],
            (3,), after,
        )

    def conv_back(shifted, index, x, stats, met, rows, name, after=()):
        return call(
            functools.partial(conv_back_kernel, index), name, (side, shifted, masks, conv_weight, x, stats, *met, rows),
            [
                SMEM, whole(3, pixels + 64, channels), mask_block, IN_HBM,
                field, stat, edge, edge, stat, stat,
            ],
            [(field, field_f32), row_out, row_out, stat_out, stat_out],
            40, 9 * matmul, row_buffer, (3,), after,
        )

    far_bit = 2 * lanes
    others = []
    bit = 8
    while bit < lanes:
        others.append(bit)
        bit *= 2

    def swap(x, bit):
        return permute(x, lambda i: i ^ bit)

    def added(left, right):
        return (left.astype(F32) + right.astype(F32)).astype(BF16)

    def halve(part, bit, *deps):
        count = part.shape[0] // 2
        return part[:count], swap(part[count:], bit)

    def split(keep, coming):
        total = added(keep, coming)
        return total[0], total[1]

    far_both = near_bit | far_bit

    def z_send(first, second):
        part = jnp.stack([first, second], axis=1)
        return part[0], swap(part[1], far_bit), swap(part[2], near_bit), swap(part[3], far_both)

    def z_sum(own, *coming):
        part = own.astype(F32)
        for other in coming:
            part = part + other.astype(F32)
        part = part.astype(BF16)
        for bit in others:
            part = added(part, swap(part, bit))
        return part

    def z_share(part):
        return part, swap(part, far_bit), swap(part, near_bit), swap(part, far_both)

    def z_join(*parts):
        part = jnp.stack(parts)
        return part[:, 0], part[:, 1]

    def both(first, second, first_bit, second_bit):
        return swap(first, first_bit), swap(second, second_bit)

    def tied(token, *values):
        return lax.optimization_barrier(values + (token,))[:-1]

    def unpack(parts, taps, at_once, start, slots, base, into, name):
        piece = pl.BlockSpec(
            (2, PIECES // 2, at_once, channels // PIECES, channels // 2), lambda i: (0, 0, start // at_once + i, 0, 0)
        )
        operands, specs = [place, *parts], [SMEM, piece, piece]
        if into is not None:
            operands, specs = operands + [into], specs + [anywhere]
        out_spec = pl.BlockSpec((at_once, channels, channels), lambda i: (base // at_once + i, 0, 0))
        (out,) = call(
            unpack_kernel, name, operands, specs, [(out_spec, shape((slots, channels, channels), F32))],
            32, grid=(taps // at_once,), aliases={} if into is None else {3: 0},
        )
        return out

    two_keep, two_send, shifted_two, bias_two, residual_grad = weight_grad(
        residual, met2[0], met2[1], stats2, met2, normed_grad, met3, stats3, norm_rows[2], act_two, cotangent,
        "weight_two_grad",
    )
    two_coming = swap(two_send, 1)
    grad_two, near4, cross4, stats4, sums4 = conv_back(
        shifted_two, 1, middle, stats1, met1, norm_rows[1], "conv_two_back"
    )
    met4 = meet(near4, cross4, stats4)
    two_first, two_second = split(two_keep, behind(two_coming, near4))
    two_first, two_second = halve(two_first, 2), halve(two_second, 4)
    one_keep, one_send, shifted_one, bias_one = weight_grad(
        middle, met1[0], met1[1], stats1, met1, grad_two, met4, stats4, norm_rows[1], act_one, None,
        "weight_one_grad",
    )
    def after_token(token, *values):
        return lax.optimization_barrier(values + (token,))[:-1]

    def add_halves(token, first, second):
        one, two = after_token(token, first[1], second[1])
        return added(first[0], one), added(second[0], two)

    def join_halves(token, first, second, coming):
        one, two = after_token(token, *coming)
        return jnp.concatenate([first, one]), jnp.concatenate([second, two])

    one_coming = swap(behind(one_send, two_first[1], two_second[1]), 1)
    two_first, two_second = add_halves(shifted_one, two_first, two_second)
    token = two_first
    two_first, two_second = halve(two_first, 4), halve(two_second, 2)
    grad_one, near5, cross5, stats5, sums5 = conv_back(
        shifted_one, 0, x, own0, met0, norm_rows[0], "conv_one_back", (two_first[0], two_second[0])
    )
    met5 = meet(near5, cross5, stats5)

    one_first, one_second = split(one_keep, *after_token(near5, one_coming))
    token = one_first
    one_first, one_second = halve(one_first, 2), halve(one_second, 4)

    two_first, two_second = add_halves(token, two_first, two_second)
    token = two_first
    two = z_send(two_first, two_second)

    piece_dims = (channels // PIECES, channels // 2)
    small_parts = shape((4,) + piece_dims, BF16)
    image_grad, small = call(
        last_kernel, "image_grad",
        (grad_one, *met5, stats5, x, own0, *met0, norm_rows[0], residual_grad,
         bias_one, bias_two, sums5, sums4, sums3, matrix_sums),
        [field, edge, edge, stat, stat, field, stat, edge, edge, stat, stat, field] + [stat] * 6,
        [(field, field_b16), (whole(4, *piece_dims), small_parts)], 32, after=(token,),
    )
    for bit in others:
        small = added(small, swap(small, bit))

    one_first, one_second = add_halves(small, one_first, one_second)
    token = one_first
    one_first, one_second = halve(one_first, 4), halve(one_second, 2)

    two = z_sum(*after_token(token, *two))
    token = two
    two = z_share(jnp.concatenate([two.reshape((-1,) + piece_dims), small]))

    one_first, one_second = add_halves(token, one_first, one_second)
    token = one_first
    one = z_send(one_first, one_second)

    two = jnp.stack(after_token(token, *two))
    token = two
    two_first = jnp.concatenate([two[:, :13], two[:, 26:]], axis=1)
    two_second = two[:, 13:26]
    two_coming = both(two_first, two_second, 4, 2)

    one = z_sum(*after_token(token, *one))
    token = one
    one = z_share(one)

    two_first, two_second = join_halves(token, two_first, two_second, two_coming)
    token = two_first
    two_coming = both(two_first, two_second, 2, 4)

    one_first, one_second = z_join(*after_token(token, *one))
    token = one_first
    one_coming = both(one_first, one_second, 4, 2)
    image_there = permute(behind(image_grad, token).reshape(1, band, width, channels), turned)

    two = jnp.concatenate(join_halves(token, two_first, two_second, two_coming), axis=1)
    token = two
    two = two, swap(two, 1)

    one_first, one_second = join_halves(token, one_first, one_second, one_coming)
    token = one_first
    one_coming = both(one_first, one_second, 2, 4)

    two = after_token(token, *two)
    weights, qk_grad, value_weight_grad, proj_weight_grad = call(
        unpack_two_kernel, "unpack_two", (place, *two), [SMEM] + [whole(*two[0].shape)] * 2,
        [
            (
                pl.BlockSpec((3, channels, channels), lambda i: (3 + jnp.minimum(i, 2), 0, 0)),
                shape((18, channels, channels), F32),
            ),
            (whole(2, channels, channels), shape((2, channels, channels), F32)),
            (square, shape((channels, channels), F32)),
            (square, shape((channels, channels), F32)),
        ],
        40, grid=(4,),
    )
    small = jnp.stack(two)[:, :, 13:17].astype(F32)
    small = jnp.sum(small.reshape((-1, 2, 2) + piece_dims), axis=(0, 1))
    small = jnp.concatenate([small[0], small[1]], axis=1)
    token = qk_grad

    one = jnp.stack(join_halves(token, one_first, one_second, one_coming))
    one, image_there = lax.optimization_barrier((one, image_there))
    token = one
    one = one, swap(one, 1)

    weights = unpack(one, 9, 3, 0, 18, 0, weights, "unpack_one")

    return (
        output_there,
        image_there,
        weights.reshape(2, 3, 3, channels, channels),
        small[0:2],
        small[2:5],
        small[5:8],
        qk_grad,
        value_weight_grad,
        proj_weight_grad,
        small[8:10],
        small[10],
    )


def solution(mesh):
    split = P("batch", "seq", None, None)
    in_specs = (split, P("batch", "seq", None), split) + (P(),) * 9
    out_specs = (split, split) + (P(),) * 9
    return jax.shard_map(body, mesh=mesh, in_specs=in_specs, out_specs=out_specs, check_vma=False)
```

```python
import functools

import jax
import jax.numpy as jnp
from jax import lax
from jax.experimental import pallas as pl
from jax.experimental.pallas import tpu as pltpu
from jax.sharding import PartitionSpec as P

GROUPS = 32
EPSILON = 1e-06
MASKED_SCORE = -1e30
F32 = jnp.float32
BF16 = jnp.bfloat16
MIB = 1024 * 1024
PIECES = 32
LIMITS = {
    "conv_one": 46, "conv_two": 46, "weight_two_grad": 24, "weight_one_grad": 20, "conv_two_back": 36, "conv_one_back": 36,
    "attend": 40, "attend_first": 32, "key_value_grad": 46, "early": 14, "matrix_grad": 16, "unpack_two": 40, "unpack_one": 16,
    "first": 8, "masks": 12, "normed": 8, "output": 8, "image_grad": 12,
}


def params(mib):
    return pltpu.CompilerParams(vmem_limit_bytes=mib * MIB)


def shape(dims, dtype):
    return jax.ShapeDtypeStruct(dims, dtype)


SMEM = pl.BlockSpec(memory_space=pltpu.SMEM)
IN_HBM = pl.BlockSpec(memory_space=pltpu.HBM)


def whole(*dims):
    return pl.BlockSpec(dims, lambda *_: (0,) * len(dims))


def group_sum(row):
    channels = row.shape[1]
    lane = lax.broadcasted_iota(jnp.int32, row.shape, 1)
    step = 1
    while step < channels // GROUPS:
        ahead = pltpu.roll(row, channels - step, 1)
        behind = pltpu.roll(row, step, 1)
        row = row + jnp.where((lane & step) == 0, ahead, behind)
        step *= 2
    return row


def rows_of(*parts):
    channels = parts[0].shape[1]
    line = lax.broadcasted_iota(jnp.int32, (8, channels), 0)
    out = jnp.zeros((8, channels), F32)
    for i, part in enumerate(parts):
        out = jnp.where(line == i, jnp.broadcast_to(part, (8, channels)), out)
    return out


def eight(row):
    return jnp.broadcast_to(row, (8, row.shape[1]))


def local_stats(values, channels, pixels):
    count = float(pixels * (channels // GROUPS))
    mean = group_sum(eight(jnp.sum(values, axis=0, keepdims=True)))[0:1] / count
    centered = values - mean
    square = group_sum(eight(jnp.sum(centered * centered, axis=0, keepdims=True)))[0:1]
    return mean, square


def joined_stats(own, near, cross, pair, pixels):
    bands = [own[0:2], near[32:34], cross[32:34], pair[0:2]]
    channels = bands[0].shape[1]
    count = float(pixels * (channels // GROUPS))
    mean = (bands[0][0:1] + bands[1][0:1] + bands[2][0:1] + bands[3][0:1]) * 0.25
    total = 0.0
    for band in bands:
        gap = band[0:1] - mean
        total = total + band[1:2] + count * gap * gap
    return mean, lax.rsqrt(total / (4.0 * count) + EPSILON)


def joined_sums(own, near, cross, pair, pixels):
    bands = [own[0:2], near[32:34], cross[32:34], pair[0:2]]
    channels = bands[0].shape[1]
    count = 4.0 * float(pixels * (channels // GROUPS))
    sums = (bands[0] + bands[1]) + (bands[2] + bands[3])
    return sums[0:1] / count, sums[1:2] / count


def sigmoid(values):
    return 0.5 * jnp.tanh(0.5 * values) + 0.5


def edges_out(side_ref, out_ref, near_ref, cross_ref, stats):
    pixels = out_ref.shape[0]
    side = side_ref[0]
    last = pixels - 32
    near_ref[0:32, :] = out_ref[pl.ds(pl.multiple_of(last * (1 - side), 32), 32), :].astype(F32)
    cross_ref[0:32, :] = out_ref[pl.ds(pl.multiple_of(last * side, 32), 32), :].astype(F32)
    near_ref[32:40, :] = stats
    cross_ref[32:40, :] = stats


def columns_of(frame, shifted, rows):
    for b in range(3):
        shifted[b] = frame[7 + b : 7 + b + rows, :].astype(BF16)


def masked(values, mask):
    channels = values.shape[1]
    return [values[:, i * 128 : (i + 1) * 128] * mask for i in range(channels // 128)]


def tap_rows(shifted, mask_ref, start, count, row):
    parts = []
    for b in range(3):
        block = shifted[b, pl.ds(pl.multiple_of(row * 32 + start, 32), count), :]
        parts += masked(block, mask_ref[b, start : start + count, :])
    return parts


def fetch_rows(weights, index, buffer, arrived, row, order):
    copies = [
        pltpu.make_async_copy(weights.at[index, r], buffer.at[r], arrived.at[r]) for r in order
    ]

    @pl.when(row == 0)
    def _():
        for copy in copies:
            copy.start()

    return copies


def wait_row(copies, row):
    for step, copy in enumerate(copies):

        @pl.when(row == step)
        def _(copy=copy):
            copy.wait()


def first_kernel(image_ref, tiles_ref, side_ref, near_ref, cross_ref, stats_ref):
    pixels, channels = image_ref.shape
    mean, square = local_stats(image_ref[...].astype(F32), channels, pixels)
    stats = rows_of(mean, square, tiles_ref[0:1], tiles_ref[1:2])
    stats_ref[...] = stats
    edges_out(side_ref, image_ref, near_ref, cross_ref, stats)


def mask_kernel(where_ref, own_ref, near_ref, cross_ref, pair_ref, mask_ref, column_ref, row_ref, frame):
    side, first, last = where_ref[0], where_ref[1], where_ref[2]

    def line(ref, base):
        return jnp.concatenate([ref[base + 2 : base + 3, :], ref[base + 3 : base + 4, :]], axis=1)

    own, near, cross, pair = line(own_ref, 0), line(near_ref, 32), line(cross_ref, 32), line(pair_ref, 0)
    pixels = own.shape[1]
    row_ref[...] = jnp.concatenate([own, pair, near, cross], axis=1)

    def upright(row):
        return jnp.transpose(jnp.broadcast_to(row, (128, row.shape[1])))

    column = upright(own)
    column_ref[...] = column
    above = jnp.where(side == 0, cross[:, pixels - 128 :], near[:, pixels - 128 :])
    below = jnp.where(side == 0, near[:, :128], cross[:, :128])
    outside = jnp.full((32, 128), -1.0, F32)
    frame[0:8, :] = jnp.zeros((8, 128), F32)
    frame[8:40, :] = jnp.where(first == 1, outside, upright(above)[96:128, :])
    frame[40 : 40 + pixels, :] = column
    frame[40 + pixels : 72 + pixels, :] = jnp.where(last == 1, outside, upright(below)[0:32, :])
    frame[72 + pixels : 80 + pixels, :] = jnp.zeros((8, 128), F32)
    place = lax.broadcasted_iota(jnp.int32, (pixels, 128), 0) & 31
    for a in range(3):
        for b in range(3):
            start = 8 + a * 32 + b - 1
            same = frame[start : start + pixels, :] == column
            if b == 0:
                same = same & (place > 0)
            if b == 2:
                same = same & (place < 31)
            mask_ref[a * 3 + b] = jnp.where(same, 1.0, 0.0).astype(BF16)


def conv_kernel(
    index, side_ref, x_ref, near_ref, cross_ref, pair_ref, stats_ref, rows_ref, mask_ref, weights, skip_ref,
    out_ref, act_ref, near_out, cross_out, stats_out, frame, shifted, buffer, arrived,
):
    row = pl.program_id(0)
    pixels, channels = x_ref.shape
    copies = fetch_rows(weights, index, buffer, arrived, row, (0, 1, 2))

    @pl.when(row == 0)
    def _():
        mean, inverse = joined_stats(stats_ref[...], near_ref[...], cross_ref[...], pair_ref[...], pixels)
        scale, shift, bias = rows_ref[0:1, :], rows_ref[1:2, :], rows_ref[2:3, :]

        def act(values):
            pre = (values - mean) * inverse * scale + shift
            return pre * sigmoid(pre)

        side = side_ref[0]
        near, cross = near_ref[0:32, :], cross_ref[0:32, :]
        frame[0:8, :] = jnp.zeros((8, channels), F32)
        frame[8:40, :] = act(jnp.where(side == 0, cross, near))
        frame[40 : 40 + pixels, :] = act(x_ref[...].astype(F32))
        frame[40 + pixels : 72 + pixels, :] = act(jnp.where(side == 0, near, cross))
        frame[72 + pixels : 80 + pixels, :] = jnp.zeros((8, channels), F32)
        columns_of(frame, shifted, pixels + 64)
        act_ref[...] = shifted[1, 32 : 32 + pixels, :]
        start = jnp.broadcast_to(bias, (pixels, channels))
        if skip_ref is not None:
            start = start + skip_ref[...].astype(F32)
        out_ref[...] = start

    wait_row(copies, row)
    weight = buffer[row].reshape(3 * channels, channels)
    for i in range(pixels // 256):
        taps = jnp.concatenate(tap_rows(shifted, mask_ref, i * 256, 256, row), axis=1)
        out_ref[i * 256 : (i + 1) * 256, :] += jnp.dot(taps, weight, preferred_element_type=F32)

    @pl.when(row == 2)
    def _():
        mean, square = local_stats(out_ref[...], channels, pixels)
        stats = rows_of(mean, square)
        stats_out[...] = stats
        edges_out(side_ref, out_ref, near_out, cross_out, stats)


def normed_kernel(x_ref, near_ref, cross_ref, pair_ref, stats_ref, rows_ref, out_ref):
    pixels = x_ref.shape[0]
    mean, inverse = joined_stats(stats_ref[...], near_ref[...], cross_ref[...], pair_ref[...], pixels)
    out_ref[...] = ((x_ref[...] - mean) * inverse * rows_ref[0:1, :] + rows_ref[1:2, :]).astype(BF16)


def nn(left, right):
    return jnp.dot(left, right, preferred_element_type=F32)


def nt(left, right):
    return lax.dot_general(left, right, (((1,), (1,)), ((), ())), preferred_element_type=F32)


def early_kernel(own_ref, pair_ref, cot_own, cot_pair, qk_ref, value_ref, proj_ref, bias_ref, *outs):
    for rows_ref, cot_ref, (keys, values, queries, grads) in ((own_ref, cot_own, outs[:4]), (pair_ref, cot_pair, outs[4:])):
        rows = rows_ref[...]
        queries[...] = (nn(rows, qk_ref[0]) + bias_ref[0:1, :]).astype(BF16)
        keys[...] = nn(rows, qk_ref[1]).astype(BF16)
        values[...] = (nn(rows, value_ref[...]) + bias_ref[1:2, :]).astype(BF16)
        grads[...] = nt(cot_ref[...], proj_ref[...]).astype(BF16)


def attend_first_kernel(
    keys_own, values_own, keys_pair, values_pair, queries_ref, column_ref, row_ref,
    weights_ref, top_ref, total_ref, sum_ref,
):
    pixels, channels = queries_ref.shape
    scale = channels ** (-0.5)
    block = 512

    def step(i, carry):
        part = pl.ds(pl.multiple_of(i * block, block), block)
        queries = queries_ref[part, :]
        column = column_ref[part, 0:1]
        scores = []
        for j, keys in enumerate((keys_own, keys_pair)):
            product = nt(queries, keys[...]) * scale
            scores.append(jnp.where(column == row_ref[:, j * pixels : (j + 1) * pixels], product, MASKED_SCORE))
        top = jnp.maximum(*[jnp.max(s, axis=1, keepdims=True) for s in scores])
        total, summed = 0.0, 0.0
        for j, (score, values) in enumerate(zip(scores, (values_own, values_pair))):
            weights = jnp.exp(score - top)
            total = total + jnp.sum(weights, axis=1, keepdims=True)
            rounded = weights.astype(BF16)
            weights_ref[part, j * pixels : (j + 1) * pixels] = rounded
            summed = summed + nn(rounded, values[...])
        top_ref[part, :] = jnp.broadcast_to(top, (block, 128))
        total_ref[part, :] = jnp.broadcast_to(total, (block, 128))
        sum_ref[part, :] = summed
        return carry

    lax.fori_loop(0, pixels // block, step, 0)


def attend_kernel(
    near_ref, cross_ref, keys_own, values_own, keys_pair, values_pair, queries_ref, grads_ref,
    weights_ref, top_ref, total_ref, sum_ref, qk_ref, value_ref, bias_ref, column_ref, row_ref,
    attended_ref, query_grad_ref, totals_ref, far_keys, far_values,
):
    pixels, channels = near_ref.shape
    scale = channels ** (-0.5)
    for i, ref in enumerate((near_ref, cross_ref)):
        part = slice(i * pixels, (i + 1) * pixels)
        rows = ref[...]
        far_keys[part, :] = nn(rows, qk_ref[1]).astype(BF16)
        far_values[part, :] = (nn(rows, value_ref[...]) + bias_ref[1:2, :]).astype(BF16)
    block = totals_ref.shape[2]

    def step(i, carry):
        part = pl.ds(pl.multiple_of(i * block, block), block)
        queries, upstream = queries_ref[part, :], grads_ref[part, :]
        product = nt(queries, far_keys[...]) * scale
        scores = jnp.where(column_ref[part, 0:1] == row_ref[:, 2 * pixels :], product, MASKED_SCORE)
        first_top = top_ref[part, 0:1]
        top = jnp.maximum(first_top, jnp.max(scores, axis=1, keepdims=True))
        shrink = jnp.exp(first_top - top)
        weights = jnp.exp(scores - top)
        total = total_ref[part, 0:1] * shrink + jnp.sum(weights, axis=1, keepdims=True)
        inverse = 1.0 / total
        attended = (sum_ref[part, :] * shrink + nn(weights.astype(BF16), far_values[...])) * inverse
        attended_ref[part, :] = attended.astype(BF16)
        delta = jnp.sum(attended * upstream.astype(F32), axis=1, keepdims=True)
        score_grad = (weights * inverse * (nt(upstream, far_values[...]) - delta)).astype(BF16)
        query_grad = nn(score_grad, far_keys[...])
        factor = shrink * inverse
        for j, (keys, values) in enumerate(((keys_own, values_own), (keys_pair, values_pair))):
            held = weights_ref[part, j * pixels : (j + 1) * pixels].astype(F32)
            score_grad = (held * factor * (nt(upstream, values[...]) - delta)).astype(BF16)
            query_grad = query_grad + nn(score_grad, keys[...])
        query_grad_ref[part, :] = (query_grad * scale).astype(BF16)
        log_total = jnp.transpose(jnp.broadcast_to(top + jnp.log(total), (block, 128)))
        turned = jnp.transpose(jnp.broadcast_to(delta, (block, 128)))
        totals_ref[i, 0:1, :] = log_total[0:1, :]
        totals_ref[i, 1:2, :] = turned[0:1, :]
        totals_ref[i, 2:8, :] = jnp.zeros((6, block), F32)
        return carry

    lax.fori_loop(0, pixels // block, step, 0)


def out_kernel(attended_ref, residual_ref, matrix_ref, bias_ref, out_ref):
    out_ref[...] = (residual_ref[...] + nn(attended_ref[...], matrix_ref[...]) + bias_ref[0:1, :]).astype(BF16)


def norm_back_sums(upstream, hat, gain):
    outer = jnp.sum(upstream * hat, axis=0, keepdims=True)
    inner = jnp.sum(upstream, axis=0, keepdims=True)
    first = group_sum(eight(inner * gain))[0:1]
    second = group_sum(eight(outer * gain))[0:1]
    return rows_of(outer, inner), rows_of(first, second)


def key_kernel(
    side_ref, keys, values, queries_own, grads_own, queries_pair, grads_pair, near_hbm, cot_near_hbm, cross_hbm,
    cot_cross_hbm, query_grad_hbm, qk_ref, value_ref, proj_ref, bias_ref,
    totals_own, totals_pair, totals_near, totals_cross, column_ref, row_ref,
    residual_hbm, stats_ref, near_ref, cross_ref, pair_ref, rows_ref,
    key_grad_ref, value_grad_ref, normed_grad_ref, near_out, cross_out, stats_out, sums_out,
    key_sum, value_sum, held, query_grad_ref, residual_ref, arrived,
):
    pixels, channels = keys.shape
    scale = channels ** (-0.5)
    sources = (
        queries_own, grads_own, queries_pair, grads_pair, near_hbm, cot_near_hbm, cross_hbm, cot_cross_hbm,
        query_grad_hbm, residual_hbm,
    )
    targets = [held.at[i] for i in range(8)] + [query_grad_ref, residual_ref]
    coming = [
        pltpu.make_async_copy(source, target, arrived.at[i]) for i, (source, target) in enumerate(zip(sources, targets))
    ]
    for copy in coming:
        copy.start()
    key_sum[...] = jnp.zeros_like(key_sum)
    value_sum[...] = jnp.zeros_like(value_sum)
    chunk = totals_own.shape[2]
    blocks = pixels // chunk

    def add(queries, upstream, totals, i, at):
        scores = nt(keys[...], queries) * scale
        weights = jnp.exp(scores - totals[i, 0:1, :])
        weights = jnp.where(column_ref[:, 0:1] == row_ref[at, 0:1, :], weights, 0.0)
        value_sum[...] += nn(weights.astype(BF16), upstream)
        prob_grad = nt(values[...], upstream)
        score_grad = (weights * (prob_grad - totals[i, 1:2, :])).astype(BF16)
        key_sum[...] += nn(score_grad, queries)

    for group, totals in enumerate((totals_own, totals_pair, totals_near, totals_cross)):
        coming[2 * group].wait()
        coming[2 * group + 1].wait()

        def step(i, carry, group=group, totals=totals):
            part = pl.ds(pl.multiple_of(i * chunk, chunk), chunk)
            queries, upstream = held[2 * group, part, :], held[2 * group + 1, part, :]
            if group >= 2:
                queries = (nn(queries, qk_ref[0]) + bias_ref[0:1, :]).astype(BF16)
                upstream = nt(upstream, proj_ref[...]).astype(BF16)
            add(queries, upstream, totals, i, group * blocks + i)
            return carry

        lax.fori_loop(0, blocks, step, 0)
    coming[8].wait()
    coming[9].wait()
    key_grad = (key_sum[...] * scale).astype(BF16)
    value_grad = value_sum[...].astype(BF16)
    key_grad_ref[...] = key_grad
    value_grad_ref[...] = value_grad
    normed_grad = nt(query_grad_ref[...], qk_ref[0]) + nt(key_grad, qk_ref[1]) + nt(value_grad, value_ref[...])
    normed_grad_ref[...] = normed_grad
    mean, inverse = joined_stats(stats_ref[...], near_ref[...], cross_ref[...], pair_ref[...], pixels)
    hat = (residual_ref[...] - mean) * inverse
    sums, groups = norm_back_sums(normed_grad, hat, rows_ref[0:1, :])
    sums_out[...] = sums
    stats_out[...] = groups
    edges_out(side_ref, normed_grad_ref, near_out, cross_out, groups)


def scatter_pieces(place_ref, product, tap, keep_ref, send_ref, matrix):
    rows, channels = product.shape
    half, height = channels // 2, rows // PIECES
    matrix[...] = product.astype(BF16)
    for q in range(PIECES):
        into = keep_ref if q < PIECES // 2 else send_ref
        for stream in range(2):
            start = pl.multiple_of((q ^ place_ref[stream]) * height, height)
            into[stream, q % (PIECES // 2), tap] = matrix[pl.ds(start, height), stream * half : (stream + 1) * half]


def tn(left, right):
    return lax.dot_general(left, right, (((0,), (0,)), ((), ())), preferred_element_type=F32)


def matrix_kernel(
    place_ref, normed_ref, query_grad_ref, key_grad_ref, value_grad_ref, attended_ref, cotangent_ref,
    keep_ref, send_ref, sums_ref, turned, matrix,
):
    turned[...] = jnp.transpose(normed_ref[...])
    for tap, ref in enumerate((query_grad_ref, key_grad_ref, value_grad_ref)):
        scatter_pieces(place_ref, nn(turned[...], ref[...]), tap, keep_ref, send_ref, matrix)
    turned[...] = jnp.transpose(attended_ref[...])
    scatter_pieces(place_ref, nn(turned[...], cotangent_ref[...]), 3, keep_ref, send_ref, matrix)
    total = [
        jnp.sum(ref[...].astype(F32), axis=0, keepdims=True)
        for ref in (query_grad_ref, value_grad_ref, cotangent_ref)
    ]
    sums_ref[...] = rows_of(*total)


def weight_grad_kernel(
    with_cotangent, place_ref, side_ref, x_ref, x_near, x_cross, stats_ref, near_ref, cross_ref, pair_ref,
    g_ref, g_near, g_cross, g_pair, g_stats, rows_ref, act_ref, mask_ref, *rest,
):
    if with_cotangent:
        cot_ref, cot_edges, matrix_keep, matrix_send = rest[0], rest[1:5], rest[5], rest[6]
        keep_ref, send_ref, shifted, sums_ref, own_ref, frame, turned, matrix = rest[7:]
    else:
        keep_ref, send_ref, shifted, sums_ref, frame, turned, matrix = rest
    row = pl.program_id(0)
    pixels, channels = x_ref.shape

    @pl.when(row == 0)
    def _():
        mean, inverse = joined_stats(stats_ref[...], near_ref[...], cross_ref[...], pair_ref[...], pixels)
        mean_h, mean_hx = joined_sums(g_stats[...], g_near[...], g_cross[...], g_pair[...], pixels)
        gain = rows_ref[0:1, :]
        side = side_ref[0]

        def back(grad, values):
            hat = (values - mean) * inverse
            return inverse * (grad * gain - mean_h - hat * mean_hx)

        def pick(near, cross):
            return jnp.where(side == 0, cross, near), jnp.where(side == 0, near, cross)

        g_above, g_below = pick(g_near[0:32, :], g_cross[0:32, :])
        x_above, x_below = pick(x_near[0:32, :], x_cross[0:32, :])
        above, below = back(g_above, x_above), back(g_below, x_below)
        own = back(g_ref[...], x_ref[...])
        if with_cotangent:
            near_top, near_bottom, cross_top, cross_bottom = [ref[...].astype(F32) for ref in cot_edges]
            above = above + jnp.where(side == 0, cross_bottom, near_bottom)
            below = below + jnp.where(side == 0, near_top, cross_top)
            own = own + cot_ref[...].astype(F32)
            own_ref[...] = own
            for tap in range(4):
                keep_ref[:, :, 9 + tap] = matrix_keep[:, :, tap]
                send_ref[:, :, 9 + tap] = matrix_send[:, :, tap]
        sums_ref[...] = rows_of(jnp.sum(own, axis=0, keepdims=True))
        frame[0:8, :] = jnp.zeros((8, channels), F32)
        frame[8:40, :] = above
        frame[40 : 40 + pixels, :] = own
        frame[40 + pixels : 72 + pixels, :] = below
        frame[72 + pixels : 80 + pixels, :] = jnp.zeros((8, channels), F32)
        columns_of(frame, shifted, pixels + 64)
        turned[...] = jnp.transpose(act_ref[...])

    for b in range(3):
        block = shifted[b, pl.ds(pl.multiple_of(row * 32, 32), pixels), :]
        block = jnp.concatenate(masked(block, mask_ref[b]), axis=1)
        product = nn(turned[...], block)
        scatter_pieces(place_ref, product, 8 - row * 3 - b, keep_ref, send_ref, matrix)


def conv_back_kernel(
    index, side_ref, shifted, mask_ref, weights, x_ref, stats_ref, near_ref, cross_ref, pair_ref, rows_ref,
    out_ref, near_out, cross_out, stats_out, sums_out, buffer, arrived,
):
    row = pl.program_id(0)
    pixels, channels = x_ref.shape
    copies = fetch_rows(weights, index, buffer, arrived, row, (2, 1, 0))

    @pl.when(row == 0)
    def _():
        out_ref[...] = jnp.zeros_like(out_ref)

    wait_row(copies, row)
    weight = jnp.concatenate([buffer[2 - row, 2 - b] for b in range(3)], axis=1)
    for i in range(pixels // 256):
        taps = jnp.concatenate(tap_rows(shifted, mask_ref, i * 256, 256, row), axis=1)
        out_ref[i * 256 : (i + 1) * 256, :] += nt(taps, weight)

    @pl.when(row == 2)
    def _():
        mean, inverse = joined_stats(stats_ref[...], near_ref[...], cross_ref[...], pair_ref[...], pixels)
        gain, shift = rows_ref[0:1, :], rows_ref[1:2, :]
        hat = (x_ref[...].astype(F32) - mean) * inverse
        pre = hat * gain + shift
        gate = sigmoid(pre)
        upstream = out_ref[...] * (gate * (1.0 + pre * (1.0 - gate)))
        out_ref[...] = upstream
        sums, groups = norm_back_sums(upstream, hat, gain)
        sums_out[...] = sums
        stats_out[...] = groups
        edges_out(side_ref, out_ref, near_out, cross_out, groups)


def last_kernel(
    g_ref, g_near, g_cross, g_pair, g_stats, x_ref, stats_ref, near_ref, cross_ref, pair_ref, rows_ref, add_ref,
    bias_one, bias_two, sums_one, sums_two, sums_three, matrix_sums, out_ref, small_ref,
):
    pixels = x_ref.shape[0]
    half = x_ref.shape[1] // 2
    parts = [bias_one[0:1], bias_two[0:1]]
    parts += [ref[i : i + 1] for i in range(2) for ref in (sums_one, sums_two, sums_three)]
    parts += [matrix_sums[i : i + 1] for i in range(3)]
    line = lax.broadcasted_iota(jnp.int32, (16, 2 * half), 0)
    rows = jnp.zeros((16, 2 * half), F32)
    for i, part in enumerate(parts):
        rows = jnp.where(line == i, jnp.broadcast_to(part, rows.shape), rows)
    high = rows.astype(BF16)
    low = (rows - high.astype(F32)).astype(BF16)
    for i, part in enumerate((high, low)):
        small_ref[2 * i] = part[:, :half]
        small_ref[2 * i + 1] = part[:, half:]
    mean, inverse = joined_stats(stats_ref[...], near_ref[...], cross_ref[...], pair_ref[...], pixels)
    mean_h, mean_hx = joined_sums(g_stats[...], g_near[...], g_cross[...], g_pair[...], pixels)
    hat = (x_ref[...].astype(F32) - mean) * inverse
    grad = inverse * (g_ref[...] * rows_ref[0:1, :] - mean_h - hat * mean_hx)
    out_ref[...] = (add_ref[...] + grad).astype(BF16)


def unpack_kernel(place_ref, own_ref, other_ref, *rest):
    out_ref = rest[-1]
    height, half = own_ref.shape[3], own_ref.shape[4]
    for tap in range(out_ref.shape[0]):
        for q in range(PIECES):
            pieces = own_ref if q < PIECES // 2 else other_ref
            for stream in range(2):
                start = pl.multiple_of((q ^ place_ref[stream]) * height, height)
                values = pieces[stream, q % (PIECES // 2), tap].astype(F32)
                out_ref[tap, pl.ds(start, height), stream * half : (stream + 1) * half] = values


def spread_pieces(place_ref, halves, tap, out):
    height, half = halves[0].shape[2], halves[0].shape[3]
    for q in range(PIECES):
        pieces = halves[q // (PIECES // 2)]
        for stream in range(2):
            start = pl.multiple_of((q ^ place_ref[stream]) * height, height)
            values = pieces[q % (PIECES // 2), stream * 17 + tap].astype(F32)
            out[pl.ds(start, height), stream * half : (stream + 1) * half] = values


def unpack_two_kernel(place_ref, own_ref, other_ref, weights_ref, qk_ref, value_ref, proj_ref):
    step = pl.program_id(0)
    halves = (own_ref, other_ref)

    @pl.when(step < 3)
    def _():
        for tap in range(3):
            spread_pieces(place_ref, halves, step * 3 + tap, weights_ref.at[tap])

    @pl.when(step == 3)
    def _():
        for tap, out in enumerate((qk_ref.at[0], qk_ref.at[1], value_ref, proj_ref)):
            spread_pieces(place_ref, halves, 9 + tap, out)


def body(
    image,
    tile_map,
    out_grad,
    conv_weight,
    conv_bias,
    norm_gain,
    norm_shift,
    qk_weight,
    value_weight,
    proj_weight,
    qv_bias,
    proj_bias,
):
    band, width, channels = image.shape[1], image.shape[2], image.shape[3]
    pixels = band * width
    lanes = lax.axis_size("batch")
    devices = 4 * lanes

    def turned(flat):
        s, b = flat // lanes, flat % lanes
        core, high = b % 2, s // 2
        return (core * 2 + s % 2) * lanes + (b - core + high)

    def xored(flat, bits):
        return flat ^ bits

    def permute(x, to):
        return lax.ppermute(x, ("seq", "batch"), [(i, to(i)) for i in range(devices)])

    near_bit, pair_bit = lanes, 1

    def to_near(i):
        return i ^ near_bit

    def to_pair(i):
        return i ^ pair_bit

    def to_cross(i):
        return i ^ (near_bit | pair_bit)

    def meet(near, cross, stats):
        return permute(near, to_near), permute(cross, to_cross), permute(stats, to_pair)

    seq, lane = lax.axis_index("seq"), lax.axis_index("batch")
    core, low, high = lane % 2, seq % 2, seq // 2
    side = low.astype(jnp.int32).reshape(1)
    spot = jnp.stack([low, ((low == 0) & (core == 0)), ((low == 1) & (core == 1))]).astype(jnp.int32)
    x_bit, y_bit = (lane // 2) % 2, (lane // 4) % 2
    tail = low * 2 + high
    place = jnp.stack(
        [core * 16 + x_bit * 8 + y_bit * 4 + tail, core * 16 + y_bit * 8 + x_bit * 4 + tail, tail]
    ).astype(jnp.int32)

    def block8(*rows):
        rows = [r.astype(F32).reshape(1, channels) for r in rows]
        return jnp.concatenate(rows + [jnp.zeros((8 - len(rows), channels), F32)], axis=0)

    norm_rows = [block8(norm_gain[i], norm_shift[i], conv_bias[min(i, 1)]) for i in range(3)]
    bias_rows = block8(qv_bias[0], qv_bias[1], proj_bias, jnp.zeros((channels,), F32))

    row_f32 = shape((40, channels), F32)
    stat_f32 = shape((8, channels), F32)
    field_f32 = shape((pixels, channels), F32)
    field_b16 = shape((pixels, channels), BF16)
    field = whole(pixels, channels)
    edge = whole(40, channels)
    stat = whole(8, channels)

    def call(kernel, name, operands, in_specs, outs, mib, flops=0, scratch=(), grid=(1,), after=(), aliases=None):
        count = len(operands)

        def run(*refs):
            kernel(*refs[:count], *refs[count + len(after) :])

        moved = sum(o.size * o.dtype.itemsize for o in operands) + sum(o.size * o.dtype.itemsize for _, o in outs)
        return pl.pallas_call(
            run if after else kernel,
            in_specs=list(in_specs) + [pl.BlockSpec(memory_space=pl.ANY)] * len(after),
            out_specs=[spec for spec, _ in outs],
            out_shape=[out for _, out in outs],
            scratch_shapes=list(scratch),
            grid=grid,
            input_output_aliases=aliases or {},
            compiler_params=params(LIMITS.get(name, mib)),
            cost_estimate=pl.CostEstimate(flops=int(flops), bytes_accessed=int(moved), transcendentals=0),
            name=name,
        )(*operands, *after)

    def behind(x, *deps):
        return lax.optimization_barrier((x,) + deps)[0]

    row_out, stat_out = (edge, row_f32), (stat, stat_f32)
    matmul = 2.0 * pixels * channels * channels

    image_flat = image.reshape(pixels, channels)
    cot_flat = out_grad.reshape(pixels, channels)
    tiles = tile_map.astype(F32).reshape(2, pixels // 2)
    x = permute(image_flat, turned)
    near0, cross0, stats0 = call(
        first_kernel, "first", (image_flat, tiles, side), [field, whole(2, pixels // 2), SMEM],
        [row_out, row_out, stat_out], 16, after=(permute(block8(norm_gain[0]), to_pair),),
    )
    own0 = permute(stats0, turned)
    pair0 = permute(stats0, lambda i: to_pair(turned(i)))
    near0 = permute(near0, lambda i: to_near(turned(i)))
    cross0 = permute(cross0, lambda i: to_cross(turned(i)))
    masks, column_tiles, row_tiles = call(
        mask_kernel, "masks", (spot, own0, near0, cross0, pair0), [SMEM, stat, edge, edge, stat],
        [
            (whole(9, pixels, 128), shape((9, pixels, 128), BF16)),
            (whole(pixels, 128), shape((pixels, 128), F32)),
            (whole(1, 4 * pixels), shape((1, 4 * pixels), F32)),
        ],
        24, scratch=[pltpu.VMEM((pixels + 80, 128), F32)],
    )

    half = pixels // 2
    cot_first = permute(behind(cot_flat[:half], x), turned)

    mask_block = pl.BlockSpec((3, pixels, 128), lambda i: (i, 0, 0))

    row_buffer = [pltpu.VMEM((3, 3, channels, channels), BF16), pltpu.SemaphoreType.DMA((3,))]

    def conv(x, met, stats, rows, index, skip, name, after=()):
        near, cross, pair = met
        specs = [
            SMEM, field, edge, edge, stat, stat, stat, mask_block, IN_HBM,
        ]
        operands = [side, x, near, cross, pair, stats, rows, masks, conv_weight]
        kernel = functools.partial(conv_kernel, index)
        if skip is None:

            def kernel(*refs):
                return conv_kernel(index, *refs[:9], None, *refs[9:])
        else:
            specs.append(field)
            operands.append(skip)
        return call(
            kernel, name, operands, specs,
            [(field, field_f32), (field, field_b16), row_out, row_out, stat_out],
            40, 9 * matmul,
            [pltpu.VMEM((pixels + 80, channels), F32), pltpu.VMEM((3, pixels + 64, channels), BF16), *row_buffer],
            (3,), after,
        )

    met0 = (near0, cross0, pair0)
    middle, act_one, near1, cross1, stats1 = conv(x, met0, own0, norm_rows[0], 0, None, "conv_one")
    met1 = meet(near1, cross1, stats1)
    cot_second = permute(behind(cot_flat[half:], cot_first, met1[2]), turned)
    residual, act_two, near2, cross2, stats2 = conv(
        middle, met1, stats1, norm_rows[1], 1, x, "conv_two", (cot_first,)
    )
    met2 = meet(near2, cross2, stats2)

    (normed,) = call(
        normed_kernel, "normed", (residual, *met2, stats2, norm_rows[2]), [field, edge, edge, stat, stat, stat],
        [(field, field_b16)], 16, after=(cot_second,),
    )
    cotangent = jnp.concatenate([cot_first, cot_second], axis=0)

    normed_near = permute(normed, to_near)
    normed_pair = permute(normed, to_pair)

    block = 512
    anywhere = pl.BlockSpec(memory_space=pl.ANY)
    blocks = pixels // block
    totals_out = (whole(blocks, 8, block), shape((blocks, 8, block), F32))
    square = whole(channels, channels)
    cot_pair = permute(cotangent, to_pair)
    keys, values, queries, grads, keys_pair, values_pair, queries_pair, grads_pair = call(
        early_kernel, "early",
        (normed, normed_pair, cotangent, cot_pair, qk_weight, value_weight, proj_weight, bias_rows),
        [field] * 4 + [whole(2, channels, channels), square, square, stat],
        [(field, field_b16)] * 8, 32, 8 * matmul,
    )
    lane_field = (whole(pixels, 128), shape((pixels, 128), F32))
    weights, tops, sums, products = call(
        attend_first_kernel, "attend_first", (keys, values, keys_pair, values_pair, queries, column_tiles, row_tiles),
        [field] * 5 + [whole(pixels, 128), whole(1, 4 * pixels)],
        [(whole(pixels, 2 * pixels), shape((pixels, 2 * pixels), BF16)), lane_field, lane_field, (field, field_f32)],
        32, 2 * 2 * matmul * pixels / channels,
    )
    normed_cross = permute(behind(normed_near, products), to_pair)
    cot_near = permute(behind(cotangent, normed_near), to_near)
    attended, query_grad, totals = call(
        attend_kernel, "attend",
        (normed_near, normed_cross, keys, values, keys_pair, values_pair, queries, grads, weights, tops, sums, products, qk_weight, value_weight, bias_rows,
         column_tiles, row_tiles),
        [field] * 8 + [whole(pixels, 2 * pixels), whole(pixels, 128), whole(pixels, 128), field] + [whole(2, channels, channels), square, stat, whole(pixels, 128), whole(1, 4 * pixels)],
        [(field, field_b16), (field, field_b16), totals_out],
        58, 4 * matmul + 4 * 4 * matmul * pixels / channels,
        [pltpu.VMEM((2 * pixels, channels), BF16)] * 2,
    )

    totals_pair, totals_near, totals_cross = (permute(totals, to) for to in (to_pair, to_near, to_cross))
    cot_cross = permute(behind(cot_near, attended), to_pair)
    (output,) = call(
        out_kernel, "output", (attended, residual, proj_weight, block8(proj_bias)), [field, field, square, stat],
        [(field, field_b16)], 16, matmul, after=(cot_near,),
    )
    output_there = permute(output.reshape(1, band, width, channels), turned)
    key_grad, value_grad, normed_grad, near3, cross3, stats3, sums3 = call(
        key_kernel, "key_value_grad",
        (side, keys, values, queries, grads, queries_pair, grads_pair, normed_near, cot_near, normed_cross, cot_cross,
         query_grad, qk_weight, value_weight, proj_weight, bias_rows,
         totals, totals_pair, totals_near, totals_cross, column_tiles, row_tiles.reshape(4 * blocks, 1, block),
         residual, stats2, *met2, norm_rows[2]),
        [SMEM] + [field] * 2 + [anywhere] * 9 + [whole(2, channels, channels), square, square, stat]
        + [totals_out[0]] * 4
        + [whole(pixels, 128), whole(4 * blocks, 1, block), anywhere, stat, edge, edge, stat, stat],
        [(field, field_b16), (field, field_b16), (field, field_f32), row_out, row_out, stat_out, stat_out],
        60, 7 * matmul + 4 * 4 * matmul * pixels / channels,
        [pltpu.VMEM((pixels, channels), F32)] * 2
        + [
            pltpu.VMEM((8, pixels, channels), BF16), pltpu.VMEM((pixels, channels), BF16),
            pltpu.VMEM((pixels, channels), F32), pltpu.SemaphoreType.DMA((10,)),
        ],
    )
    met3 = meet(near3, cross3, stats3)


    def pieces(taps):
        dims = (2, PIECES // 2, taps, channels // PIECES, channels // 2)
        return [(whole(*dims), shape(dims, BF16))] * 2

    matrix_keep, matrix_send, matrix_sums = call(
        matrix_kernel, "matrix_grad", (place, normed, query_grad, key_grad, value_grad, attended, cotangent),
        [SMEM] + [field] * 6, pieces(4) + [stat_out], 32, 4 * matmul,
        [pltpu.VMEM((channels, pixels), BF16), pltpu.VMEM((channels, channels), BF16)], after=(output_there,),
    )

    def weight_grad(x, x_near, x_cross, stats, met, grad, grad_met, grad_stats, rows, act, cot, name, after=()):
        near, cross, pair = met
        g_near, g_cross, g_pair = grad_met
        spread = (3, pixels + 64, channels)
        extra, extra_in, extra_out = [], [], []
        if cot is not None:
            top = pl.BlockSpec((32, channels), lambda i: (0, 0))
            bottom = pl.BlockSpec((32, channels), lambda i: (pixels // 32 - 1, 0))
            extra = [cot, cot_near, cot_near, cot_cross, cot_cross, matrix_keep, matrix_send]
            extra_in = [field, top, bottom, top, bottom] + [spec for spec, _ in pieces(4)]
            extra_out = [(field, field_f32)]
        return call(
            functools.partial(weight_grad_kernel, cot is not None), name,
            [place, side, x, x_near, x_cross, stats, near, cross, pair, grad, g_near, g_cross, g_pair, grad_stats,
             rows, act, masks] + extra,
            [SMEM, SMEM, field, edge, edge, stat, edge, edge, stat, field, edge, edge, stat, stat, stat, field, mask_block]
            + extra_in,
            pieces(9 if cot is None else 13) + [(whole(*spread), shape(spread, BF16)), stat_out] + extra_out,
            58, 9 * matmul,
            [pltpu.VMEM((pixels + 80, channels), F32), pltpu.VMEM((channels, pixels), BF16), pltpu.VMEM((channels, channels), BF16)],
            (3,), after,
        )

    def conv_back(shifted, index, x, stats, met, rows, name, after=()):
        return call(
            functools.partial(conv_back_kernel, index), name, (side, shifted, masks, conv_weight, x, stats, *met, rows),
            [
                SMEM, whole(3, pixels + 64, channels), mask_block, IN_HBM,
                field, stat, edge, edge, stat, stat,
            ],
            [(field, field_f32), row_out, row_out, stat_out, stat_out],
            40, 9 * matmul, row_buffer, (3,), after,
        )

    far_bit = 2 * lanes
    others = []
    bit = 8
    while bit < lanes:
        others.append(bit)
        bit *= 2

    def swap(x, bit):
        return permute(x, lambda i: i ^ bit)

    def added(left, right):
        return (left.astype(F32) + right.astype(F32)).astype(BF16)

    def halve(part, bit, *deps):
        count = part.shape[0] // 2
        return part[:count], swap(part[count:], bit)

    def split(keep, coming):
        total = added(keep, coming)
        return total[0], total[1]

    far_both = near_bit | far_bit

    def z_send(first, second):
        part = jnp.stack([first, second], axis=1)
        return part[0], swap(part[1], far_bit), swap(part[2], near_bit), swap(part[3], far_both)

    def z_sum(own, *coming):
        part = own.astype(F32)
        for other in coming:
            part = part + other.astype(F32)
        part = part.astype(BF16)
        for bit in others:
            part = added(part, swap(part, bit))
        return part

    def z_share(part):
        return part, swap(part, far_bit), swap(part, near_bit), swap(part, far_both)

    def z_join(*parts):
        part = jnp.stack(parts)
        return part[:, 0], part[:, 1]

    def both(first, second, first_bit, second_bit):
        return swap(first, first_bit), swap(second, second_bit)

    def tied(token, *values):
        return lax.optimization_barrier(values + (token,))[:-1]

    def unpack(parts, taps, at_once, start, slots, base, into, name):
        piece = pl.BlockSpec(
            (2, PIECES // 2, at_once, channels // PIECES, channels // 2), lambda i: (0, 0, start // at_once + i, 0, 0)
        )
        operands, specs = [place, *parts], [SMEM, piece, piece]
        if into is not None:
            operands, specs = operands + [into], specs + [anywhere]
        out_spec = pl.BlockSpec((at_once, channels, channels), lambda i: (base // at_once + i, 0, 0))
        (out,) = call(
            unpack_kernel, name, operands, specs, [(out_spec, shape((slots, channels, channels), F32))],
            32, grid=(taps // at_once,), aliases={} if into is None else {3: 0},
        )
        return out

    two_keep, two_send, shifted_two, bias_two, residual_grad = weight_grad(
        residual, met2[0], met2[1], stats2, met2, normed_grad, met3, stats3, norm_rows[2], act_two, cotangent,
        "weight_two_grad",
    )
    two_coming = swap(two_send, 1)
    grad_two, near4, cross4, stats4, sums4 = conv_back(
        shifted_two, 1, middle, stats1, met1, norm_rows[1], "conv_two_back"
    )
    met4 = meet(near4, cross4, stats4)
    two_first, two_second = split(two_keep, behind(two_coming, near4))
    two_first, two_second = halve(two_first, 2), halve(two_second, 4)
    one_keep, one_send, shifted_one, bias_one = weight_grad(
        middle, met1[0], met1[1], stats1, met1, grad_two, met4, stats4, norm_rows[1], act_one, None,
        "weight_one_grad",
    )
    def after_token(token, *values):
        return lax.optimization_barrier(values + (token,))[:-1]

    def add_halves(token, first, second):
        one, two = after_token(token, first[1], second[1])
        return added(first[0], one), added(second[0], two)

    def join_halves(token, first, second, coming):
        one, two = after_token(token, *coming)
        return jnp.concatenate([first, one]), jnp.concatenate([second, two])

    one_coming = swap(behind(one_send, two_first[1], two_second[1]), 1)
    two_first, two_second = add_halves(shifted_one, two_first, two_second)
    token = two_first
    two_first, two_second = halve(two_first, 4), halve(two_second, 2)
    grad_one, near5, cross5, stats5, sums5 = conv_back(
        shifted_one, 0, x, own0, met0, norm_rows[0], "conv_one_back", (two_first[0], two_second[0])
    )
    met5 = meet(near5, cross5, stats5)

    one_first, one_second = split(one_keep, *after_token(near5, one_coming))
    token = one_first
    one_first, one_second = halve(one_first, 2), halve(one_second, 4)

    two_first, two_second = add_halves(token, two_first, two_second)
    token = two_first
    two = z_send(two_first, two_second)

    piece_dims = (channels // PIECES, channels // 2)
    small_parts = shape((4,) + piece_dims, BF16)
    image_grad, small = call(
        last_kernel, "image_grad",
        (grad_one, *met5, stats5, x, own0, *met0, norm_rows[0], residual_grad,
         bias_one, bias_two, sums5, sums4, sums3, matrix_sums),
        [field, edge, edge, stat, stat, field, stat, edge, edge, stat, stat, field] + [stat] * 6,
        [(field, field_b16), (whole(4, *piece_dims), small_parts)], 32, after=(token,),
    )
    for bit in others:
        small = added(small, swap(small, bit))

    one_first, one_second = add_halves(small, one_first, one_second)
    token = one_first
    one_first, one_second = halve(one_first, 4), halve(one_second, 2)

    two = z_sum(*after_token(token, *two))
    token = two
    two = z_share(jnp.concatenate([two.reshape((-1,) + piece_dims), small]))

    one_first, one_second = add_halves(token, one_first, one_second)
    token = one_first
    one = z_send(one_first, one_second)

    two = jnp.stack(after_token(token, *two))
    token = two
    two_first = jnp.concatenate([two[:, :13], two[:, 26:]], axis=1)
    two_second = two[:, 13:26]
    two_coming = both(two_first, two_second, 4, 2)

    one = z_sum(*after_token(token, *one))
    token = one
    one = z_share(one)

    two_first, two_second = join_halves(token, two_first, two_second, two_coming)
    token = two_first
    two_coming = both(two_first, two_second, 2, 4)

    one_first, one_second = z_join(*after_token(token, *one))
    token = one_first
    one_coming = both(one_first, one_second, 4, 2)
    image_there = permute(behind(image_grad, token).reshape(1, band, width, channels), turned)

    two = jnp.concatenate(join_halves(token, two_first, two_second, two_coming), axis=1)
    token = two
    two = two, swap(two, 1)

    one_first, one_second = join_halves(token, one_first, one_second, one_coming)
    token = one_first
    one_coming = both(one_first, one_second, 2, 4)

    two = after_token(token, *two)
    weights, qk_grad, value_weight_grad, proj_weight_grad = call(
        unpack_two_kernel, "unpack_two", (place, *two), [SMEM] + [whole(*two[0].shape)] * 2,
        [
            (
                pl.BlockSpec((3, channels, channels), lambda i: (3 + jnp.minimum(i, 2), 0, 0)),
                shape((18, channels, channels), F32),
            ),
            (whole(2, channels, channels), shape((2, channels, channels), F32)),
            (square, shape((channels, channels), F32)),
            (square, shape((channels, channels), F32)),
        ],
        40, grid=(4,),
    )
    small = jnp.stack(two)[:, :, 13:17].astype(F32)
    small = jnp.sum(small.reshape((-1, 2, 2) + piece_dims), axis=(0, 1))
    small = jnp.concatenate([small[0], small[1]], axis=1)
    token = qk_grad

    one = jnp.stack(join_halves(token, one_first, one_second, one_coming))
    one, image_there = lax.optimization_barrier((one, image_there))
    token = one
    one = one, swap(one, 1)

    weights = unpack(one, 9, 3, 0, 18, 0, weights, "unpack_one")

    return (
        output_there,
        image_there,
        weights.reshape(2, 3, 3, channels, channels),
        small[0:2],
        small[2:5],
        small[5:8],
        qk_grad,
        value_weight_grad,
        proj_weight_grad,
        small[8:10],
        small[10],
    )


def solution(mesh):
    split = P("batch", "seq", None, None)
    in_specs = (split, P("batch", "seq", None), split) + (P(),) * 9
    out_specs = (split, split) + (P(),) * 9
    return jax.shard_map(body, mesh=mesh, in_specs=in_specs, out_specs=out_specs, check_vma=False)
```

```python
import functools

import jax
import jax.numpy as jnp
from jax import lax
from jax.experimental import pallas as pl
from jax.experimental.pallas import tpu as pltpu
from jax.sharding import PartitionSpec as P

GROUPS = 32
EPSILON = 1e-06
MASKED_SCORE = -1e30
F32 = jnp.float32
BF16 = jnp.bfloat16
MIB = 1024 * 1024
PIECES = 32
LIMITS = {
    "conv_one": 46, "conv_two": 46, "weight_two_grad": 24, "weight_one_grad": 20, "conv_two_back": 36, "conv_one_back": 36,
    "attend": 40, "attend_first": 32, "key_value_grad": 46, "early": 14, "matrix_grad": 16, "unpack_two": 40, "unpack_one": 16,
    "first": 8, "masks": 12, "normed": 8, "output": 8, "image_grad": 12,
}


def params(mib):
    return pltpu.CompilerParams(vmem_limit_bytes=mib * MIB)


def shape(dims, dtype):
    return jax.ShapeDtypeStruct(dims, dtype)


SMEM = pl.BlockSpec(memory_space=pltpu.SMEM)
IN_HBM = pl.BlockSpec(memory_space=pltpu.HBM)


def whole(*dims):
    return pl.BlockSpec(dims, lambda *_: (0,) * len(dims))


def group_sum(row):
    channels = row.shape[1]
    lane = lax.broadcasted_iota(jnp.int32, row.shape, 1)
    step = 1
    while step < channels // GROUPS:
        ahead = pltpu.roll(row, channels - step, 1)
        behind = pltpu.roll(row, step, 1)
        row = row + jnp.where((lane & step) == 0, ahead, behind)
        step *= 2
    return row


def rows_of(*parts):
    channels = parts[0].shape[1]
    line = lax.broadcasted_iota(jnp.int32, (8, channels), 0)
    out = jnp.zeros((8, channels), F32)
    for i, part in enumerate(parts):
        out = jnp.where(line == i, jnp.broadcast_to(part, (8, channels)), out)
    return out


def eight(row):
    return jnp.broadcast_to(row, (8, row.shape[1]))


def local_stats(values, channels, pixels):
    count = float(pixels * (channels // GROUPS))
    mean = group_sum(eight(jnp.sum(values, axis=0, keepdims=True)))[0:1] / count
    centered = values - mean
    square = group_sum(eight(jnp.sum(centered * centered, axis=0, keepdims=True)))[0:1]
    return mean, square


def joined_stats(own, near, cross, pair, pixels):
    bands = [own[0:2], near[32:34], cross[32:34], pair[0:2]]
    channels = bands[0].shape[1]
    count = float(pixels * (channels // GROUPS))
    mean = (bands[0][0:1] + bands[1][0:1] + bands[2][0:1] + bands[3][0:1]) * 0.25
    total = 0.0
    for band in bands:
        gap = band[0:1] - mean
        total = total + band[1:2] + count * gap * gap
    return mean, lax.rsqrt(total / (4.0 * count) + EPSILON)


def joined_sums(own, near, cross, pair, pixels):
    bands = [own[0:2], near[32:34], cross[32:34], pair[0:2]]
    channels = bands[0].shape[1]
    count = 4.0 * float(pixels * (channels // GROUPS))
    sums = (bands[0] + bands[1]) + (bands[2] + bands[3])
    return sums[0:1] / count, sums[1:2] / count


def sigmoid(values):
    return 0.5 * jnp.tanh(0.5 * values) + 0.5


def edges_out(side_ref, out_ref, near_ref, cross_ref, stats):
    pixels = out_ref.shape[0]
    side = side_ref[0]
    last = pixels - 32
    near_ref[0:32, :] = out_ref[pl.ds(pl.multiple_of(last * (1 - side), 32), 32), :].astype(F32)
    cross_ref[0:32, :] = out_ref[pl.ds(pl.multiple_of(last * side, 32), 32), :].astype(F32)
    near_ref[32:40, :] = stats
    cross_ref[32:40, :] = stats


def columns_of(frame, shifted, rows):
    for b in range(3):
        shifted[b] = frame[7 + b : 7 + b + rows, :].astype(BF16)


def masked(values, mask):
    channels = values.shape[1]
    return [values[:, i * 128 : (i + 1) * 128] * mask for i in range(channels // 128)]


def tap_rows(shifted, mask_ref, start, count, row):
    parts = []
    for b in range(3):
        block = shifted[b, pl.ds(pl.multiple_of(row * 32 + start, 32), count), :]
        parts += masked(block, mask_ref[b, start : start + count, :])
    return parts


def fetch_rows(weights, index, buffer, arrived, row, order):
    copies = [
        pltpu.make_async_copy(weights.at[index, r], buffer.at[r], arrived.at[r]) for r in order
    ]

    @pl.when(row == 0)
    def _():
        for copy in copies:
            copy.start()

    return copies


def wait_row(copies, row):
    for step, copy in enumerate(copies):

        @pl.when(row == step)
        def _(copy=copy):
            copy.wait()


def first_kernel(image_ref, tiles_ref, side_ref, near_ref, cross_ref, stats_ref):
    pixels, channels = image_ref.shape
    mean, square = local_stats(image_ref[...].astype(F32), channels, pixels)
    stats = rows_of(mean, square, tiles_ref[0:1], tiles_ref[1:2])
    stats_ref[...] = stats
    edges_out(side_ref, image_ref, near_ref, cross_ref, stats)


def mask_kernel(where_ref, own_ref, near_ref, cross_ref, pair_ref, mask_ref, column_ref, row_ref, frame):
    side, first, last = where_ref[0], where_ref[1], where_ref[2]

    def line(ref, base):
        return jnp.concatenate([ref[base + 2 : base + 3, :], ref[base + 3 : base + 4, :]], axis=1)

    own, near, cross, pair = line(own_ref, 0), line(near_ref, 32), line(cross_ref, 32), line(pair_ref, 0)
    pixels = own.shape[1]
    row_ref[...] = jnp.concatenate([own, pair, near, cross], axis=1)

    def upright(row):
        return jnp.transpose(jnp.broadcast_to(row, (128, row.shape[1])))

    column = upright(own)
    column_ref[...] = column
    above = jnp.where(side == 0, cross[:, pixels - 128 :], near[:, pixels - 128 :])
    below = jnp.where(side == 0, near[:, :128], cross[:, :128])
    outside = jnp.full((32, 128), -1.0, F32)
    frame[0:8, :] = jnp.zeros((8, 128), F32)
    frame[8:40, :] = jnp.where(first == 1, outside, upright(above)[96:128, :])
    frame[40 : 40 + pixels, :] = column
    frame[40 + pixels : 72 + pixels, :] = jnp.where(last == 1, outside, upright(below)[0:32, :])
    frame[72 + pixels : 80 + pixels, :] = jnp.zeros((8, 128), F32)
    place = lax.broadcasted_iota(jnp.int32, (pixels, 128), 0) & 31
    for a in range(3):
        for b in range(3):
            start = 8 + a * 32 + b - 1
            same = frame[start : start + pixels, :] == column
            if b == 0:
                same = same & (place > 0)
            if b == 2:
                same = same & (place < 31)
            mask_ref[a * 3 + b] = jnp.where(same, 1.0, 0.0).astype(BF16)


def conv_kernel(
    index, side_ref, x_ref, near_ref, cross_ref, pair_ref, stats_ref, rows_ref, mask_ref, weights, skip_ref,
    out_ref, act_hbm, near_out, cross_out, stats_out, frame, shifted, buffer, arrived, stored,
):
    row = pl.program_id(0)
    pixels, channels = x_ref.shape
    store_act = pltpu.make_async_copy(shifted.at[1, pl.ds(32, pixels), :], act_hbm, stored)
    copies = fetch_rows(weights, index, buffer, arrived, row, (0, 1, 2))

    @pl.when(row == 0)
    def _():
        mean, inverse = joined_stats(stats_ref[...], near_ref[...], cross_ref[...], pair_ref[...], pixels)
        scale, shift, bias = rows_ref[0:1, :], rows_ref[1:2, :], rows_ref[2:3, :]

        def act(values):
            pre = (values - mean) * inverse * scale + shift
            return pre * sigmoid(pre)

        side = side_ref[0]
        near, cross = near_ref[0:32, :], cross_ref[0:32, :]
        frame[0:8, :] = jnp.zeros((8, channels), F32)
        frame[8:40, :] = act(jnp.where(side == 0, cross, near))
        frame[40 : 40 + pixels, :] = act(x_ref[...].astype(F32))
        frame[40 + pixels : 72 + pixels, :] = act(jnp.where(side == 0, near, cross))
        frame[72 + pixels : 80 + pixels, :] = jnp.zeros((8, channels), F32)
        columns_of(frame, shifted, pixels + 64)
        store_act.start()
        start = jnp.broadcast_to(bias, (pixels, channels))
        if skip_ref is not None:
            start = start + skip_ref[...].astype(F32)
        out_ref[...] = start

    wait_row(copies, row)
    weight = buffer[row].reshape(3 * channels, channels)
    for i in range(pixels // 256):
        taps = jnp.concatenate(tap_rows(shifted, mask_ref, i * 256, 256, row), axis=1)
        out_ref[i * 256 : (i + 1) * 256, :] += jnp.dot(taps, weight, preferred_element_type=F32)

    @pl.when(row == 2)
    def _():
        mean, square = local_stats(out_ref[...], channels, pixels)
        stats = rows_of(mean, square)
        stats_out[...] = stats
        edges_out(side_ref, out_ref, near_out, cross_out, stats)
        store_act.wait()


def normed_kernel(x_ref, near_ref, cross_ref, pair_ref, stats_ref, rows_ref, out_ref):
    pixels = x_ref.shape[0]
    mean, inverse = joined_stats(stats_ref[...], near_ref[...], cross_ref[...], pair_ref[...], pixels)
    out_ref[...] = ((x_ref[...] - mean) * inverse * rows_ref[0:1, :] + rows_ref[1:2, :]).astype(BF16)


def nn(left, right):
    return jnp.dot(left, right, preferred_element_type=F32)


def nt(left, right):
    return lax.dot_general(left, right, (((1,), (1,)), ((), ())), preferred_element_type=F32)


def early_kernel(own_ref, pair_ref, cot_own, cot_pair, qk_ref, value_ref, proj_ref, bias_ref, *outs):
    for rows_ref, cot_ref, (keys, values, queries, grads) in ((own_ref, cot_own, outs[:4]), (pair_ref, cot_pair, outs[4:])):
        rows = rows_ref[...]
        queries[...] = (nn(rows, qk_ref[0]) + bias_ref[0:1, :]).astype(BF16)
        keys[...] = nn(rows, qk_ref[1]).astype(BF16)
        values[...] = (nn(rows, value_ref[...]) + bias_ref[1:2, :]).astype(BF16)
        grads[...] = nt(cot_ref[...], proj_ref[...]).astype(BF16)


def attend_first_kernel(
    keys_own, values_own, keys_pair, values_pair, queries_ref, column_ref, row_ref,
    weights_ref, top_ref, total_ref, sum_ref,
):
    pixels, channels = queries_ref.shape
    scale = channels ** (-0.5)
    block = 512

    def step(i, carry):
        part = pl.ds(pl.multiple_of(i * block, block), block)
        queries = queries_ref[part, :]
        column = column_ref[part, 0:1]
        scores = []
        for j, keys in enumerate((keys_own, keys_pair)):
            product = nt(queries, keys[...]) * scale
            scores.append(jnp.where(column == row_ref[:, j * pixels : (j + 1) * pixels], product, MASKED_SCORE))
        top = jnp.maximum(*[jnp.max(s, axis=1, keepdims=True) for s in scores])
        total, summed = 0.0, 0.0
        for j, (score, values) in enumerate(zip(scores, (values_own, values_pair))):
            weights = jnp.exp(score - top)
            total = total + jnp.sum(weights, axis=1, keepdims=True)
            rounded = weights.astype(BF16)
            weights_ref[part, j * pixels : (j + 1) * pixels] = rounded
            summed = summed + nn(rounded, values[...])
        top_ref[part, :] = jnp.broadcast_to(top, (block, 128))
        total_ref[part, :] = jnp.broadcast_to(total, (block, 128))
        sum_ref[part, :] = summed
        return carry

    lax.fori_loop(0, pixels // block, step, 0)


def attend_kernel(
    near_ref, cross_ref, keys_own, values_own, keys_pair, values_pair, queries_ref, grads_ref,
    weights_ref, top_ref, total_ref, sum_ref, qk_ref, value_ref, bias_ref, column_ref, row_ref,
    attended_ref, query_grad_ref, totals_ref, far_keys, far_values,
):
    pixels, channels = near_ref.shape
    scale = channels ** (-0.5)
    for i, ref in enumerate((near_ref, cross_ref)):
        part = slice(i * pixels, (i + 1) * pixels)
        rows = ref[...]
        far_keys[part, :] = nn(rows, qk_ref[1]).astype(BF16)
        far_values[part, :] = (nn(rows, value_ref[...]) + bias_ref[1:2, :]).astype(BF16)
    block = totals_ref.shape[2]

    def step(i, carry):
        part = pl.ds(pl.multiple_of(i * block, block), block)
        queries, upstream = queries_ref[part, :], grads_ref[part, :]
        product = nt(queries, far_keys[...]) * scale
        scores = jnp.where(column_ref[part, 0:1] == row_ref[:, 2 * pixels :], product, MASKED_SCORE)
        first_top = top_ref[part, 0:1]
        top = jnp.maximum(first_top, jnp.max(scores, axis=1, keepdims=True))
        shrink = jnp.exp(first_top - top)
        weights = jnp.exp(scores - top)
        total = total_ref[part, 0:1] * shrink + jnp.sum(weights, axis=1, keepdims=True)
        inverse = 1.0 / total
        attended = (sum_ref[part, :] * shrink + nn(weights.astype(BF16), far_values[...])) * inverse
        attended_ref[part, :] = attended.astype(BF16)
        delta = jnp.sum(attended * upstream.astype(F32), axis=1, keepdims=True)
        score_grad = (weights * inverse * (nt(upstream, far_values[...]) - delta)).astype(BF16)
        query_grad = nn(score_grad, far_keys[...])
        factor = shrink * inverse
        for j, (keys, values) in enumerate(((keys_own, values_own), (keys_pair, values_pair))):
            held = weights_ref[part, j * pixels : (j + 1) * pixels].astype(F32)
            score_grad = (held * factor * (nt(upstream, values[...]) - delta)).astype(BF16)
            query_grad = query_grad + nn(score_grad, keys[...])
        query_grad_ref[part, :] = (query_grad * scale).astype(BF16)
        log_total = jnp.transpose(jnp.broadcast_to(top + jnp.log(total), (block, 128)))
        turned = jnp.transpose(jnp.broadcast_to(delta, (block, 128)))
        totals_ref[i, 0:1, :] = log_total[0:1, :]
        totals_ref[i, 1:2, :] = turned[0:1, :]
        totals_ref[i, 2:8, :] = jnp.zeros((6, block), F32)
        return carry

    lax.fori_loop(0, pixels // block, step, 0)


def out_kernel(attended_ref, residual_ref, matrix_ref, bias_ref, out_ref):
    out_ref[...] = (residual_ref[...] + nn(attended_ref[...], matrix_ref[...]) + bias_ref[0:1, :]).astype(BF16)


def norm_back_sums(upstream, hat, gain):
    outer = jnp.sum(upstream * hat, axis=0, keepdims=True)
    inner = jnp.sum(upstream, axis=0, keepdims=True)
    first = group_sum(eight(inner * gain))[0:1]
    second = group_sum(eight(outer * gain))[0:1]
    return rows_of(outer, inner), rows_of(first, second)


def key_kernel(
    side_ref, keys, values, queries_own, grads_own, queries_pair, grads_pair, near_hbm, cot_near_hbm, cross_hbm,
    cot_cross_hbm, query_grad_hbm, qk_ref, value_ref, proj_ref, bias_ref,
    totals_own, totals_pair, totals_near, totals_cross, column_ref, row_ref,
    residual_hbm, stats_ref, near_ref, cross_ref, pair_ref, rows_ref,
    key_grad_ref, value_grad_ref, normed_grad_ref, near_out, cross_out, stats_out, sums_out,
    key_sum, value_sum, held, query_grad_ref, residual_ref, arrived,
):
    pixels, channels = keys.shape
    scale = channels ** (-0.5)
    sources = (
        queries_own, grads_own, queries_pair, grads_pair, near_hbm, cot_near_hbm, cross_hbm, cot_cross_hbm,
        query_grad_hbm, residual_hbm,
    )
    targets = [held.at[i] for i in range(8)] + [query_grad_ref, residual_ref]
    coming = [
        pltpu.make_async_copy(source, target, arrived.at[i]) for i, (source, target) in enumerate(zip(sources, targets))
    ]
    for copy in coming:
        copy.start()
    key_sum[...] = jnp.zeros_like(key_sum)
    value_sum[...] = jnp.zeros_like(value_sum)
    chunk = totals_own.shape[2]
    blocks = pixels // chunk

    def add(queries, upstream, totals, i, at):
        scores = nt(keys[...], queries) * scale
        weights = jnp.exp(scores - totals[i, 0:1, :])
        weights = jnp.where(column_ref[:, 0:1] == row_ref[at, 0:1, :], weights, 0.0)
        value_sum[...] += nn(weights.astype(BF16), upstream)
        prob_grad = nt(values[...], upstream)
        score_grad = (weights * (prob_grad - totals[i, 1:2, :])).astype(BF16)
        key_sum[...] += nn(score_grad, queries)

    for group, totals in enumerate((totals_own, totals_pair, totals_near, totals_cross)):
        coming[2 * group].wait()
        coming[2 * group + 1].wait()

        def step(i, carry, group=group, totals=totals):
            part = pl.ds(pl.multiple_of(i * chunk, chunk), chunk)
            queries, upstream = held[2 * group, part, :], held[2 * group + 1, part, :]
            if group >= 2:
                queries = (nn(queries, qk_ref[0]) + bias_ref[0:1, :]).astype(BF16)
                upstream = nt(upstream, proj_ref[...]).astype(BF16)
            add(queries, upstream, totals, i, group * blocks + i)
            return carry

        lax.fori_loop(0, blocks, step, 0)
    coming[8].wait()
    coming[9].wait()
    key_grad = (key_sum[...] * scale).astype(BF16)
    value_grad = value_sum[...].astype(BF16)
    key_grad_ref[...] = key_grad
    value_grad_ref[...] = value_grad
    normed_grad = nt(query_grad_ref[...], qk_ref[0]) + nt(key_grad, qk_ref[1]) + nt(value_grad, value_ref[...])
    normed_grad_ref[...] = normed_grad
    mean, inverse = joined_stats(stats_ref[...], near_ref[...], cross_ref[...], pair_ref[...], pixels)
    hat = (residual_ref[...] - mean) * inverse
    sums, groups = norm_back_sums(normed_grad, hat, rows_ref[0:1, :])
    sums_out[...] = sums
    stats_out[...] = groups
    edges_out(side_ref, normed_grad_ref, near_out, cross_out, groups)


def scatter_pieces(place_ref, product, tap, keep_ref, send_ref, matrix):
    rows, channels = product.shape
    half, height = channels // 2, rows // PIECES
    matrix[...] = product.astype(BF16)
    for q in range(PIECES):
        into = keep_ref if q < PIECES // 2 else send_ref
        for stream in range(2):
            start = pl.multiple_of((q ^ place_ref[stream]) * height, height)
            into[stream, q % (PIECES // 2), tap] = matrix[pl.ds(start, height), stream * half : (stream + 1) * half]


def tn(left, right):
    return lax.dot_general(left, right, (((0,), (0,)), ((), ())), preferred_element_type=F32)


def matrix_kernel(
    place_ref, normed_ref, query_grad_ref, key_grad_ref, value_grad_ref, attended_ref, cotangent_ref,
    keep_ref, send_ref, sums_ref, turned, matrix,
):
    turned[...] = jnp.transpose(normed_ref[...])
    for tap, ref in enumerate((query_grad_ref, key_grad_ref, value_grad_ref)):
        scatter_pieces(place_ref, nn(turned[...], ref[...]), tap, keep_ref, send_ref, matrix)
    turned[...] = jnp.transpose(attended_ref[...])
    scatter_pieces(place_ref, nn(turned[...], cotangent_ref[...]), 3, keep_ref, send_ref, matrix)
    total = [
        jnp.sum(ref[...].astype(F32), axis=0, keepdims=True)
        for ref in (query_grad_ref, value_grad_ref, cotangent_ref)
    ]
    sums_ref[...] = rows_of(*total)


def weight_grad_kernel(
    with_cotangent, place_ref, side_ref, x_ref, x_near, x_cross, stats_ref, near_ref, cross_ref, pair_ref,
    g_ref, g_near, g_cross, g_pair, g_stats, rows_ref, act_ref, mask_ref, *rest,
):
    if with_cotangent:
        cot_ref, cot_edges, matrix_keep, matrix_send = rest[0], rest[1:5], rest[5], rest[6]
        keep_ref, send_ref, shifted, sums_ref, own_ref, frame, turned, matrix = rest[7:]
    else:
        keep_ref, send_ref, shifted, sums_ref, frame, turned, matrix = rest
    row = pl.program_id(0)
    pixels, channels = x_ref.shape

    @pl.when(row == 0)
    def _():
        mean, inverse = joined_stats(stats_ref[...], near_ref[...], cross_ref[...], pair_ref[...], pixels)
        mean_h, mean_hx = joined_sums(g_stats[...], g_near[...], g_cross[...], g_pair[...], pixels)
        gain = rows_ref[0:1, :]
        side = side_ref[0]

        def back(grad, values):
            hat = (values - mean) * inverse
            return inverse * (grad * gain - mean_h - hat * mean_hx)

        def pick(near, cross):
            return jnp.where(side == 0, cross, near), jnp.where(side == 0, near, cross)

        g_above, g_below = pick(g_near[0:32, :], g_cross[0:32, :])
        x_above, x_below = pick(x_near[0:32, :], x_cross[0:32, :])
        above, below = back(g_above, x_above), back(g_below, x_below)
        own = back(g_ref[...], x_ref[...])
        if with_cotangent:
            near_top, near_bottom, cross_top, cross_bottom = [ref[...].astype(F32) for ref in cot_edges]
            above = above + jnp.where(side == 0, cross_bottom, near_bottom)
            below = below + jnp.where(side == 0, near_top, cross_top)
            own = own + cot_ref[...].astype(F32)
            own_ref[...] = own
            for tap in range(4):
                keep_ref[:, :, 9 + tap] = matrix_keep[:, :, tap]
                send_ref[:, :, 9 + tap] = matrix_send[:, :, tap]
        sums_ref[...] = rows_of(jnp.sum(own, axis=0, keepdims=True))
        frame[0:8, :] = jnp.zeros((8, channels), F32)
        frame[8:40, :] = above
        frame[40 : 40 + pixels, :] = own
        frame[40 + pixels : 72 + pixels, :] = below
        frame[72 + pixels : 80 + pixels, :] = jnp.zeros((8, channels), F32)
        columns_of(frame, shifted, pixels + 64)
        turned[...] = jnp.transpose(act_ref[...])

    for b in range(3):
        block = shifted[b, pl.ds(pl.multiple_of(row * 32, 32), pixels), :]
        block = jnp.concatenate(masked(block, mask_ref[b]), axis=1)
        product = nn(turned[...], block)
        scatter_pieces(place_ref, product, 8 - row * 3 - b, keep_ref, send_ref, matrix)


def conv_back_kernel(
    index, side_ref, shifted, mask_ref, weights, x_ref, stats_ref, near_ref, cross_ref, pair_ref, rows_ref,
    out_ref, near_out, cross_out, stats_out, sums_out, buffer, arrived,
):
    row = pl.program_id(0)
    pixels, channels = x_ref.shape
    copies = fetch_rows(weights, index, buffer, arrived, row, (2, 1, 0))

    @pl.when(row == 0)
    def _():
        out_ref[...] = jnp.zeros_like(out_ref)

    wait_row(copies, row)
    weight = jnp.concatenate([buffer[2 - row, 2 - b] for b in range(3)], axis=1)
    for i in range(pixels // 256):
        taps = jnp.concatenate(tap_rows(shifted, mask_ref, i * 256, 256, row), axis=1)
        out_ref[i * 256 : (i + 1) * 256, :] += nt(taps, weight)

    @pl.when(row == 2)
    def _():
        mean, inverse = joined_stats(stats_ref[...], near_ref[...], cross_ref[...], pair_ref[...], pixels)
        gain, shift = rows_ref[0:1, :], rows_ref[1:2, :]
        hat = (x_ref[...].astype(F32) - mean) * inverse
        pre = hat * gain + shift
        gate = sigmoid(pre)
        upstream = out_ref[...] * (gate * (1.0 + pre * (1.0 - gate)))
        out_ref[...] = upstream
        sums, groups = norm_back_sums(upstream, hat, gain)
        sums_out[...] = sums
        stats_out[...] = groups
        edges_out(side_ref, out_ref, near_out, cross_out, groups)


def last_kernel(
    g_ref, g_near, g_cross, g_pair, g_stats, x_ref, stats_ref, near_ref, cross_ref, pair_ref, rows_ref, add_ref,
    bias_one, bias_two, sums_one, sums_two, sums_three, matrix_sums, out_ref, small_ref,
):
    pixels = x_ref.shape[0]
    half = x_ref.shape[1] // 2
    parts = [bias_one[0:1], bias_two[0:1]]
    parts += [ref[i : i + 1] for i in range(2) for ref in (sums_one, sums_two, sums_three)]
    parts += [matrix_sums[i : i + 1] for i in range(3)]
    line = lax.broadcasted_iota(jnp.int32, (16, 2 * half), 0)
    rows = jnp.zeros((16, 2 * half), F32)
    for i, part in enumerate(parts):
        rows = jnp.where(line == i, jnp.broadcast_to(part, rows.shape), rows)
    high = rows.astype(BF16)
    low = (rows - high.astype(F32)).astype(BF16)
    for i, part in enumerate((high, low)):
        small_ref[2 * i] = part[:, :half]
        small_ref[2 * i + 1] = part[:, half:]
    mean, inverse = joined_stats(stats_ref[...], near_ref[...], cross_ref[...], pair_ref[...], pixels)
    mean_h, mean_hx = joined_sums(g_stats[...], g_near[...], g_cross[...], g_pair[...], pixels)
    hat = (x_ref[...].astype(F32) - mean) * inverse
    grad = inverse * (g_ref[...] * rows_ref[0:1, :] - mean_h - hat * mean_hx)
    out_ref[...] = (add_ref[...] + grad).astype(BF16)


def unpack_kernel(place_ref, own_ref, other_ref, *rest):
    out_ref = rest[-1]
    height, half = own_ref.shape[3], own_ref.shape[4]
    for tap in range(out_ref.shape[0]):
        for q in range(PIECES):
            pieces = own_ref if q < PIECES // 2 else other_ref
            for stream in range(2):
                start = pl.multiple_of((q ^ place_ref[stream]) * height, height)
                values = pieces[stream, q % (PIECES // 2), tap].astype(F32)
                out_ref[tap, pl.ds(start, height), stream * half : (stream + 1) * half] = values


def spread_pieces(place_ref, halves, tap, out):
    height, half = halves[0].shape[2], halves[0].shape[3]
    for q in range(PIECES):
        pieces = halves[q // (PIECES // 2)]
        for stream in range(2):
            start = pl.multiple_of((q ^ place_ref[stream]) * height, height)
            values = pieces[q % (PIECES // 2), stream * 17 + tap].astype(F32)
            out[pl.ds(start, height), stream * half : (stream + 1) * half] = values


def unpack_two_kernel(place_ref, own_ref, other_ref, weights_ref, qk_ref, value_ref, proj_ref):
    step = pl.program_id(0)
    halves = (own_ref, other_ref)

    @pl.when(step < 3)
    def _():
        for tap in range(3):
            spread_pieces(place_ref, halves, step * 3 + tap, weights_ref.at[tap])

    @pl.when(step == 3)
    def _():
        for tap, out in enumerate((qk_ref.at[0], qk_ref.at[1], value_ref, proj_ref)):
            spread_pieces(place_ref, halves, 9 + tap, out)


def body(
    image,
    tile_map,
    out_grad,
    conv_weight,
    conv_bias,
    norm_gain,
    norm_shift,
    qk_weight,
    value_weight,
    proj_weight,
    qv_bias,
    proj_bias,
):
    band, width, channels = image.shape[1], image.shape[2], image.shape[3]
    pixels = band * width
    lanes = lax.axis_size("batch")
    devices = 4 * lanes

    def turned(flat):
        s, b = flat // lanes, flat % lanes
        core, high = b % 2, s // 2
        return (core * 2 + s % 2) * lanes + (b - core + high)

    def xored(flat, bits):
        return flat ^ bits

    def permute(x, to):
        return lax.ppermute(x, ("seq", "batch"), [(i, to(i)) for i in range(devices)])

    near_bit, pair_bit = lanes, 1

    def to_near(i):
        return i ^ near_bit

    def to_pair(i):
        return i ^ pair_bit

    def to_cross(i):
        return i ^ (near_bit | pair_bit)

    def meet(near, cross, stats):
        return permute(near, to_near), permute(cross, to_cross), permute(stats, to_pair)

    seq, lane = lax.axis_index("seq"), lax.axis_index("batch")
    core, low, high = lane % 2, seq % 2, seq // 2
    side = low.astype(jnp.int32).reshape(1)
    spot = jnp.stack([low, ((low == 0) & (core == 0)), ((low == 1) & (core == 1))]).astype(jnp.int32)
    x_bit, y_bit = (lane // 2) % 2, (lane // 4) % 2
    tail = low * 2 + high
    place = jnp.stack(
        [core * 16 + x_bit * 8 + y_bit * 4 + tail, core * 16 + y_bit * 8 + x_bit * 4 + tail, tail]
    ).astype(jnp.int32)

    def block8(*rows):
        rows = [r.astype(F32).reshape(1, channels) for r in rows]
        return jnp.concatenate(rows + [jnp.zeros((8 - len(rows), channels), F32)], axis=0)

    norm_rows = [block8(norm_gain[i], norm_shift[i], conv_bias[min(i, 1)]) for i in range(3)]
    bias_rows = block8(qv_bias[0], qv_bias[1], proj_bias, jnp.zeros((channels,), F32))

    row_f32 = shape((40, channels), F32)
    stat_f32 = shape((8, channels), F32)
    field_f32 = shape((pixels, channels), F32)
    field_b16 = shape((pixels, channels), BF16)
    field = whole(pixels, channels)
    edge = whole(40, channels)
    stat = whole(8, channels)

    def call(kernel, name, operands, in_specs, outs, mib, flops=0, scratch=(), grid=(1,), after=(), aliases=None):
        count = len(operands)

        def run(*refs):
            kernel(*refs[:count], *refs[count + len(after) :])

        moved = sum(o.size * o.dtype.itemsize for o in operands) + sum(o.size * o.dtype.itemsize for _, o in outs)
        return pl.pallas_call(
            run if after else kernel,
            in_specs=list(in_specs) + [pl.BlockSpec(memory_space=pl.ANY)] * len(after),
            out_specs=[spec for spec, _ in outs],
            out_shape=[out for _, out in outs],
            scratch_shapes=list(scratch),
            grid=grid,
            input_output_aliases=aliases or {},
            compiler_params=params(LIMITS.get(name, mib)),
            cost_estimate=pl.CostEstimate(flops=int(flops), bytes_accessed=int(moved), transcendentals=0),
            name=name,
        )(*operands, *after)

    def behind(x, *deps):
        return lax.optimization_barrier((x,) + deps)[0]

    row_out, stat_out = (edge, row_f32), (stat, stat_f32)
    matmul = 2.0 * pixels * channels * channels

    image_flat = image.reshape(pixels, channels)
    cot_flat = out_grad.reshape(pixels, channels)
    tiles = tile_map.astype(F32).reshape(2, pixels // 2)
    x = permute(image_flat, turned)
    near0, cross0, stats0 = call(
        first_kernel, "first", (image_flat, tiles, side), [field, whole(2, pixels // 2), SMEM],
        [row_out, row_out, stat_out], 16, after=(permute(block8(norm_gain[0]), to_pair),),
    )
    own0 = permute(stats0, turned)
    pair0 = permute(stats0, lambda i: to_pair(turned(i)))
    near0 = permute(near0, lambda i: to_near(turned(i)))
    cross0 = permute(cross0, lambda i: to_cross(turned(i)))
    masks, column_tiles, row_tiles = call(
        mask_kernel, "masks", (spot, own0, near0, cross0, pair0), [SMEM, stat, edge, edge, stat],
        [
            (whole(9, pixels, 128), shape((9, pixels, 128), BF16)),
            (whole(pixels, 128), shape((pixels, 128), F32)),
            (whole(1, 4 * pixels), shape((1, 4 * pixels), F32)),
        ],
        24, scratch=[pltpu.VMEM((pixels + 80, 128), F32)],
    )

    half = pixels // 2
    cot_first = permute(behind(cot_flat[:half], x), turned)

    mask_block = pl.BlockSpec((3, pixels, 128), lambda i: (i, 0, 0))

    row_buffer = [pltpu.VMEM((3, 3, channels, channels), BF16), pltpu.SemaphoreType.DMA((3,))]

    def conv(x, met, stats, rows, index, skip, name, after=()):
        near, cross, pair = met
        specs = [
            SMEM, field, edge, edge, stat, stat, stat, mask_block, IN_HBM,
        ]
        operands = [side, x, near, cross, pair, stats, rows, masks, conv_weight]
        kernel = functools.partial(conv_kernel, index)
        if skip is None:

            def kernel(*refs):
                return conv_kernel(index, *refs[:9], None, *refs[9:])
        else:
            specs.append(field)
            operands.append(skip)
        return call(
            kernel, name, operands, specs,
            [(field, field_f32), (IN_HBM, field_b16), row_out, row_out, stat_out],
            40, 9 * matmul,
            [
                pltpu.VMEM((pixels + 80, channels), F32), pltpu.VMEM((3, pixels + 64, channels), BF16), *row_buffer,
                pltpu.SemaphoreType.DMA,
            ],
            (3,), after,
        )

    met0 = (near0, cross0, pair0)
    middle, act_one, near1, cross1, stats1 = conv(x, met0, own0, norm_rows[0], 0, None, "conv_one")
    met1 = meet(near1, cross1, stats1)
    cot_second = permute(behind(cot_flat[half:], cot_first, met1[2]), turned)
    residual, act_two, near2, cross2, stats2 = conv(
        middle, met1, stats1, norm_rows[1], 1, x, "conv_two", (cot_first,)
    )
    met2 = meet(near2, cross2, stats2)

    (normed,) = call(
        normed_kernel, "normed", (residual, *met2, stats2, norm_rows[2]), [field, edge, edge, stat, stat, stat],
        [(field, field_b16)], 16, after=(cot_second,),
    )
    cotangent = jnp.concatenate([cot_first, cot_second], axis=0)

    normed_near = permute(normed, to_near)
    normed_pair = permute(normed, to_pair)

    block = 512
    anywhere = pl.BlockSpec(memory_space=pl.ANY)
    blocks = pixels // block
    totals_out = (whole(blocks, 8, block), shape((blocks, 8, block), F32))
    square = whole(channels, channels)
    cot_pair = permute(cotangent, to_pair)
    keys, values, queries, grads, keys_pair, values_pair, queries_pair, grads_pair = call(
        early_kernel, "early",
        (normed, normed_pair, cotangent, cot_pair, qk_weight, value_weight, proj_weight, bias_rows),
        [field] * 4 + [whole(2, channels, channels), square, square, stat],
        [(field, field_b16)] * 8, 32, 8 * matmul,
    )
    lane_field = (whole(pixels, 128), shape((pixels, 128), F32))
    weights, tops, sums, products = call(
        attend_first_kernel, "attend_first", (keys, values, keys_pair, values_pair, queries, column_tiles, row_tiles),
        [field] * 5 + [whole(pixels, 128), whole(1, 4 * pixels)],
        [(whole(pixels, 2 * pixels), shape((pixels, 2 * pixels), BF16)), lane_field, lane_field, (field, field_f32)],
        32, 2 * 2 * matmul * pixels / channels,
    )
    normed_cross = permute(behind(normed_near, products), to_pair)
    cot_near = permute(behind(cotangent, normed_near), to_near)
    attended, query_grad, totals = call(
        attend_kernel, "attend",
        (normed_near, normed_cross, keys, values, keys_pair, values_pair, queries, grads, weights, tops, sums, products, qk_weight, value_weight, bias_rows,
         column_tiles, row_tiles),
        [field] * 8 + [whole(pixels, 2 * pixels), whole(pixels, 128), whole(pixels, 128), field] + [whole(2, channels, channels), square, stat, whole(pixels, 128), whole(1, 4 * pixels)],
        [(field, field_b16), (field, field_b16), totals_out],
        58, 4 * matmul + 4 * 4 * matmul * pixels / channels,
        [pltpu.VMEM((2 * pixels, channels), BF16)] * 2,
    )

    totals_pair, totals_near, totals_cross = (permute(totals, to) for to in (to_pair, to_near, to_cross))
    cot_cross = permute(behind(cot_near, attended), to_pair)
    (output,) = call(
        out_kernel, "output", (attended, residual, proj_weight, block8(proj_bias)), [field, field, square, stat],
        [(field, field_b16)], 16, matmul, after=(cot_near,),
    )
    output_there = permute(output.reshape(1, band, width, channels), turned)
    key_grad, value_grad, normed_grad, near3, cross3, stats3, sums3 = call(
        key_kernel, "key_value_grad",
        (side, keys, values, queries, grads, queries_pair, grads_pair, normed_near, cot_near, normed_cross, cot_cross,
         query_grad, qk_weight, value_weight, proj_weight, bias_rows,
         totals, totals_pair, totals_near, totals_cross, column_tiles, row_tiles.reshape(4 * blocks, 1, block),
         residual, stats2, *met2, norm_rows[2]),
        [SMEM] + [field] * 2 + [anywhere] * 9 + [whole(2, channels, channels), square, square, stat]
        + [totals_out[0]] * 4
        + [whole(pixels, 128), whole(4 * blocks, 1, block), anywhere, stat, edge, edge, stat, stat],
        [(field, field_b16), (field, field_b16), (field, field_f32), row_out, row_out, stat_out, stat_out],
        60, 7 * matmul + 4 * 4 * matmul * pixels / channels,
        [pltpu.VMEM((pixels, channels), F32)] * 2
        + [
            pltpu.VMEM((8, pixels, channels), BF16), pltpu.VMEM((pixels, channels), BF16),
            pltpu.VMEM((pixels, channels), F32), pltpu.SemaphoreType.DMA((10,)),
        ],
    )
    met3 = meet(near3, cross3, stats3)


    def pieces(taps):
        dims = (2, PIECES // 2, taps, channels // PIECES, channels // 2)
        return [(whole(*dims), shape(dims, BF16))] * 2

    matrix_keep, matrix_send, matrix_sums = call(
        matrix_kernel, "matrix_grad", (place, normed, query_grad, key_grad, value_grad, attended, cotangent),
        [SMEM] + [field] * 6, pieces(4) + [stat_out], 32, 4 * matmul,
        [pltpu.VMEM((channels, pixels), BF16), pltpu.VMEM((channels, channels), BF16)], after=(output_there,),
    )

    def weight_grad(x, x_near, x_cross, stats, met, grad, grad_met, grad_stats, rows, act, cot, name, after=()):
        near, cross, pair = met
        g_near, g_cross, g_pair = grad_met
        spread = (3, pixels + 64, channels)
        extra, extra_in, extra_out = [], [], []
        if cot is not None:
            top = pl.BlockSpec((32, channels), lambda i: (0, 0))
            bottom = pl.BlockSpec((32, channels), lambda i: (pixels // 32 - 1, 0))
            extra = [cot, cot_near, cot_near, cot_cross, cot_cross, matrix_keep, matrix_send]
            extra_in = [field, top, bottom, top, bottom] + [spec for spec, _ in pieces(4)]
            extra_out = [(field, field_f32)]
        return call(
            functools.partial(weight_grad_kernel, cot is not None), name,
            [place, side, x, x_near, x_cross, stats, near, cross, pair, grad, g_near, g_cross, g_pair, grad_stats,
             rows, act, masks] + extra,
            [SMEM, SMEM, field, edge, edge, stat, edge, edge, stat, field, edge, edge, stat, stat, stat, field, mask_block]
            + extra_in,
            pieces(9 if cot is None else 13) + [(whole(*spread), shape(spread, BF16)), stat_out] + extra_out,
            58, 9 * matmul,
            [pltpu.VMEM((pixels + 80, channels), F32), pltpu.VMEM((channels, pixels), BF16), pltpu.VMEM((channels, channels), BF16)],
            (3,), after,
        )

    def conv_back(shifted, index, x, stats, met, rows, name, after=()):
        return call(
            functools.partial(conv_back_kernel, index), name, (side, shifted, masks, conv_weight, x, stats, *met, rows),
            [
                SMEM, whole(3, pixels + 64, channels), mask_block, IN_HBM,
                field, stat, edge, edge, stat, stat,
            ],
            [(field, field_f32), row_out, row_out, stat_out, stat_out],
            40, 9 * matmul, row_buffer, (3,), after,
        )

    far_bit = 2 * lanes
    others = []
    bit = 8
    while bit < lanes:
        others.append(bit)
        bit *= 2

    def swap(x, bit):
        return permute(x, lambda i: i ^ bit)

    def added(left, right):
        return (left.astype(F32) + right.astype(F32)).astype(BF16)

    def halve(part, bit, *deps):
        count = part.shape[0] // 2
        return part[:count], swap(part[count:], bit)

    def split(keep, coming):
        total = added(keep, coming)
        return total[0], total[1]

    far_both = near_bit | far_bit

    def z_send(first, second):
        part = jnp.stack([first, second], axis=1)
        return part[0], swap(part[1], far_bit), swap(part[2], near_bit), swap(part[3], far_both)

    def z_sum(own, *coming):
        part = own.astype(F32)
        for other in coming:
            part = part + other.astype(F32)
        part = part.astype(BF16)
        for bit in others:
            part = added(part, swap(part, bit))
        return part

    def z_share(part):
        return part, swap(part, far_bit), swap(part, near_bit), swap(part, far_both)

    def z_join(*parts):
        part = jnp.stack(parts)
        return part[:, 0], part[:, 1]

    def both(first, second, first_bit, second_bit):
        return swap(first, first_bit), swap(second, second_bit)

    def tied(token, *values):
        return lax.optimization_barrier(values + (token,))[:-1]

    def unpack(parts, taps, at_once, start, slots, base, into, name):
        piece = pl.BlockSpec(
            (2, PIECES // 2, at_once, channels // PIECES, channels // 2), lambda i: (0, 0, start // at_once + i, 0, 0)
        )
        operands, specs = [place, *parts], [SMEM, piece, piece]
        if into is not None:
            operands, specs = operands + [into], specs + [anywhere]
        out_spec = pl.BlockSpec((at_once, channels, channels), lambda i: (base // at_once + i, 0, 0))
        (out,) = call(
            unpack_kernel, name, operands, specs, [(out_spec, shape((slots, channels, channels), F32))],
            32, grid=(taps // at_once,), aliases={} if into is None else {3: 0},
        )
        return out

    two_keep, two_send, shifted_two, bias_two, residual_grad = weight_grad(
        residual, met2[0], met2[1], stats2, met2, normed_grad, met3, stats3, norm_rows[2], act_two, cotangent,
        "weight_two_grad",
    )
    two_coming = swap(two_send, 1)
    grad_two, near4, cross4, stats4, sums4 = conv_back(
        shifted_two, 1, middle, stats1, met1, norm_rows[1], "conv_two_back"
    )
    met4 = meet(near4, cross4, stats4)
    two_first, two_second = split(two_keep, behind(two_coming, near4))
    two_first, two_second = halve(two_first, 2), halve(two_second, 4)
    one_keep, one_send, shifted_one, bias_one = weight_grad(
        middle, met1[0], met1[1], stats1, met1, grad_two, met4, stats4, norm_rows[1], act_one, None,
        "weight_one_grad",
    )
    def after_token(token, *values):
        return lax.optimization_barrier(values + (token,))[:-1]

    def add_halves(token, first, second):
        one, two = after_token(token, first[1], second[1])
        return added(first[0], one), added(second[0], two)

    def join_halves(token, first, second, coming):
        one, two = after_token(token, *coming)
        return jnp.concatenate([first, one]), jnp.concatenate([second, two])

    one_coming = swap(behind(one_send, two_first[1], two_second[1]), 1)
    two_first, two_second = add_halves(shifted_one, two_first, two_second)
    token = two_first
    two_first, two_second = halve(two_first, 4), halve(two_second, 2)
    grad_one, near5, cross5, stats5, sums5 = conv_back(
        shifted_one, 0, x, own0, met0, norm_rows[0], "conv_one_back", (two_first[0], two_second[0])
    )
    met5 = meet(near5, cross5, stats5)

    one_first, one_second = split(one_keep, *after_token(near5, one_coming))
    token = one_first
    one_first, one_second = halve(one_first, 2), halve(one_second, 4)

    two_first, two_second = add_halves(token, two_first, two_second)
    token = two_first
    two = z_send(two_first, two_second)

    piece_dims = (channels // PIECES, channels // 2)
    small_parts = shape((4,) + piece_dims, BF16)
    image_grad, small = call(
        last_kernel, "image_grad",
        (grad_one, *met5, stats5, x, own0, *met0, norm_rows[0], residual_grad,
         bias_one, bias_two, sums5, sums4, sums3, matrix_sums),
        [field, edge, edge, stat, stat, field, stat, edge, edge, stat, stat, field] + [stat] * 6,
        [(field, field_b16), (whole(4, *piece_dims), small_parts)], 32, after=(token,),
    )
    for bit in others:
        small = added(small, swap(small, bit))

    one_first, one_second = add_halves(small, one_first, one_second)
    token = one_first
    one_first, one_second = halve(one_first, 4), halve(one_second, 2)

    two = z_sum(*after_token(token, *two))
    token = two
    two = z_share(jnp.concatenate([two.reshape((-1,) + piece_dims), small]))

    one_first, one_second = add_halves(token, one_first, one_second)
    token = one_first
    one = z_send(one_first, one_second)

    two = jnp.stack(after_token(token, *two))
    token = two
    two_first = jnp.concatenate([two[:, :13], two[:, 26:]], axis=1)
    two_second = two[:, 13:26]
    two_coming = both(two_first, two_second, 4, 2)

    one = z_sum(*after_token(token, *one))
    token = one
    one = z_share(one)

    two_first, two_second = join_halves(token, two_first, two_second, two_coming)
    token = two_first
    two_coming = both(two_first, two_second, 2, 4)

    one_first, one_second = z_join(*after_token(token, *one))
    token = one_first
    one_coming = both(one_first, one_second, 4, 2)
    image_there = permute(behind(image_grad, token).reshape(1, band, width, channels), turned)

    two = jnp.concatenate(join_halves(token, two_first, two_second, two_coming), axis=1)
    token = two
    two = two, swap(two, 1)

    one_first, one_second = join_halves(token, one_first, one_second, one_coming)
    token = one_first
    one_coming = both(one_first, one_second, 2, 4)

    two = after_token(token, *two)
    weights, qk_grad, value_weight_grad, proj_weight_grad = call(
        unpack_two_kernel, "unpack_two", (place, *two), [SMEM] + [whole(*two[0].shape)] * 2,
        [
            (
                pl.BlockSpec((3, channels, channels), lambda i: (3 + jnp.minimum(i, 2), 0, 0)),
                shape((18, channels, channels), F32),
            ),
            (whole(2, channels, channels), shape((2, channels, channels), F32)),
            (square, shape((channels, channels), F32)),
            (square, shape((channels, channels), F32)),
        ],
        40, grid=(4,),
    )
    small = jnp.stack(two)[:, :, 13:17].astype(F32)
    small = jnp.sum(small.reshape((-1, 2, 2) + piece_dims), axis=(0, 1))
    small = jnp.concatenate([small[0], small[1]], axis=1)
    token = qk_grad

    one = jnp.stack(join_halves(token, one_first, one_second, one_coming))
    one, image_there = lax.optimization_barrier((one, image_there))
    token = one
    one = one, swap(one, 1)

    weights = unpack(one, 9, 3, 0, 18, 0, weights, "unpack_one")

    return (
        output_there,
        image_there,
        weights.reshape(2, 3, 3, channels, channels),
        small[0:2],
        small[2:5],
        small[5:8],
        qk_grad,
        value_weight_grad,
        proj_weight_grad,
        small[8:10],
        small[10],
    )


def solution(mesh):
    split = P("batch", "seq", None, None)
    in_specs = (split, P("batch", "seq", None), split) + (P(),) * 9
    out_specs = (split, split) + (P(),) * 9
    return jax.shard_map(body, mesh=mesh, in_specs=in_specs, out_specs=out_specs, check_vma=False)
```
